32 devices in a mesh: ens: 2 (over x), lon: 16 (over z, y, core).
Axes of the slice: x: 2, y: 2, z: 4, core: 2. Of those that a mesh axis runs over, the one named last changes fastest.
Arguments:
- tracers: float32 [2, 50, 32, 2048], P(None, 'ens', None, 'lon'), parts along dimension 1, may hold values from -6 to 6
- east_flow: float32 [50, 32, 2048], P('ens', None, 'lon'), parts along dimension 0, may hold values from -0.3 to 0.3
- north_flow: float32 [50, 32, 2048], P('ens', None, 'lon'), parts along dimension 0, may hold values from -0.3 to 0.3
- mixing: float32 [48, 32, 2048], P('ens', None, 'lon'), parts along dimension 0, may hold values from 0.05 to 5
- depth_levels: int32 [32, 2048], P(None, 'lon'), may hold values from 0 to 25
- atm_flux: float32 [4, 128, 128], P('ens', 'lon'), parts along dimension 0, may hold values from -6 to 6
- source_blocks: int32 [16, 16, 2], P('lon'), may hold values from 0 to 7
- target_rows: int32 [16, 16, 2], P(None, 'lon'), may hold values from 0 to 31
- regrid_weights: float32 [16, 16, 2, 128, 128], P('lon'), may hold values from -0.5 to 0.5
Outputs:
- tracers_out: float32 [2, 50, 32, 2048], P(None, 'ens', None, 'lon'), parts along dimension 1
The draws below stay inside these ranges and needn't reach their ends.
There are 2 independent parts, one for each index of `ens`. The reference program is written for one: setup_inputs(seed, part) draws one part's arguments, and reference() takes and returns one part's arrays. A program takes and returns all parts, laid end to end along the dimension named above; an argument that names none is the same for every part. Nothing has to cross between parts.
All inputs are finite; a program needn't handle non-finite values.
Results may differ from the reference program's by a relative error of at most 0.0001.
Values sent between devices are 32-bit elements; how exact they have to be, the bound alone decides.
No kernel may reach another device: no remote copies, remote signals or barrier semaphores. Data moves between devices by JAX's collectives and lax.ppermute only.
A program may use at most 64 MiB of HBM per device.

```python
import math
import jax
import jax.numpy as jnp
from jax import lax

CLON = 128
LAT = 32
LEV = 25
SUB = 4
NFLUX = 2
AB = 128
ABLK = 8
CAP = 2
NLON = 2048
NATM = 128
LEVM = 24
N_LON = 16


def with_ends(values, key, smallest, high):
    spot = [jax.random.randint(jax.random.fold_in(key, axis), (), 0, length) for axis, length in enumerate(values.shape)]
    main_axis = values.shape.index(max(values.shape))
    beside = spot[:main_axis] + [(spot[main_axis] + 1) % values.shape[main_axis]] + spot[main_axis + 1:]
    return values.at[tuple(spot)].set(smallest).at[tuple(beside)].set(high)


def steps_of(key, dims, cuts, least, high):
    def one(axis_at, blocks):
        steps = jax.random.uniform(jax.random.fold_in(jax.random.fold_in(key, 6), axis_at), (blocks,), jnp.float32, least / len(cuts), high / len(cuts))
        return jnp.repeat(jnp.exp(steps), dims[axis_at] // blocks).reshape((-1,) + (1,) * (len(dims) - axis_at - 1))

    gain = one(*cuts[0])
    for cut in cuts[1:]:
        gain = gain * one(*cut)
    return gain


def noise(key, extent, scale, most, split=(), kind=jnp.bfloat16):
    drawn = scale * jax.random.normal(key, extent, jnp.float32)
    if split:
        drawn = drawn * steps_of(key, extent, split, -0.22, 0.18)
    return jnp.clip(drawn, -most, most).astype(kind)


def setup_inputs(seed: int = 0, part: int = 0) -> dict:
    keys = jax.random.split(jax.random.key(seed), 10)
    part_splits = jax.random.split(jax.random.fold_in(keys[9], part), 10)
    tracers = noise(part_splits[0], (2, LEV, LAT, NLON), 1.0, 6.0, ((3, 16),), jnp.float32)
    east_flow = noise(part_splits[1], (LEV, LAT, NLON), 0.1, 0.3, ((2, 16),), jnp.float32)
    north_flow = noise(part_splits[2], (LEV, LAT, NLON), 0.1, 0.3, ((2, 16),), jnp.float32)
    mixing = jnp.clip(jnp.exp(math.log(5.0) - 4.6051702 * jax.random.uniform(part_splits[3], (LEVM, LAT, NLON), jnp.float32) ** steps_of(part_splits[3], (LEVM, LAT, NLON), ((2, 16),), -0.2, 0.2)), 0.05, 5.0)
    depth_levels = with_ends(jax.random.randint(keys[4], (LAT, NLON), 0, LEV + 1), jax.random.fold_in(keys[4], 1), 0, LEV).astype(jnp.int32)
    atm_flux = noise(part_splits[5], (NFLUX, NATM, AB), 1.0, 6.0, ((1, 16),), jnp.float32)
    source_blocks = with_ends(jax.random.randint(keys[6], (N_LON, N_LON, CAP), 0, ABLK), jax.random.fold_in(keys[6], 1), 0, ABLK - 1).astype(jnp.int32)
    target_rows = with_ends(jax.random.randint(keys[7], (N_LON, N_LON, CAP), 0, LAT), jax.random.fold_in(keys[7], 1), 0, LAT - 1).astype(jnp.int32)
    regrid_weights = noise(keys[8], (N_LON, N_LON, CAP, AB, CLON), AB ** -0.5, 0.5, ((0, 16),), jnp.float32)
    return {"tracers": tracers, "east_flow": east_flow, "north_flow": north_flow, "mixing": mixing, "depth_levels": depth_levels, "atm_flux": atm_flux, "source_blocks": source_blocks, "target_rows": target_rows, "regrid_weights": regrid_weights}


DIFFUSION = 0.12
FLUX_GAIN = 0.5


def face_flux(velocity, inside, beyond, wet_inside, wet_beyond):
    return wet_inside * wet_beyond * (velocity * (0.5 * (inside + beyond)) - DIFFUSION * (beyond - inside))


def solve_columns(rhs, links):
    depth = rhs.shape[1]
    nothing = jnp.zeros_like(links[0])
    above = [nothing] + [links[level] for level in range(depth - 1)]
    below = [links[level] for level in range(depth - 1)] + [nothing]
    ratios = []
    partial_value = []
    for level in range(depth):
        if level == 0:
            pivot_value = 1.0 + above[level] + below[level]
            ratios.append(-below[level] / pivot_value)
            partial_value.append(rhs[:, level] / pivot_value)
        else:
            pivot_value = 1.0 + above[level] + below[level] + above[level] * ratios[level - 1]
            ratios.append(-below[level] / pivot_value)
            partial_value.append((rhs[:, level] + above[level] * partial_value[level - 1]) / pivot_value)
    levels_out = [None] * depth
    levels_out[depth - 1] = partial_value[depth - 1]
    for level in range(depth - 2, -1, -1):
        levels_out[level] = partial_value[level] - ratios[level] * levels_out[level + 1]
    return jnp.stack(levels_out, axis=1)


def reference(tracers, east_flow, north_flow, mixing, depth_levels, atm_flux, source_blocks, target_rows, regrid_weights):
    levels = jnp.arange(LEV, dtype=jnp.int32)[:, None, None]
    wet_mask = (levels < depth_levels[None]).astype(jnp.float32)
    tracer = tracers
    for substep in range(SUB):
        east_cells = jnp.roll(tracer, -1, axis=3)
        east_wet = jnp.roll(wet_mask, -1, axis=2)
        east_flux = face_flux(east_flow, tracer, east_cells, wet_mask, east_wet)
        west_flux = jnp.roll(east_flux, 1, axis=3)
        north_cells = jnp.concatenate([tracer[:, :, 1:, :], tracer[:, :, -1:, ::-1]], axis=2)
        north_wet = jnp.concatenate([wet_mask[:, 1:, :], wet_mask[:, -1:, ::-1]], axis=1)
        north_flux = face_flux(north_flow, tracer, north_cells, wet_mask, north_wet)
        south_flux = jnp.concatenate([jnp.zeros_like(north_flux[:, :, :1]), north_flux[:, :, :-1]], axis=2)
        tracer = tracer - (east_flux - west_flux + north_flux - south_flux)
    atm_blocks = atm_flux.reshape(NFLUX, N_LON, ABLK, AB)
    rows_index = jnp.arange(LAT, dtype=jnp.int32)

    def add_source(source, running):
        chosen = lax.dynamic_index_in_dim(source_blocks, source, 0, keepdims=False)
        source_block = lax.dynamic_index_in_dim(atm_blocks, source, 1, keepdims=False)
        picked = source_block[:, chosen]
        matrices = lax.dynamic_index_in_dim(regrid_weights, source, 0, keepdims=False)
        pieces = jnp.einsum("nesa,esao->esno", picked, matrices, precision=lax.Precision.HIGHEST)
        targets = lax.dynamic_index_in_dim(target_rows, source, 0, keepdims=False)
        one_hot = (targets[:, :, None] == rows_index).astype(jnp.float32)
        return running + jnp.einsum("esj,esno->njeo", one_hot, pieces, precision=lax.Precision.HIGHEST)

    start = jnp.zeros((NFLUX, LAT, N_LON, CLON), jnp.float32)
    surface = lax.fori_loop(0, N_LON, add_source, start).reshape(NFLUX, LAT, NLON)
    rhs = tracer.at[:, 0].add(FLUX_GAIN * surface * wet_mask[0])
    links = mixing * wet_mask[1:]
    return solve_columns(rhs, links)
```

```python
import functools

import jax
import jax.numpy as jnp
from jax import lax
from jax.experimental import pallas as pl
from jax.experimental.pallas import tpu as pltpu
from jax.sharding import PartitionSpec as P

SUB = 4
DIFFUSION = 0.12
FLUX_GAIN = 0.5
GROUP = 5
F32 = jnp.float32
VMEM = pl.BlockSpec(memory_space=pltpu.VMEM)
SMEM = pl.BlockSpec(memory_space=pltpu.SMEM)
HBM = pl.BlockSpec(memory_space=pltpu.HBM)
VMEM_LIMIT = 16 * 1024 * 1024


def lane_index():
    return lax.broadcasted_iota(jnp.int32, (8, 128), 1)


def row_index():
    return lax.broadcasted_iota(jnp.int32, (8, 128), 0)


def lanes(tile, shift):
    shift = shift % 128
    return pltpu.roll(tile, shift, 1) if shift else tile


def rows(tile, shift):
    shift = shift % 8
    return pltpu.roll(tile, shift, 0) if shift else tile


def take(tile, index):
    return jnp.take_along_axis(tile, index, axis=1)


def spread_order():
    lane = lane_index()
    return 4 * (lane & 31) + (lane >> 5)


def gather_order():
    lane = lane_index()
    return 32 * (lane & 3) + (lane >> 2)


def call(body, out, in_specs, scratch=(), out_specs=None, cost=None, name=None):
    return pl.pallas_call(
        body,
        out_shape=out,
        in_specs=in_specs,
        out_specs=out_specs if out_specs is not None else [VMEM] * len(out),
        scratch_shapes=list(scratch),
        compiler_params=pltpu.CompilerParams(vmem_limit_bytes=VMEM_LIMIT),
        cost_estimate=cost,
        name=name,
    )


def cost(micros):
    return pl.CostEstimate(flops=0, bytes_accessed=int(micros * 3.0e6), transcendentals=0)


def shape(*dims):
    return pltpu.VMEM(dims, F32)


def in_hbm(*arrays):
    return [pltpu.with_memory_space_constraint(x, pltpu.HBM) for x in arrays]


def in_vmem(*arrays):
    return [pltpu.with_memory_space_constraint(x, pltpu.VMEM) for x in arrays]


def face(flow, mask):
    half = 0.5 * flow
    return mask * (half + DIFFUSION), mask * (half - DIFFUSION)


def stencil(east, north, west, south):
    a_e, b_e = east
    a_n, b_n = north
    a_w, b_w = west
    a_s, b_s = south
    return (((1.0 - a_e) + b_w) - a_n) + b_s, b_e, a_w, b_n, a_s


def advance(weights, cell, east, west, north, south):
    own, b_e, a_w, b_n, a_s = weights
    return (own * cell + (a_w * west - b_e * east)) + (a_s * south - b_n * north)


def north_of(tiles, beyond):
    row = row_index()
    turned = [rows(t, -1) for t in tiles]
    return [jnp.where(row == 7, n, t) for t, n in zip(turned, turned[1:] + [beyond])]


def south_of(tiles):
    row = row_index()
    turned = [rows(t, 1) for t in tiles]
    return [turned[0]] + [jnp.where(row == 0, p, t) for p, t in zip(turned, turned[1:])]


def northern_rows(t_hbm, e_hbm, n_hbm, d_hbm, t, e, n, d, sems):
    top = pl.ds(t_hbm.shape[2] - 8, 8)
    return [
        pltpu.make_async_copy(t_hbm.at[:, :, top], t, sems.at[0]),
        pltpu.make_async_copy(e_hbm.at[:, top], e, sems.at[1]),
        pltpu.make_async_copy(n_hbm.at[:, top], n, sems.at[2]),
        pltpu.make_async_copy(d_hbm.at[top], d, sems.at[3]),
    ]


def fold_kernel(depth, t_hbm, e_hbm, n_hbm, d_hbm, out, west, east, t, e, n, d, sems):
    copies = northern_rows(t_hbm, e_hbm, n_hbm, d_hbm, t, e, n, d, sems)
    for copy in copies:
        copy.start()
    for copy in copies:
        copy.wait()
    lane, row = lane_index(), row_index()
    turn = 127 - lane
    levels = d[...].astype(F32)
    wests = [jnp.zeros((8, 128), F32)] * 2
    easts = [jnp.zeros((8, 128), F32)] * 2
    for k in range(depth + 1):
        if k < depth:
            cells = jnp.where(row < 4, rows(t[0, k], 4), t[1, k])
            flows = jnp.where(row < 4, rows(n[k], 4), e[k])
            if k < 4:
                flows = jnp.where(row == 4, rows(levels, -k), flows)
            tiles = (cells, flows)
        else:
            tiles = (None, levels)
        for half, tile in enumerate(tiles):
            if tile is None:
                continue
            tile = take(tile, turn)
            if k < depth:
                out[k, 8 * half : 8 * half + 8] = tile
            tile = lanes(tile, 4 * k)
            easts[half] = jnp.where((lane >= 4 * k) & (lane < 4 * k + 4), tile, easts[half])
            last = (4 * k - 4) % 128
            wests[half] = jnp.where((lane >= last) & (lane < last + 4), tile, wests[half])
    order = spread_order()
    for half in range(2):
        west[8 * half : 8 * half + 8] = take(lanes(wests[half], 4), order)
        east[8 * half : 8 * half + 8] = take(easts[half], order)


def edge_columns(planes, levels_tile):
    lane = lane_index()
    zero = jnp.zeros((8, 128), F32)
    first, last = [zero, zero], [zero, zero]
    items = list(planes)
    if levels_tile is not None:
        items.append(levels_tile)
    for k, tile in enumerate(items):
        tile = lanes(tile, 4 * k)
        low = 4 * k
        inside = (lane >= low) & (lane < low + 8)
        if low + 8 > 128:
            inside = inside | (lane < low + 8 - 128)
        first[k % 2] = jnp.where(inside, tile, first[k % 2])
        high = (4 * k - 8) % 128
        inside = (lane >= high) & (lane < high + 8)
        if high + 8 > 128:
            inside = inside | (lane < high + 8 - 128)
        last[k % 2] = jnp.where(inside, tile, last[k % 2])
    even = ((lane >> 2) & 1) == 0
    order = spread_order()
    w1 = jnp.where(even, first[0], first[1])
    w2 = lanes(jnp.where(even, first[1], first[0]), -4)
    e1 = lanes(jnp.where(even, last[1], last[0]), 4)
    e2 = lanes(jnp.where(even, last[0], last[1]), 8)
    return [take(x, order) for x in (w1, w2, e2, e1)]


def columns_kernel(depth, t_hbm, e_hbm, n_hbm, d_hbm, blocks, to_core, to_odd, t, e, n, d, sems):
    copies = [
        pltpu.make_async_copy(d_hbm, d, sems.at[4]),
        pltpu.make_async_copy(t_hbm.at[0], t.at[0], sems.at[0]),
        pltpu.make_async_copy(t_hbm.at[1], t.at[1], sems.at[1]),
        pltpu.make_async_copy(e_hbm, e, sems.at[2]),
        pltpu.make_async_copy(n_hbm, n, sems.at[3]),
    ]
    for copy in copies:
        copy.start()
    even = lax.rem(lax.axis_index("lon"), 2) == 0
    count = t.shape[2] // 8
    copies[0].wait()
    for f, field in enumerate((t.at[0], t.at[1], e, n)):
        copies[f + 1].wait()
        for j in range(count):
            span = slice(8 * j, 8 * j + 8)
            planes = [field[k, span] for k in range(depth)]
            found = edge_columns(planes, d[span].astype(F32) if f == 0 else None)
            for b, tile in enumerate(found):
                blocks[b, f, span] = tile
            w1, e1 = found[0], found[3]
            to_core[f, span] = jnp.where(even, e1, w1)
            to_odd[f, span] = jnp.where(even, w1, e1)


def regrid_kernel(size, atm_hbm, w_hbm, src_hbm, out, wide, w, atm, src, sems, w_sems):
    first = [pltpu.make_async_copy(atm_hbm, atm, sems.at[0]), pltpu.make_async_copy(src_hbm, src, sems.at[1])]
    for copy in first:
        copy.start()
    parts = w_sems.shape[0]
    each = size // parts
    weights = [
        pltpu.make_async_copy(w_hbm.at[0, pl.ds(p * each, each)], w.at[pl.ds(p * each, each)], w_sems.at[p])
        for p in range(parts)
    ]
    for copy in weights:
        copy.start()
    for copy in first:
        copy.wait()
    flat = atm[...].reshape(atm.shape[0] * atm.shape[1], atm.shape[2])
    count = flat.shape[0]
    blocks = atm.shape[1]
    columns = jnp.transpose(jnp.concatenate([flat, jnp.zeros((128 - count, 128), F32)], axis=0))
    for c in range(count):
        wide[c] = jnp.broadcast_to(columns[:, c : c + 1], (128, 128))
    def owner(e, carry):
        for s in range(2):
            block = src[s, e]
            sums = [None, None]
            for i in range(16):
                span = slice(8 * i, 8 * i + 8)
                weight = w[e, s, span]
                for f in range(2):
                    term = weight * wide[f * blocks + block, span]
                    sums[f] = term if sums[f] is None else sums[f] + term
            for f in range(2):
                out[e, 2 * f + s : 2 * f + s + 1] = jnp.sum(sums[f], axis=0, keepdims=True)
        return carry

    for p in range(parts):
        weights[p].wait()
        lax.fori_loop(p * each, (p + 1) * each, owner, 0, unroll=2)


def inner_kernel(
    depth, t_hbm, e_hbm, n_hbm, d_hbm, mix_hbm, out, inverse, linked, surface_wet, t, e, n, d, mix, sems, other
):
    levels = pltpu.make_async_copy(d_hbm, d, other.at[0])
    mixing = pltpu.make_async_copy(mix_hbm, mix, other.at[1])

    def parts(g):
        part = pl.ds(g * GROUP, GROUP)
        return (
            pltpu.make_async_copy(t_hbm.at[:, part], t.at[:, part], sems.at[g]),
            pltpu.make_async_copy(e_hbm.at[part], e.at[part], sems.at[g]),
            pltpu.make_async_copy(n_hbm.at[part], n.at[part], sems.at[g]),
        )

    levels.start()
    for g in range(depth // GROUP):
        for copy in parts(g):
            copy.start()
        if g == 0:
            mixing.start()
    levels.wait()
    row = row_index()
    count = t.shape[2] // 8
    spans = [slice(8 * j, 8 * j + 8) for j in range(count)]
    deep = [d[s] for s in spans]

    def wet_at(k):
        return [jnp.where(x > k, 1.0, 0.0).astype(F32) for x in deep]

    def level(k):
        wet = wet_at(k)
        easts = [face(e[k, s], w * lanes(w, -1)) for s, w in zip(spans, wet)]
        norths = [face(n[k, s], w * v) for s, w, v in zip(spans, wet, north_of(wet, wet[0]))]
        wests = [(lanes(a, 1), lanes(b, 1)) for a, b in easts]
        a_s = south_of([a for a, _ in norths])
        b_s = south_of([b for _, b in norths])
        a_s[0] = jnp.where(row == 0, 0.0, a_s[0])
        b_s[0] = jnp.where(row == 0, 0.0, b_s[0])
        weights = [stencil(*faces) for faces in zip(easts, norths, wests, zip(a_s, b_s))]
        state = [[t[f, k, s] for s in spans] for f in range(2)]
        for _ in range(SUB):
            for f in range(2):
                cells = state[f]
                up, down = north_of(cells, cells[-1]), south_of(cells)
                state[f] = [
                    advance(w, c, lanes(c, -1), lanes(c, 1), u, v)
                    for w, c, u, v in zip(weights, cells, up, down)
                ]
        for f in range(2):
            for s, c in zip(spans, state[f]):
                out[f, k, s] = c

    def some(g, carry):
        for copy in parts(g):
            copy.wait()
        for i in range(GROUP):
            level(g * GROUP + i)
        return carry

    lax.fori_loop(0, depth // GROUP, some, 0)

    zero = jnp.zeros((8, 128), F32)
    mixing.wait()
    link_above = [zero] * count
    last_ratio = [zero] * count
    for s, wet in zip(spans, wet_at(0)):
        surface_wet[s] = wet
    for k in range(depth):
        wet = wet_at(k + 1)
        for j, s in enumerate(spans):
            link = mix[k, s] * wet[j] if k < depth - 1 else zero
            inv = 1.0 / (1.0 + link_above[j] + link + link_above[j] * last_ratio[j])
            inverse[k, s] = inv
            if k < depth - 1:
                linked[k, s] = link
            last_ratio[j] = -link * inv
            link_above[j] = link


def fold_weights(flows, wet, own_wet, toward_east, toward_west):
    row = row_index()
    result = []
    e_flow = [jnp.where(row < 4, rows(x, 4), x) for x in flows]
    n_flow = [jnp.where(row < 4, x, rows(x, 4)) for x in flows]
    easts = [face(x, w * v) for x, w, v in zip(e_flow, wet, toward_east(wet))]
    a_w = toward_west([a for a, _ in easts])
    b_w = toward_west([b for _, b in easts])
    for i in range(len(flows)):
        up = fold_north(wet[i], own_wet[i], own_wet[i])
        north = face(n_flow[i], wet[i] * up)
        south = (rows(north[0], 1), rows(north[1], 1))
        result.append(stencil(easts[i], north, (a_w[i], b_w[i]), south))
    return result


def fold_north(fold, first, second):
    row = row_index()
    return jnp.where((row & 3) == 3, jnp.where(row < 4, rows(first, 4), second), rows(fold, -1))


def strip_kernel(depth, t_hbm, e_hbm, n_hbm, d_hbm, fold, strip, t, e, n, d, sems):
    copies = northern_rows(t_hbm, e_hbm, n_hbm, d_hbm, t, e, n, d, sems)
    for copy in copies:
        copy.start()
    for copy in copies:
        copy.wait()
    row = row_index()
    deep = d[...]
    fold_deep = fold_levels(fold)

    def plus(tiles):
        return [lanes(x, 1) for x in tiles]

    def minus(tiles):
        return [lanes(x, -1) for x in tiles]

    def level(k):
        wet = jnp.where(deep > k, 1.0, 0.0).astype(F32)
        wet_fold = jnp.where(fold_deep > jnp.asarray(k).astype(F32), 1.0, 0.0).astype(F32)
        over = fold_weights([fold[k, 8:16]], [wet_fold], [wet], plus, minus)[0]
        east = face(e[k], wet * lanes(wet, -1))
        north = face(n[k], wet * jnp.where(row == 7, wet_fold, rows(wet, -1)))
        weights = stencil(
            east, north, (lanes(east[0], 1), lanes(east[1], 1)), (rows(north[0], 1), rows(north[1], 1))
        )
        one, two, cells = t[0, k], t[1, k], fold[k, 0:8]
        for step in range(SUB):
            up_one = jnp.where(row == 7, rows(cells, 4), rows(one, -1))
            up_two = jnp.where(row == 7, cells, rows(two, -1))
            if step < SUB - 1:
                up = fold_north(cells, one, two)
                cells = advance(over, cells, lanes(cells, 1), lanes(cells, -1), up, rows(cells, 1))
            one = advance(weights, one, lanes(one, -1), lanes(one, 1), up_one, rows(one, 1))
            two = advance(weights, two, lanes(two, -1), lanes(two, 1), up_two, rows(two, 1))
        strip[0, k] = one
        strip[1, k] = two

    def some(g, carry):
        for i in range(GROUP):
            level(g * GROUP + i)
        return carry

    lax.fori_loop(0, depth // GROUP, some, 0)


def fold_levels(fold):
    row = row_index()
    deep = jnp.zeros((8, 128), F32)
    for r in range(4):
        deep = jnp.where((row & 3) == r, jnp.broadcast_to(fold[r, 12:13], (8, 128)), deep)
    return deep


def fold_columns(depth, fold):
    return [
        edge_columns([fold[k, 8 * half : 8 * half + 8] for k in range(depth)], fold_levels(fold) if half else None)
        for half in range(2)
    ]


def corners_kernel(depth, size, fold, west, east, blocks, to_core, to_odd):
    me = lax.axis_index("lon")
    even = lax.rem(me, 2) == 0
    for half, found in enumerate(fold_columns(depth, fold)):
        span = slice(8 * half, 8 * half + 8)
        for b, tile in enumerate(found):
            blocks[b, span] = tile
        w1, e1 = found[0], found[3]
        to_core[span] = jnp.where(even, e1, w1)
        odd = jnp.where(even, w1, e1)
        odd = jnp.where(me == 0, west[span], odd)
        to_odd[span] = jnp.where(me == size - 1, east[span], odd)


def edge_side(depth, rows_count, cells, flows, fold_cells, fold_flows):
    lane, row = lane_index(), row_index()
    level = lane & 31
    count = rows_count // 8

    def plus(tiles):
        turned = [lanes(x, 32) for x in tiles]
        return [turned[0]] + [jnp.where(lane < 32, p, x) for p, x in zip(turned, turned[1:])]

    def minus(tiles):
        turned = [lanes(x, -32) for x in tiles]
        return [jnp.where(lane >= 96, q, x) for x, q in zip(turned, turned[1:])] + [turned[2]]

    at_levels = (lane & 96) + depth
    wet = [
        [
            jnp.where(take(cells[b][0][j], at_levels) > level.astype(F32), 1.0, 0.0).astype(F32)
            for j in range(count)
        ]
        for b in range(3)
    ]
    wet_fold = []
    for b in range(3):
        deep = take(fold_flows[b], at_levels)
        deep = jnp.where(row < 4, rows(deep, 4), deep)
        wet_fold.append(jnp.where(deep > level.astype(F32), 1.0, 0.0).astype(F32))
    over = fold_weights(fold_flows, wet_fold, [wet[b][-1] for b in range(3)], plus, minus)

    easts = [[None] * count for _ in range(3)]
    wests = [[None] * count for _ in range(3)]
    for j in range(count):
        beyond = minus([wet[b][j] for b in range(3)])
        found = [face(flows[b][0][j], wet[b][j] * beyond[b]) for b in range(3)]
        a_w, b_w = plus([a for a, _ in found]), plus([b for _, b in found])
        for b in range(3):
            easts[b][j] = found[b]
            wests[b][j] = (a_w[b], b_w[b])
    weights = []
    for b in range(3):
        up = north_of(wet[b], wet_fold[b])
        norths = [face(flows[b][1][j], wet[b][j] * up[j]) for j in range(count)]
        a_s, b_s = south_of([a for a, _ in norths]), south_of([c for _, c in norths])
        a_s[0] = jnp.where(row == 0, 0.0, a_s[0])
        b_s[0] = jnp.where(row == 0, 0.0, b_s[0])
        weights.append(
            [stencil(easts[b][j], norths[j], wests[b][j], (a_s[j], b_s[j])) for j in range(count)]
        )

    state = [[list(cells[b][f]) for f in range(2)] for b in range(3)]
    folded = list(fold_cells)
    for step in range(SUB):
        fold_east, fold_west = plus(folded), minus(folded)
        following = [[[None] * count for _ in range(2)] for _ in range(3)]
        for f in range(2):
            for j in range(count):
                line = [state[b][f][j] for b in range(3)]
                east, west = minus(line), plus(line)
                for b in range(3):
                    following[b][f][j] = (east[b], west[b])
        next_fold = []
        for b in range(3):
            up = fold_north(folded[b], state[b][0][-1], state[b][1][-1])
            next_fold.append(
                advance(over[b], folded[b], fold_east[b], fold_west[b], up, rows(folded[b], 1))
            )
        for b in range(3):
            beyond = (rows(folded[b], 4), folded[b])
            for f in range(2):
                tiles = state[b][f]
                up, down = north_of(tiles, beyond[f]), south_of(tiles)
                state[b][f] = [
                    advance(weights[b][j], tiles[j], *following[b][f][j], up[j], down[j]) for j in range(count)
                ]
        folded = next_fold
    return state[1]


def last_kernel(
    depth, strip, wet, inner, inverse, link, blocks, core, odd, fold, fold_core, fold_odd, pieces, target_hbm,
    out_hbm, merged, out, target, sems, other,
):
    targets = pltpu.make_async_copy(target_hbm, target, other.at[0])
    targets.start()
    lane, row = lane_index(), row_index()
    size = pieces.shape[0]
    rows_count = inner.shape[2]
    count = rows_count // 8
    spans = [slice(8 * j, 8 * j + 8) for j in range(count)]
    me = lax.axis_index("lon")
    even = lax.rem(me, 2) == 0

    def received(f, s, west):
        a, b = core[f, s], odd[f, s]
        return jnp.where(even, b, a) if west else jnp.where(even, a, b)

    def own(b, f, s):
        return blocks[b, f, s]

    sides = []
    for west in (True, False):
        near, far = (0, 1) if west else (3, 2)
        here = [[[own(b, f, s) for s in spans] for f in range(4)] for b in (near, far)]
        there = [[received(f, s, west) for s in spans] for f in range(4)]
        a, b = fold_core[...], fold_odd[...]
        letter = jnp.where(even, b, a) if west else jnp.where(even, a, b)
        line = [there, here[0], here[1]] if west else [here[1], here[0], there]
        cells_near = [fold[near, 0:8], fold[far, 0:8]]
        flows_near = [fold[near, 8:16], fold[far, 8:16]]
        if west:
            fold_cells = [letter[0:8]] + cells_near
            fold_flows = [letter[8:16]] + flows_near
        else:
            fold_cells = cells_near[::-1] + [letter[0:8]]
            fold_flows = flows_near[::-1] + [letter[8:16]]
        sides.append(
            edge_side(depth, rows_count, [x[0:2] for x in line], [x[2:4] for x in line], fold_cells, fold_flows)
        )

    order = gather_order()
    group_even = ((lane >> 2) & 1) == 0
    for f in range(2):
        for j, s in enumerate(spans):
            a = take(sides[0][f][j], order)
            b = lanes(take(sides[1][f][j], order), -4)
            merged[0, f, s] = jnp.where(group_even, a, b)
            merged[1, f, s] = jnp.where(group_even, b, a)

    surface = [[jnp.zeros((8, 128), F32) for _ in spans] for _ in range(2)]
    targets.wait()
    for a in range(size):
        for s in range(2):
            goal = target[s, a]
            hits = [row + 8 * j == goal for j in range(count)]
            for f in range(2):
                piece = jnp.broadcast_to(pieces[a, 2 * f + s : 2 * f + s + 1], (8, 128))
                surface[f] = [x + jnp.where(hit, piece, 0.0) for x, hit in zip(surface[f], hits)]

    outer = (lane < 4) | (lane >= 124)
    partial_value = [[None] * count for _ in range(2)]
    for k in range(depth):
        for f in range(2):
            for j, s in enumerate(spans):
                cell = inner[f, k, s]
                if j == count - 1:
                    cell = jnp.where(row >= 4, strip[f, k], cell)
                cell = jnp.where(outer, lanes(merged[k % 2, f, s], -4 * k), cell)
                if k == 0:
                    cell = cell + FLUX_GAIN * surface[f][j] * wet[s]
                else:
                    cell = cell + link[k - 1, s] * partial_value[f][j]
                value = cell * inverse[k, s]
                partial_value[f][j] = value
                out[f, k, s] = value
    copies = []
    for k in range(depth - 1, -1, -1):
        if k < depth - 1:
            for f in range(2):
                for j, s in enumerate(spans):
                    value = out[f, k, s] + link[k, s] * inverse[k, s] * partial_value[f][j]
                    partial_value[f][j] = value
                    out[f, k, s] = value
        if k % GROUP == 0:
            part = pl.ds(k, min(GROUP, depth - k))
            copy = pltpu.make_async_copy(out.at[:, part], out_hbm.at[:, part], sems.at[k // GROUP])
            copy.start()
            copies.append(copy)
    for copy in copies:
        copy.wait()


def on_device(
    tracers,
    east_flow,
    north_flow,
    mixing,
    depth_levels,
    atm_flux,
    source_blocks,
    target_rows,
    regrid_weights,
):
    size = lax.axis_size("lon")
    depth, lat = tracers.shape[1], tracers.shape[2]
    dma = pltpu.SemaphoreType.DMA
    band = [
        pltpu.VMEM((2, depth, 8, 128), F32),
        pltpu.VMEM((depth, 8, 128), F32),
        pltpu.VMEM((depth, 8, 128), F32),
        pltpu.VMEM((8, 128), jnp.int32),
    ]
    top, west_corner, east_corner = call(
        functools.partial(fold_kernel, depth),
        (shape(depth, 16, 128), shape(16, 128), shape(16, 128)),
        [HBM] * 4,
        [*band, dma((4,))],
        cost=cost(0.1),
        name="fold_rows",
    )(*in_hbm(tracers, east_flow, north_flow, depth_levels))
    fold = lax.ppermute(top, "lon", [(i, size - 1 - i) for i in range(size)])

    plane = shape(depth, lat, 128)
    block = [shape(2, depth, lat, 128), plane, plane, pltpu.VMEM((lat, 128), jnp.int32)]
    blocks, to_core, to_odd = call(
        functools.partial(columns_kernel, depth),
        (shape(4, 4, lat, 128), shape(4, lat, 128), shape(4, lat, 128)),
        [HBM] * 4,
        [*block, dma((5,))],
        cost=cost(0.1),
        name="edge_columns",
    )(*in_hbm(tracers, east_flow, north_flow, depth_levels))
    core = lax.ppermute(to_core, "lon", [(i, i ^ 1) for i in range(size)])
    odd = lax.ppermute(to_odd, "lon", [(i, (i + (1 if i % 2 else -1)) % size) for i in range(size)])

    (pieces,) = call(
        functools.partial(regrid_kernel, size),
        (shape(size, 4, 128),),
        [HBM, HBM, HBM],
        [
            pltpu.VMEM((2 * atm_flux.shape[1], 128, 128), F32),
            pltpu.VMEM((size, 2, 128, 128), F32),
            pltpu.VMEM(atm_flux.shape, F32),
            pltpu.SMEM((2, size), jnp.int32),
            dma((2,)),
            dma((4,)),
        ],
        cost=cost(0.1),
        name="regrid",
    )(*in_hbm(atm_flux, regrid_weights, jnp.transpose(source_blocks[0])))
    received = lax.all_to_all(pieces, "lon", split_axis=0, concat_axis=0, tiled=True)

    inner, inverse, link, wet = call(
        functools.partial(inner_kernel, depth),
        (shape(2, depth, lat, 128), plane, shape(depth - 1, lat, 128), shape(lat, 128)),
        [HBM] * 5,
        [*block, shape(depth - 1, lat, 128), dma((depth // GROUP + 1,)), dma((2,))],
        cost=cost(0.1),
        name="inner_cells",
    )(*in_hbm(tracers, east_flow, north_flow, depth_levels, mixing))

    fold_blocks, fold_core, fold_odd = call(
        functools.partial(corners_kernel, depth, size),
        (shape(4, 16, 128), shape(16, 128), shape(16, 128)),
        [VMEM] * 3,
        cost=cost(0.1),
        name="fold_corners",
    )(*in_vmem(fold, west_corner, east_corner))
    fold_core = lax.ppermute(fold_core, "lon", [(i, i ^ 1) for i in range(size)])
    near = [(i, i + (1 if i % 2 else -1)) for i in range(1, size - 1)]
    fold_odd = lax.ppermute(fold_odd, "lon", [(0, 0), *near, (size - 1, size - 1)])

    (strip,) = call(
        functools.partial(strip_kernel, depth),
        (shape(2, depth, 8, 128),),
        [HBM] * 4 + [VMEM],
        [*band, dma((4,))],
        cost=cost(0.1),
        name="top_strip",
    )(*in_hbm(tracers, east_flow, north_flow, depth_levels), *in_vmem(fold))

    (result,) = call(
        functools.partial(last_kernel, depth),
        (jax.ShapeDtypeStruct((2, depth, lat, 128), F32),),
        [VMEM] * 12 + [HBM],
        [
            pltpu.VMEM((2, 2, lat, 128), F32),
            pltpu.VMEM((2, depth, lat, 128), F32),
            pltpu.SMEM((2, size), jnp.int32),
            dma((-(-depth // GROUP),)),
            dma((1,)),
        ],
        out_specs=[HBM],
        cost=cost(0.1),
        name="edges_and_columns",
    )(
        *in_vmem(strip, wet, inner, inverse, link, blocks, core, odd, fold_blocks, fold_core, fold_odd, received),
        *in_hbm(jnp.transpose(target_rows[:, 0, :])),
    )
    return result


def solution(mesh):
    return jax.shard_map(
        on_device,
        mesh=mesh,
        in_specs=(
            P(None, "ens", None, "lon"),
            P("ens", None, "lon"),
            P("ens", None, "lon"),
            P("ens", None, "lon"),
            P(None, "lon"),
            P("ens", "lon", None),
            P("lon", None, None),
            P(None, "lon", None),
            P("lon", None, None, None, None),
        ),
        out_specs=P(None, "ens", None, "lon"),
        check_vma=False,
    )
```

```python
import functools

import jax
import jax.numpy as jnp
from jax import lax
from jax.experimental import pallas as pl
from jax.experimental.pallas import tpu as pltpu
from jax.sharding import PartitionSpec as P

SUB = 4
DIFFUSION = 0.12
FLUX_GAIN = 0.5
GROUP = 5
PART = 13
F32 = jnp.float32
VMEM = pl.BlockSpec(memory_space=pltpu.VMEM)
SMEM = pl.BlockSpec(memory_space=pltpu.SMEM)
HBM = pl.BlockSpec(memory_space=pltpu.HBM)
VMEM_LIMIT = 16 * 1024 * 1024


def lane_index():
    return lax.broadcasted_iota(jnp.int32, (8, 128), 1)


def row_index():
    return lax.broadcasted_iota(jnp.int32, (8, 128), 0)


def lanes(tile, shift):
    shift = shift % 128
    return pltpu.roll(tile, shift, 1) if shift else tile


def rows(tile, shift):
    shift = shift % 8
    return pltpu.roll(tile, shift, 0) if shift else tile


def take(tile, index):
    return jnp.take_along_axis(tile, index, axis=1)


def spread_order():
    lane = lane_index()
    return 4 * (lane & 31) + (lane >> 5)


def gather_order():
    lane = lane_index()
    return 32 * (lane & 3) + (lane >> 2)


def call(body, out, in_specs, scratch=(), out_specs=None, cost=None, name=None):
    return pl.pallas_call(
        body,
        out_shape=out,
        in_specs=in_specs,
        out_specs=out_specs if out_specs is not None else [VMEM] * len(out),
        scratch_shapes=list(scratch),
        compiler_params=pltpu.CompilerParams(vmem_limit_bytes=VMEM_LIMIT),
        cost_estimate=cost,
        name=name,
    )


def cost(micros):
    return pl.CostEstimate(flops=0, bytes_accessed=int(micros * 3.0e6), transcendentals=0)


def shape(*dims):
    return pltpu.VMEM(dims, F32)


def in_hbm(*arrays):
    return [pltpu.with_memory_space_constraint(x, pltpu.HBM) for x in arrays]


def in_vmem(*arrays):
    return [pltpu.with_memory_space_constraint(x, pltpu.VMEM) for x in arrays]


def face(half, open_face):
    return jnp.where(open_face, half + DIFFUSION, 0.0), jnp.where(open_face, half - DIFFUSION, 0.0)


def stencil(east, north, west, south):
    a_e, b_e = east
    a_n, b_n = north
    a_w, b_w = west
    a_s, b_s = south
    return (((1.0 - a_e) + b_w) - a_n) + b_s, b_e, a_w, b_n, a_s


def advance(weights, cell, east, west, north, south):
    own, b_e, a_w, b_n, a_s = weights
    return (own * cell + (a_w * west - b_e * east)) + (a_s * south - b_n * north)


def north_of(tiles, beyond):
    row = row_index()
    turned = [rows(t, -1) for t in tiles]
    return [jnp.where(row == 7, n, t) for t, n in zip(turned, turned[1:] + [beyond])]


def south_of(tiles):
    row = row_index()
    turned = [rows(t, 1) for t in tiles]
    return [turned[0]] + [jnp.where(row == 0, p, t) for p, t in zip(turned, turned[1:])]


def northern_rows(t_hbm, e_hbm, n_hbm, d_hbm, t, e, n, d, sems):
    top = pl.ds(t_hbm.shape[2] - 8, 8)
    return [
        pltpu.make_async_copy(t_hbm.at[:, :, top], t, sems.at[0]),
        pltpu.make_async_copy(e_hbm.at[:, top], e, sems.at[1]),
        pltpu.make_async_copy(n_hbm.at[:, top], n, sems.at[2]),
        pltpu.make_async_copy(d_hbm.at[top], d, sems.at[3]),
    ]


def fold_kernel(depth, t_hbm, e_hbm, n_hbm, d_hbm, out, west, east, t, e, n, d, sems):
    copies = northern_rows(t_hbm, e_hbm, n_hbm, d_hbm, t, e, n, d, sems)
    for copy in copies:
        copy.start()
    for copy in copies:
        copy.wait()
    row = row_index()
    turn = 127 - lane_index()
    levels = d[...].astype(F32)
    for k in range(depth):
        cells = jnp.where(row < 4, rows(t[0, k], 4), t[1, k])
        flows = jnp.where(row < 4, rows(n[k], 4), e[k])
        if k < 4:
            flows = jnp.where(row == 4, rows(levels, -k), flows)
        out[k, 0:8] = take(cells, turn)
        out[k, 8:16] = take(flows, turn)
    spans, stacks = [], []
    for half in range(2):
        span = slice(8 * half, 8 * half + 8)
        spans.append(span)
        stacks.append(stack_of(out, depth, span))
    stacks[1].append(lambda: take(levels, turn))
    for span, found in zip(spans, edge_columns(stacks)):
        east[span], west[span] = found[0], found[3]


def edge_columns(stacks):
    lane = lane_index()
    outer = (lane < 8) | (lane >= 120)
    group = [((lane >> 2) & 3) == c for c in range(3)]
    sums = [[None] * 4 for _ in stacks]
    for k in range(max(len(x) for x in stacks)):
        for total, stack in zip(sums, stacks):
            if k < len(stack):
                tile = lanes(jnp.where(outer, stack[k](), 0.0), 4 * k)
                total[k % 4] = tile if total[k % 4] is None else total[k % 4] + tile
    offsets = (0, 1, -2, -1)
    found = []
    for offset in offsets:
        for total in sums:
            a, b, c, d = [total[(g - offset) % 4] for g in range(4)]
            tile = jnp.where(group[0], a, jnp.where(group[1], b, jnp.where(group[2], c, d)))
            found.append(lanes(tile, -4 * offset))
    order = spread_order()
    found = [take(x, order) for x in found]
    return [[found[b * len(stacks) + i] for b in range(4)] for i in range(len(stacks))]


def stack_of(ref, depth, *where):
    return [lambda k=k: ref[(k, *where)] for k in range(depth)]


def columns_kernel(depth, t_hbm, e_hbm, n_hbm, d_hbm, blocks, to_core, to_odd, t, e, n, d, sems):
    copies = [
        pltpu.make_async_copy(d_hbm, d, sems.at[4]),
        pltpu.make_async_copy(t_hbm.at[0], t.at[0], sems.at[0]),
        pltpu.make_async_copy(t_hbm.at[1], t.at[1], sems.at[1]),
        pltpu.make_async_copy(e_hbm, e, sems.at[2]),
        pltpu.make_async_copy(n_hbm, n, sems.at[3]),
    ]
    for copy in copies:
        copy.start()
    even = lax.rem(lax.axis_index("lon"), 2) == 0
    count = t.shape[2] // 8
    copies[0].wait()
    spans = [slice(8 * j, 8 * j + 8) for j in range(count)]
    fields = (t.at[0], t.at[1], e, n)
    for pair in ((0, 1), (2, 3)):
        for f in pair:
            copies[f + 1].wait()
        places = [(f, span) for f in pair for span in spans]
        stacks = [stack_of(fields[f], depth, span) for f, span in places]
        if 0 in pair:
            for stack, span in zip(stacks, spans):
                stack.append(lambda span=span: d[span].astype(F32))
        for (f, span), found in zip(places, edge_columns(stacks)):
            for b, tile in enumerate(found):
                blocks[b, f, span] = tile
            w1, e1 = found[0], found[3]
            to_core[f, span] = jnp.where(even, e1, w1)
            to_odd[f, span] = jnp.where(even, w1, e1)


def regrid_kernel(size, atm_hbm, w_hbm, src_hbm, out, wide, w, part, atm, src, sems, w_sems):
    first = [pltpu.make_async_copy(atm_hbm, atm, sems.at[0]), pltpu.make_async_copy(src_hbm, src, sems.at[1])]
    for copy in first:
        copy.start()
    parts = w_sems.shape[0]
    each = size // parts
    weights = [
        pltpu.make_async_copy(w_hbm.at[0, pl.ds(p * each, each)], w.at[pl.ds(p * each, each)], w_sems.at[p])
        for p in range(parts)
    ]
    for copy in weights:
        copy.start()
    for copy in first:
        copy.wait()
    flat = atm[...].reshape(atm.shape[0] * atm.shape[1], atm.shape[2])
    count = flat.shape[0]
    blocks = atm.shape[1]
    columns = jnp.transpose(jnp.concatenate([flat, jnp.zeros((128 - count, 128), F32)], axis=0))
    for c in range(count):
        wide[c] = jnp.broadcast_to(columns[:, c : c + 1], (128, 128))
    def owner(e, carry):
        for s in range(2):
            block = src[s, e]
            sums = [None, None]
            for i in range(16):
                span = slice(8 * i, 8 * i + 8)
                weight = w[e, s, span]
                for f in range(2):
                    term = weight * wide[f * blocks + block, span]
                    sums[f] = term if sums[f] is None else sums[f] + term
            for f in range(2):
                part[e, 2 * f + s] = sums[f]
        return carry

    for p in range(parts):
        weights[p].wait()
        lax.fori_loop(p * each, (p + 1) * each, owner, 0, unroll=4)

    def pair(e, carry):
        out[e] = totals([part[2 * e + i // 4, i % 4] for i in range(8)])
        return carry

    lax.fori_loop(0, size // 2, pair, 0, unroll=8)


def totals(tiles):
    row = row_index()
    for step in (4, 2, 1):
        low = (row & step) == 0
        half = len(tiles) // 2
        merged = []
        for a, b in zip(tiles[:half], tiles[half:]):
            kept, moved = jnp.where(low, a, b), jnp.where(low, b, a)
            if step == 4:
                turned = rows(moved, 4)
            else:
                turned = jnp.where(low, rows(moved, -step), rows(moved, step))
            merged.append(kept + turned)
        tiles = merged
    return tiles[0]


def inner_kernel(
    depth, t_hbm, e_hbm, n_hbm, d_hbm, mix_hbm, fold, out, surface_wet, columns,
    t, e, n, d, mix, weights, folded, over, sems, flow_sems, cell_sems,
):
    levels = pltpu.make_async_copy(d_hbm, d, sems.at[0])
    mixing = pltpu.make_async_copy(mix_hbm, mix, sems.at[1])
    parts = [pl.ds(k, min(PART, depth - k)) for k in range(0, depth, PART)]
    flows = [
        (
            pltpu.make_async_copy(e_hbm.at[p], e.at[p], flow_sems.at[0, i]),
            pltpu.make_async_copy(n_hbm.at[p], n.at[p], flow_sems.at[1, i]),
        )
        for i, p in enumerate(parts)
    ]
    cells = [pltpu.make_async_copy(t_hbm.at[:, p], t.at[:, p], cell_sems.at[i]) for i, p in enumerate(parts)]
    levels.start()
    for pair in flows:
        for copy in pair:
            copy.start()
    for copy in cells:
        copy.start()
    mixing.start()
    levels.wait()
    row = row_index()
    count = t.shape[2] // 8
    spans = [slice(8 * j, 8 * j + 8) for j in range(count)]
    deep = [d[s].astype(F32) for s in spans]
    fold_deep = fold_levels(fold)

    def plus(tiles):
        return [lanes(x, 1) for x in tiles]

    def minus(tiles):
        return [lanes(x, -1) for x in tiles]

    over_faces = fold_faces([fold_deep], [deep[-1]], plus, minus)
    east_faces = [jnp.minimum(x, y) for x, y in zip(deep, minus(deep))]
    faces = list(zip(east_faces, plus(east_faces), block_faces(deep, fold_deep)))

    def fold_coefficients(levels):
        found = fold_weights(
            [fold[k, 8:16] for k in levels], over_faces * len(levels), [float(k) for k in levels], minus
        )
        for k, tiles in zip(levels, found):
            for i, x in enumerate(tiles):
                over[i, k] = x

    def coefficients(k):
        e_half = [0.5 * e[k, s] for s in spans]
        n_half = [0.5 * n[k, s] for s in spans]
        for s, he, hw, hn, hs, (east, west, (north, south)) in zip(
            spans, e_half, plus(e_half), n_half, south_of(n_half), faces
        ):
            found = stencil(
                face(he, east > float(k)),
                face(hn, north > float(k)),
                face(hw, west > float(k)),
                face(hs, south > float(k)),
            )
            for i, x in enumerate(found):
                weights[i, k, s] = x

    def substep(k, step):
        source = out if step else t
        state = [[source[f, k, s] for s in spans] for f in range(2)]
        cells = folded[k] if step else fold[k, 0:8]
        beyond = (rows(cells, 4), cells)
        for f in range(2):
            up, down = north_of(state[f], beyond[f]), south_of(state[f])
            for s, c, u, v in zip(spans, state[f], up, down):
                w = [weights[i, k, s] for i in range(5)]
                out[f, k, s] = advance(w, c, lanes(c, -1), lanes(c, 1), u, v)
        if step < SUB - 1:
            up = fold_north(cells, state[0][-1], state[1][-1])
            w = [over[i, k] for i in range(5)]
            folded[k] = advance(w, cells, lanes(cells, 1), lanes(cells, -1), up, rows(cells, 1))

    zero = jnp.zeros((8, 128), F32)
    above, ratio = [zero] * count, [zero] * count

    def pivots(k):
        for j, s in enumerate(spans):
            link = jnp.where(deep[j] > float(k + 1), mix[k, s], 0.0) if k < depth - 1 else zero
            inv = 1.0 / (1.0 + above[j] + link + above[j] * ratio[j])
            columns[0, k, s] = inv
            columns[1, k, s] = link
            above[j], ratio[j] = link, -link * inv

    for s, x in zip(spans, deep):
        surface_wet[s] = jnp.where(x > 0.0, 1.0, 0.0)
    for k in range(0, depth, GROUP):
        fold_coefficients(range(k, min(k + GROUP, depth)))
    for k in range(depth):
        if k % PART == 0:
            for copy in flows[k // PART]:
                copy.wait()
        coefficients(k)
    for k in range(depth):
        if k % PART == 0:
            cells[k // PART].wait()
        substep(k, 0)
    mixing.wait()
    for step in range(1, SUB):
        for k in range(depth):
            substep(k, step)
            if step == 1:
                pivots(k)


def fold_faces(deep, own_deep, toward_east, toward_west):
    easts = [jnp.minimum(x, y) for x, y in zip(deep, toward_east(deep))]
    norths = [jnp.minimum(x, fold_north(x, y, y)) for x, y in zip(deep, own_deep)]
    return list(zip(easts, toward_west(easts), norths, [rows(x, 1) for x in norths]))


def fold_weights(flows, faces, levels, toward_west):
    row = row_index()
    turned = [rows(x, 4) for x in flows]
    e_half = [0.5 * jnp.where(row < 4, y, x) for x, y in zip(flows, turned)]
    n_half = [0.5 * jnp.where(row < 4, x, y) for x, y in zip(flows, turned)]
    w_half = toward_west(e_half)
    s_half = [rows(x, 1) for x in n_half]
    return [
        stencil(face(e, east > k), face(n, north > k), face(w, west > k), face(s, south > k))
        for e, n, w, s, (east, west, north, south), k in zip(e_half, n_half, w_half, s_half, faces, levels)
    ]


def block_faces(deep, beyond):
    norths = [jnp.minimum(x, y) for x, y in zip(deep, north_of(deep, beyond))]
    souths = south_of(norths)
    souths[0] = jnp.where(row_index() == 0, 0.0, souths[0])
    return list(zip(norths, souths))


def fold_north(fold, first, second):
    row = row_index()
    return jnp.where((row & 3) == 3, jnp.where(row < 4, rows(first, 4), second), rows(fold, -1))


def fold_levels(fold):
    row = row_index()
    deep = jnp.zeros((8, 128), F32)
    for r in range(4):
        deep = jnp.where((row & 3) == r, jnp.broadcast_to(fold[r, 12:13], (8, 128)), deep)
    return deep


def corners_kernel(depth, size, fold, west, east, blocks, to_core, to_odd):
    me = lax.axis_index("lon")
    even = lax.rem(me, 2) == 0
    spans = [slice(0, 8), slice(8, 16)]
    stacks = [stack_of(fold, depth, span) for span in spans]
    stacks[1].append(lambda: fold_levels(fold))
    for span, found in zip(spans, edge_columns(stacks)):
        for b, tile in enumerate(found):
            blocks[b, span] = tile
        w1, e1 = found[0], found[3]
        to_core[span] = jnp.where(even, e1, w1)
        odd = jnp.where(even, w1, e1)
        odd = jnp.where(me == 0, west[span], odd)
        to_odd[span] = jnp.where(me == size - 1, east[span], odd)


def edge_side(depth, rows_count, cells, flows, fold_cells, fold_flows):
    lane, row = lane_index(), row_index()
    level = (lane & 31).astype(F32)
    count = rows_count // 8

    def plus(tiles):
        turned = [lanes(x, 32) for x in tiles]
        return [turned[0]] + [jnp.where(lane < 32, p, x) for p, x in zip(turned, turned[1:])]

    def minus(tiles):
        turned = [lanes(x, -32) for x in tiles]
        return [jnp.where(lane >= 96, q, x) for x, q in zip(turned, turned[1:])] + [turned[2]]

    at_levels = (lane & 96) + depth
    deep = [[take(cells[b][0][j], at_levels) for j in range(count)] for b in range(3)]
    fold_deep = []
    for b in range(3):
        found = take(fold_flows[b], at_levels)
        fold_deep.append(jnp.where(row < 4, rows(found, 4), found))
    over_faces = fold_faces(fold_deep, [deep[b][-1] for b in range(3)], plus, minus)
    over = fold_weights(fold_flows, over_faces, [level] * 3, minus)

    weights = [[None] * count for _ in range(3)]
    meridional = [block_faces(deep[b], fold_deep[b]) for b in range(3)]
    halves = [[0.5 * x for x in flows[b][1]] for b in range(3)]
    southern = [south_of(x) for x in halves]
    for j in range(count):
        line = [deep[b][j] for b in range(3)]
        easts = [jnp.minimum(x, y) for x, y in zip(line, minus(line))]
        e_half = [0.5 * flows[b][0][j] for b in range(3)]
        for b, (east, west, he, hw) in enumerate(zip(easts, plus(easts), e_half, plus(e_half))):
            north, south = meridional[b][j]
            weights[b][j] = stencil(
                face(he, east > level),
                face(halves[b][j], north > level),
                face(hw, west > level),
                face(southern[b][j], south > level),
            )

    state = [[list(cells[b][f]) for f in range(2)] for b in range(3)]
    folded = list(fold_cells)
    for step in range(SUB):
        fold_east, fold_west = plus(folded), minus(folded)
        following = [[[None] * count for _ in range(2)] for _ in range(3)]
        for f in range(2):
            for j in range(count):
                line = [state[b][f][j] for b in range(3)]
                east, west = minus(line), plus(line)
                for b in range(3):
                    following[b][f][j] = (east[b], west[b])
        next_fold = []
        for b in range(3):
            up = fold_north(folded[b], state[b][0][-1], state[b][1][-1])
            next_fold.append(
                advance(over[b], folded[b], fold_east[b], fold_west[b], up, rows(folded[b], 1))
            )
        for b in range(3):
            beyond = (rows(folded[b], 4), folded[b])
            for f in range(2):
                tiles = state[b][f]
                up, down = north_of(tiles, beyond[f]), south_of(tiles)
                state[b][f] = [
                    advance(weights[b][j], tiles[j], *following[b][f][j], up[j], down[j]) for j in range(count)
                ]
        folded = next_fold
    return state[1]


def last_kernel(
    depth, wet, inner, blocks, core, odd, fold, fold_core, fold_odd, pieces, columns, target_hbm,
    out_hbm, merged, out, target, sems, other,
):
    targets = pltpu.make_async_copy(target_hbm, target, other.at[0])
    targets.start()
    lane, row = lane_index(), row_index()
    size = pieces.shape[0]
    rows_count = inner.shape[2]
    count = rows_count // 8
    spans = [slice(8 * j, 8 * j + 8) for j in range(count)]
    me = lax.axis_index("lon")
    even = lax.rem(me, 2) == 0

    def received(f, s, west):
        a, b = core[f, s], odd[f, s]
        return jnp.where(even, b, a) if west else jnp.where(even, a, b)

    def own(b, f, s):
        return blocks[b, f, s]

    sides = []
    for west in (True, False):
        near, far = (0, 1) if west else (3, 2)
        here = [[[own(b, f, s) for s in spans] for f in range(4)] for b in (near, far)]
        there = [[received(f, s, west) for s in spans] for f in range(4)]
        a, b = fold_core[...], fold_odd[...]
        letter = jnp.where(even, b, a) if west else jnp.where(even, a, b)
        line = [there, here[0], here[1]] if west else [here[1], here[0], there]
        cells_near = [fold[near, 0:8], fold[far, 0:8]]
        flows_near = [fold[near, 8:16], fold[far, 8:16]]
        if west:
            fold_cells = [letter[0:8]] + cells_near
            fold_flows = [letter[8:16]] + flows_near
        else:
            fold_cells = cells_near[::-1] + [letter[0:8]]
            fold_flows = flows_near[::-1] + [letter[8:16]]
        sides.append(
            edge_side(depth, rows_count, [x[0:2] for x in line], [x[2:4] for x in line], fold_cells, fold_flows)
        )

    order = gather_order()
    group_even = ((lane >> 2) & 1) == 0
    for f in range(2):
        for j, s in enumerate(spans):
            a = take(sides[0][f][j], order)
            b = lanes(take(sides[1][f][j], order), -4)
            merged[0, f, s] = jnp.where(group_even, a, b)
            merged[1, f, s] = jnp.where(group_even, b, a)

    surface = [[jnp.zeros((8, 128), F32) for _ in spans] for _ in range(2)]
    targets.wait()
    for a in range(size):
        for s in range(2):
            goal = target[s, a]
            hits = [row + 8 * j == goal for j in range(count)]
            for f in range(2):
                piece = jnp.broadcast_to(pieces[a, 2 * f + s : 2 * f + s + 1], (8, 128))
                surface[f] = [x + jnp.where(hit, piece, 0.0) for x, hit in zip(surface[f], hits)]

    outer = (lane < 4) | (lane >= 124)
    partial_value = [[None] * count for _ in range(2)]
    for k in range(depth):
        for f in range(2):
            for j, s in enumerate(spans):
                cell = inner[f, k, s]
                cell = jnp.where(outer, lanes(merged[k % 2, f, s], -4 * k), cell)
                if k == 0:
                    cell = cell + FLUX_GAIN * surface[f][j] * wet[s]
                else:
                    cell = cell + columns[1, k - 1, s] * partial_value[f][j]
                value = cell * columns[0, k, s]
                partial_value[f][j] = value
                out[f, k, s] = value
    copies = []
    for k in range(depth - 1, -1, -1):
        if k < depth - 1:
            for f in range(2):
                for j, s in enumerate(spans):
                    value = out[f, k, s] + columns[1, k, s] * columns[0, k, s] * partial_value[f][j]
                    partial_value[f][j] = value
                    out[f, k, s] = value
        if k % GROUP == 0:
            part = pl.ds(k, min(GROUP, depth - k))
            copy = pltpu.make_async_copy(out.at[:, part], out_hbm.at[:, part], sems.at[k // GROUP])
            copy.start()
            copies.append(copy)
    for copy in copies:
        copy.wait()


def on_device(
    tracers,
    east_flow,
    north_flow,
    mixing,
    depth_levels,
    atm_flux,
    source_blocks,
    target_rows,
    regrid_weights,
):
    size = lax.axis_size("lon")
    depth, lat = tracers.shape[1], tracers.shape[2]
    dma = pltpu.SemaphoreType.DMA
    band = [
        pltpu.VMEM((2, depth, 8, 128), F32),
        pltpu.VMEM((depth, 8, 128), F32),
        pltpu.VMEM((depth, 8, 128), F32),
        pltpu.VMEM((8, 128), jnp.int32),
    ]
    top, west_corner, east_corner = call(
        functools.partial(fold_kernel, depth),
        (shape(depth, 16, 128), shape(16, 128), shape(16, 128)),
        [HBM] * 4,
        [*band, dma((4,))],
        cost=cost(0.1),
        name="fold_rows",
    )(*in_hbm(tracers, east_flow, north_flow, depth_levels))
    fold = lax.ppermute(top, "lon", [(i, size - 1 - i) for i in range(size)])

    plane = shape(depth, lat, 128)
    block = [shape(2, depth, lat, 128), plane, plane, pltpu.VMEM((lat, 128), jnp.int32)]
    blocks, to_core, to_odd = call(
        functools.partial(columns_kernel, depth),
        (shape(4, 4, lat, 128), shape(4, lat, 128), shape(4, lat, 128)),
        [HBM] * 4,
        [*block, dma((5,))],
        cost=cost(0.1),
        name="edge_columns",
    )(*in_hbm(tracers, east_flow, north_flow, depth_levels))
    core = lax.ppermute(to_core, "lon", [(i, i ^ 1) for i in range(size)])
    odd = lax.ppermute(to_odd, "lon", [(i, (i + (1 if i % 2 else -1)) % size) for i in range(size)])

    (pieces,) = call(
        functools.partial(regrid_kernel, size),
        (shape(size // 2, 8, 128),),
        [HBM, HBM, HBM],
        [
            pltpu.VMEM((2 * atm_flux.shape[1], 128, 128), F32),
            pltpu.VMEM((size, 2, 128, 128), F32),
            pltpu.VMEM((size, 4, 8, 128), F32),
            pltpu.VMEM(atm_flux.shape, F32),
            pltpu.SMEM((2, size), jnp.int32),
            dma((2,)),
            dma((4,)),
        ],
        cost=cost(0.1),
        name="regrid",
    )(*in_hbm(atm_flux, regrid_weights, jnp.transpose(source_blocks[0])))
    pieces = pieces.reshape(size, 4, 128)
    received = lax.all_to_all(pieces, "lon", split_axis=0, concat_axis=0, tiled=True)

    fold_blocks, fold_core, fold_odd = call(
        functools.partial(corners_kernel, depth, size),
        (shape(4, 16, 128), shape(16, 128), shape(16, 128)),
        [VMEM] * 3,
        cost=cost(0.1),
        name="fold_corners",
    )(*in_vmem(fold, west_corner, east_corner))
    fold_core = lax.ppermute(fold_core, "lon", [(i, i ^ 1) for i in range(size)])
    near = [(i, i + (1 if i % 2 else -1)) for i in range(1, size - 1)]
    fold_odd = lax.ppermute(fold_odd, "lon", [(0, 0), *near, (size - 1, size - 1)])

    inner, wet, columns = call(
        functools.partial(inner_kernel, depth),
        (
            shape(2, depth, lat, 128), shape(lat, 128),
            shape(2, depth, lat, 128),
        ),
        [HBM] * 5 + [VMEM],
        [
            *block,
            shape(depth - 1, lat, 128),
            shape(5, depth, lat, 128),
            shape(depth, 8, 128),
            shape(5, depth, 8, 128),
            dma((2,)),
            dma((2, -(-depth // PART))),
            dma((-(-depth // PART),)),
        ],
        cost=cost(0.1),
        name="inner_cells",
    )(*in_hbm(tracers, east_flow, north_flow, depth_levels, mixing), *in_vmem(fold))

    (result,) = call(
        functools.partial(last_kernel, depth),
        (jax.ShapeDtypeStruct((2, depth, lat, 128), F32),),
        [VMEM] * 10 + [HBM],
        [
            pltpu.VMEM((2, 2, lat, 128), F32),
            pltpu.VMEM((2, depth, lat, 128), F32),
            pltpu.SMEM((2, size), jnp.int32),
            dma((-(-depth // GROUP),)),
            dma((1,)),
        ],
        out_specs=[HBM],
        cost=cost(0.1),
        name="edges_and_columns",
    )(
        *in_vmem(wet, inner, blocks, core, odd, fold_blocks, fold_core, fold_odd, received, columns),
        *in_hbm(jnp.transpose(target_rows[:, 0, :])),
    )
    return result


def solution(mesh):
    return jax.shard_map(
        on_device,
        mesh=mesh,
        in_specs=(
            P(None, "ens", None, "lon"),
            P("ens", None, "lon"),
            P("ens", None, "lon"),
            P("ens", None, "lon"),
            P(None, "lon"),
            P("ens", "lon", None),
            P("lon", None, None),
            P(None, "lon", None),
            P("lon", None, None, None, None),
        ),
        out_specs=P(None, "ens", None, "lon"),
        check_vma=False,
    )
```

```python
import functools

import jax
import jax.numpy as jnp
from jax import lax
from jax.experimental import pallas as pl
from jax.experimental.pallas import tpu as pltpu
from jax.sharding import PartitionSpec as P

SUB = 4
DIFFUSION = 0.12
FLUX_GAIN = 0.5
GROUP = 5
PART = 13
PIECE_ROW = ((0, 4), (8, 12))
F32 = jnp.float32
VMEM = pl.BlockSpec(memory_space=pltpu.VMEM)
SMEM = pl.BlockSpec(memory_space=pltpu.SMEM)
HBM = pl.BlockSpec(memory_space=pltpu.HBM)
VMEM_LIMIT = 16 * 1024 * 1024


def lane_index():
    return lax.broadcasted_iota(jnp.int32, (8, 128), 1)


def row_index():
    return lax.broadcasted_iota(jnp.int32, (8, 128), 0)


def lanes(tile, shift):
    shift = shift % 128
    return pltpu.roll(tile, shift, 1) if shift else tile


def rows(tile, shift):
    shift = shift % 8
    return pltpu.roll(tile, shift, 0) if shift else tile


def take(tile, index):
    return jnp.take_along_axis(tile, index, axis=1)


def spread_order():
    lane = lane_index()
    return 4 * (lane & 31) + (lane >> 5)


def gather_order():
    lane = lane_index()
    return 32 * (lane & 3) + (lane >> 2)


def call(body, out, in_specs, scratch=(), out_specs=None, cost=None, name=None):
    return pl.pallas_call(
        body,
        out_shape=out,
        in_specs=in_specs,
        out_specs=out_specs if out_specs is not None else [VMEM] * len(out),
        scratch_shapes=list(scratch),
        compiler_params=pltpu.CompilerParams(vmem_limit_bytes=VMEM_LIMIT),
        cost_estimate=cost,
        name=name,
    )


def cost(micros):
    return pl.CostEstimate(flops=0, bytes_accessed=int(micros * 3.0e6), transcendentals=0)


def shape(*dims):
    return pltpu.VMEM(dims, F32)


def in_hbm(*arrays):
    return [pltpu.with_memory_space_constraint(x, pltpu.HBM) for x in arrays]


def in_vmem(*arrays):
    return [pltpu.with_memory_space_constraint(x, pltpu.VMEM) for x in arrays]


def face(half, open_face):
    return jnp.where(open_face, half + DIFFUSION, 0.0), jnp.where(open_face, half - DIFFUSION, 0.0)


def stencil(east, north, west, south):
    a_e, b_e = east
    a_n, b_n = north
    a_w, b_w = west
    a_s, b_s = south
    return (((1.0 - a_e) + b_w) - a_n) + b_s, b_e, a_w, b_n, a_s


def advance(weights, cell, east, west, north, south):
    own, b_e, a_w, b_n, a_s = weights
    return (own * cell + (a_w * west - b_e * east)) + (a_s * south - b_n * north)


def north_of(tiles, beyond):
    row = row_index()
    turned = [rows(t, -1) for t in tiles]
    return [jnp.where(row == 7, n, t) for t, n in zip(turned, turned[1:] + [beyond])]


def south_of(tiles):
    row = row_index()
    turned = [rows(t, 1) for t in tiles]
    return [turned[0]] + [jnp.where(row == 0, p, t) for p, t in zip(turned, turned[1:])]


def northern_rows(t_hbm, e_hbm, n_hbm, d_hbm, t, e, n, d, sems):
    top = pl.ds(t_hbm.shape[2] - 8, 8)
    return [
        pltpu.make_async_copy(t_hbm.at[:, :, top], t, sems.at[0]),
        pltpu.make_async_copy(e_hbm.at[:, top], e, sems.at[1]),
        pltpu.make_async_copy(n_hbm.at[:, top], n, sems.at[2]),
        pltpu.make_async_copy(d_hbm.at[top], d, sems.at[3]),
    ]


def edge_columns(stacks):
    lane = lane_index()
    outer = (lane < 8) | (lane >= 120)
    group = [((lane >> 2) & 3) == c for c in range(3)]
    sums = [[None] * 4 for _ in stacks]
    for k in range(max(len(x) for x in stacks)):
        for total, stack in zip(sums, stacks):
            if k < len(stack):
                tile = lanes(jnp.where(outer, stack[k](), 0.0), 4 * k)
                total[k % 4] = tile if total[k % 4] is None else total[k % 4] + tile
    offsets = (0, 1, -2, -1)
    found = []
    for offset in offsets:
        for total in sums:
            a, b, c, d = [total[(g - offset) % 4] for g in range(4)]
            tile = jnp.where(group[0], a, jnp.where(group[1], b, jnp.where(group[2], c, d)))
            found.append(lanes(tile, -4 * offset))
    order = spread_order()
    found = [take(x, order) for x in found]
    return [[found[b * len(stacks) + i] for b in range(4)] for i in range(len(stacks))]


def stack_of(ref, depth, *where):
    return [lambda k=k: ref[(k, *where)] for k in range(depth)]


def pack_kernel(
    depth, t_hbm, e_hbm, n_hbm, d_hbm, out, west, east, blocks, to_core, to_odd, t, e, n, d, sems
):
    copies = [
        pltpu.make_async_copy(d_hbm, d, sems.at[0]),
        pltpu.make_async_copy(t_hbm, t, sems.at[1]),
        pltpu.make_async_copy(e_hbm, e, sems.at[2]),
        pltpu.make_async_copy(n_hbm, n, sems.at[3]),
    ]
    for copy in copies:
        copy.start()
    me = lax.axis_index("lon")
    even = lax.rem(me, 2) == 0
    row = row_index()
    turn = 127 - lane_index()
    count = t.shape[2] // 8
    spans = [slice(8 * j, 8 * j + 8) for j in range(count)]
    fields = (t.at[0], t.at[1], e, n)

    def columns(chosen):
        places = [(f, j) for f in chosen for j in range(count)]
        stacks = [stack_of(fields[f], depth, spans[j]) for f, j in places]
        if 0 in chosen:
            for stack, span in zip(stacks, spans):
                stack.append(lambda span=span: d[span].astype(F32))
        for (f, j), found in zip(places, edge_columns(stacks)):
            for b, tile in enumerate(found):
                blocks[b, f, spans[j]] = tile
            w1, e1 = found[0], found[3]
            to_core[f, spans[j]] = jnp.where(even, e1, w1)
            to_odd[f, spans[j]] = jnp.where(even, w1, e1)
            place = f * count + j
            out[depth + place // 2, 8 * (place % 2) : 8 * (place % 2) + 8] = jnp.where(me == 0, w1, e1)

    copies[0].wait()
    copies[1].wait()
    columns((0, 1))
    copies[2].wait()
    copies[3].wait()
    levels = d[spans[-1]].astype(F32)
    for k in range(depth):
        cells = jnp.where(row < 4, rows(t[0, k, spans[-1]], 4), t[1, k, spans[-1]])
        flows = jnp.where(row < 4, rows(n[k, spans[-1]], 4), e[k, spans[-1]])
        if k < 4:
            flows = jnp.where(row == 4, rows(levels, -k), flows)
        out[k, 0:8] = take(cells, turn)
        out[k, 8:16] = take(flows, turn)
    columns((2, 3))
    halves = [slice(0, 8), slice(8, 16)]
    stacks = [stack_of(out, depth, span) for span in halves]
    stacks[1].append(lambda: take(levels, turn))
    for span, found in zip(halves, edge_columns(stacks)):
        east[span], west[span] = found[0], found[3]


def regrid_kernel(size, atm_hbm, w_hbm, src_hbm, west, east, out, wide, w, part, atm, src, sems, w_sems):
    first = [pltpu.make_async_copy(atm_hbm, atm, sems.at[0]), pltpu.make_async_copy(src_hbm, src, sems.at[1])]
    for copy in first:
        copy.start()
    parts = w_sems.shape[0]
    each = size // parts
    weights = [
        pltpu.make_async_copy(w_hbm.at[0, pl.ds(p * each, each)], w.at[pl.ds(p * each, each)], w_sems.at[p])
        for p in range(parts)
    ]
    for copy in weights:
        copy.start()
    for copy in first:
        copy.wait()
    flat = atm[...].reshape(atm.shape[0] * atm.shape[1], atm.shape[2])
    count = flat.shape[0]
    blocks = atm.shape[1]
    columns = jnp.transpose(jnp.concatenate([flat, jnp.zeros((128 - count, 128), F32)], axis=0))
    for c in range(count):
        wide[c] = jnp.broadcast_to(columns[:, c : c + 1], (128, 128))
    row = row_index()
    me = lax.axis_index("lon")
    message = west[...]

    def fill(e, carry):
        out[e] = message
        return carry

    lax.fori_loop(0, size, fill, 0, unroll=8)
    out[lax.rem(2 * size - 2 - me, size)] = east[...]

    def owner(e, carry):
        for s in range(2):
            block = src[s, e]
            sums = [None, None]
            for i in range(16):
                span = slice(8 * i, 8 * i + 8)
                weight = w[e, s, span]
                for f in range(2):
                    term = weight * wide[f * blocks + block, span]
                    sums[f] = term if sums[f] is None else sums[f] + term
            for f in range(2):
                part[e, 2 * f + s] = sums[f]
        return carry

    def letter(e, carry):
        for f in range(2):
            a, b = part[e, 2 * f], part[e, 2 * f + 1]
            tile = jnp.where(row < 4, a, b) + rows(jnp.where(row < 4, b, a), 4)
            tile = tile + rows(tile, -1)
            tile = tile + rows(tile, -2)
            span = slice(8 * f, 8 * f + 8)
            out[e, span] = jnp.where((row & 3) == 0, tile, out[e, span])
        return carry

    for p in range(parts):
        weights[p].wait()
        lax.fori_loop(p * each, (p + 1) * each, owner, 0, unroll=4)
        lax.fori_loop(p * each, (p + 1) * each, letter, 0, unroll=8)


def inner_kernel(
    depth, t_hbm, e_hbm, n_hbm, d_hbm, mix_hbm, out, surface_wet, columns,
    t, e, n, d, mix, weights, sems, flow_sems, cell_sems,
):
    levels = pltpu.make_async_copy(d_hbm, d, sems.at[0])
    mixing = pltpu.make_async_copy(mix_hbm, mix, sems.at[1])
    parts = [pl.ds(k, min(PART, depth - k)) for k in range(0, depth, PART)]
    flows = [
        (
            pltpu.make_async_copy(e_hbm.at[p], e.at[p], flow_sems.at[0, i]),
            pltpu.make_async_copy(n_hbm.at[p], n.at[p], flow_sems.at[1, i]),
        )
        for i, p in enumerate(parts)
    ]
    cells = [pltpu.make_async_copy(t_hbm.at[:, p], t.at[:, p], cell_sems.at[i]) for i, p in enumerate(parts)]
    levels.start()
    for pair in flows:
        for copy in pair:
            copy.start()
    for copy in cells:
        copy.start()
    mixing.start()
    levels.wait()
    row = row_index()
    count = t.shape[2] // 8
    spans = [slice(8 * j, 8 * j + 8) for j in range(count)]
    deep = [d[s].astype(F32) for s in spans]

    def plus(tiles):
        return [lanes(x, 1) for x in tiles]

    def minus(tiles):
        return [lanes(x, -1) for x in tiles]

    east_faces = [jnp.minimum(x, y) for x, y in zip(deep, minus(deep))]
    faces = list(zip(east_faces, plus(east_faces), block_faces(deep, deep[-1])))

    def coefficients(k):
        e_half = [0.5 * e[k, s] for s in spans]
        n_half = [0.5 * n[k, s] for s in spans]
        for s, he, hw, hn, hs, (east, west, (north, south)) in zip(
            spans, e_half, plus(e_half), n_half, south_of(n_half), faces
        ):
            found = stencil(
                face(he, east > float(k)),
                face(hn, north > float(k)),
                face(hw, west > float(k)),
                face(hs, south > float(k)),
            )
            for i, x in enumerate(found):
                weights[i, k, s] = x

    def substep(k, step):
        source = out if step else t
        for f in range(2):
            state = [source[f, k, s] for s in spans]
            up, down = north_of(state, state[-1]), south_of(state)
            for s, c, u, v in zip(spans, state, up, down):
                w = [weights[i, k, s] for i in range(5)]
                out[f, k, s] = advance(w, c, lanes(c, -1), lanes(c, 1), u, v)

    zero = jnp.zeros((8, 128), F32)
    above, ratio = [zero] * count, [zero] * count

    def pivots(k):
        for j, s in enumerate(spans):
            link = jnp.where(deep[j] > float(k + 1), mix[k, s], 0.0) if k < depth - 1 else zero
            inv = 1.0 / (1.0 + above[j] + link + above[j] * ratio[j])
            columns[0, k, s] = inv
            columns[1, k, s] = link
            above[j], ratio[j] = link, -link * inv

    for s, x in zip(spans, deep):
        surface_wet[s] = jnp.where(x > 0.0, 1.0, 0.0)
    for k in range(depth):
        if k % PART == 0:
            for copy in flows[k // PART]:
                copy.wait()
        coefficients(k)
    for k in range(depth):
        if k % PART == 0:
            cells[k // PART].wait()
        substep(k, 0)
    mixing.wait()
    for step in range(1, SUB):
        for k in range(depth):
            substep(k, step)
            if step == 1:
                pivots(k)


def fold_faces(deep, own_deep, toward_east, toward_west):
    easts = [jnp.minimum(x, y) for x, y in zip(deep, toward_east(deep))]
    norths = [jnp.minimum(x, fold_north(x, y, y)) for x, y in zip(deep, own_deep)]
    return list(zip(easts, toward_west(easts), norths, [rows(x, 1) for x in norths]))


def fold_weights(flows, faces, levels, toward_west):
    row = row_index()
    turned = [rows(x, 4) for x in flows]
    e_half = [0.5 * jnp.where(row < 4, y, x) for x, y in zip(flows, turned)]
    n_half = [0.5 * jnp.where(row < 4, x, y) for x, y in zip(flows, turned)]
    w_half = toward_west(e_half)
    s_half = [rows(x, 1) for x in n_half]
    return [
        stencil(face(e, east > k), face(n, north > k), face(w, west > k), face(s, south > k))
        for e, n, w, s, (east, west, north, south), k in zip(e_half, n_half, w_half, s_half, faces, levels)
    ]


def block_faces(deep, beyond):
    norths = [jnp.minimum(x, y) for x, y in zip(deep, north_of(deep, beyond))]
    souths = south_of(norths)
    souths[0] = jnp.where(row_index() == 0, 0.0, souths[0])
    return list(zip(norths, souths))


def fold_north(fold, first, second):
    row = row_index()
    return jnp.where((row & 3) == 3, jnp.where(row < 4, rows(first, 4), second), rows(fold, -1))


def fold_levels(fold):
    row = row_index()
    deep = jnp.zeros((8, 128), F32)
    for r in range(4):
        deep = jnp.where((row & 3) == r, jnp.broadcast_to(fold[r, 12:13], (8, 128)), deep)
    return deep


def top_strip(depth, t, e, n, d, fold, strip, folded, weights, over):
    row = row_index()
    deep = d[...].astype(F32)
    fold_deep = fold_levels(fold)

    def plus(tiles):
        return [lanes(x, 1) for x in tiles]

    def minus(tiles):
        return [lanes(x, -1) for x in tiles]

    over_faces = fold_faces([fold_deep], [deep], plus, minus)
    east = jnp.minimum(deep, lanes(deep, -1))
    west = lanes(east, 1)
    north = jnp.minimum(deep, jnp.where(row == 7, fold_deep, rows(deep, -1)))
    south = rows(north, 1)
    for k in range(0, depth, GROUP):
        levels = range(k, min(k + GROUP, depth))
        found = fold_weights(
            [fold[k, 8:16] for k in levels], over_faces * len(levels), [float(k) for k in levels], minus
        )
        for k, tiles in zip(levels, found):
            for i, x in enumerate(tiles):
                over[i, k] = x
    for k in range(depth):
        he, hn = 0.5 * e[k], 0.5 * n[k]
        level = float(k)
        found = stencil(
            face(he, east > level),
            face(hn, north > level),
            face(lanes(he, 1), west > level),
            face(rows(hn, 1), south > level),
        )
        for i, x in enumerate(found):
            weights[i, k] = x
    for step in range(SUB):
        for k in range(depth):
            if step:
                one, two, cells = strip[0, k], strip[1, k], folded[k]
            else:
                one, two, cells = t[0, k], t[1, k], fold[k, 0:8]
            up_one = jnp.where(row == 7, rows(cells, 4), rows(one, -1))
            up_two = jnp.where(row == 7, cells, rows(two, -1))
            if step < SUB - 1:
                up = fold_north(cells, one, two)
                w = [over[i, k] for i in range(5)]
                folded[k] = advance(w, cells, lanes(cells, 1), lanes(cells, -1), up, rows(cells, 1))
            w = [weights[i, k] for i in range(5)]
            strip[0, k] = advance(w, one, lanes(one, -1), lanes(one, 1), up_one, rows(one, 1))
            strip[1, k] = advance(w, two, lanes(two, -1), lanes(two, 1), up_two, rows(two, 1))


def edge_side(depth, rows_count, cells, flows, fold_cells, fold_flows):
    lane, row = lane_index(), row_index()
    level = (lane & 31).astype(F32)
    count = rows_count // 8

    def plus(tiles):
        turned = [lanes(x, 32) for x in tiles]
        return [turned[0]] + [jnp.where(lane < 32, p, x) for p, x in zip(turned, turned[1:])]

    def minus(tiles):
        turned = [lanes(x, -32) for x in tiles]
        return [jnp.where(lane >= 96, q, x) for x, q in zip(turned, turned[1:])] + [turned[2]]

    at_levels = (lane & 96) + depth
    deep = [[take(cells[b][0][j], at_levels) for j in range(count)] for b in range(3)]
    fold_deep = []
    for b in range(3):
        found = take(fold_flows[b], at_levels)
        fold_deep.append(jnp.where(row < 4, rows(found, 4), found))
    over_faces = fold_faces(fold_deep, [deep[b][-1] for b in range(3)], plus, minus)
    over = fold_weights(fold_flows, over_faces, [level] * 3, minus)

    weights = [[None] * count for _ in range(3)]
    meridional = [block_faces(deep[b], fold_deep[b]) for b in range(3)]
    halves = [[0.5 * x for x in flows[b][1]] for b in range(3)]
    southern = [south_of(x) for x in halves]
    for j in range(count):
        yield
        line = [deep[b][j] for b in range(3)]
        easts = [jnp.minimum(x, y) for x, y in zip(line, minus(line))]
        e_half = [0.5 * flows[b][0][j] for b in range(3)]
        for b, (east, west, he, hw) in enumerate(zip(easts, plus(easts), e_half, plus(e_half))):
            north, south = meridional[b][j]
            weights[b][j] = stencil(
                face(he, east > level),
                face(halves[b][j], north > level),
                face(hw, west > level),
                face(southern[b][j], south > level),
            )

    state = [[list(cells[b][f]) for f in range(2)] for b in range(3)]
    folded = list(fold_cells)
    for step in range(SUB):
        yield
        beyond = [(rows(x, 4), x) for x in folded]
        if step < SUB - 1:
            fold_east, fold_west = plus(folded), minus(folded)
            ups = [fold_north(folded[b], state[b][0][-1], state[b][1][-1]) for b in range(3)]
            folded = [
                advance(over[b], folded[b], fold_east[b], fold_west[b], ups[b], rows(folded[b], 1)) for b in range(3)
            ]
        for f in range(2):
            yield
            east, west = [], []
            for j in range(count):
                line = [state[b][f][j] for b in range(3)]
                east.append(minus(line))
                west.append(plus(line))
            yield
            for b in range(3):
                tiles = state[b][f]
                up, down = north_of(tiles, beyond[b][f]), south_of(tiles)
                state[b][f] = [
                    advance(weights[b][j], tiles[j], east[j][b], west[j][b], up[j], down[j]) for j in range(count)
                ]
    return state[1]


def side_by_side(stages):
    results = [None] * len(stages)
    running = list(enumerate(stages))
    while running:
        left = []
        for i, stage in running:
            try:
                next(stage)
                left.append((i, stage))
            except StopIteration as end:
                results[i] = end.value
        running = left
    return results


def last_kernel(
    depth, t_hbm, e_hbm, n_hbm, d_hbm, wet, inner, blocks, core, odd, fold, mail, columns, target_hbm,
    out_hbm, t, e, n, d, strip, folded, top_weights, over, merged, out, target, sems, other,
):
    targets = pltpu.make_async_copy(target_hbm, target, other.at[4])
    band = northern_rows(t_hbm, e_hbm, n_hbm, d_hbm, t, e, n, d, other)
    for copy in band:
        copy.start()
    targets.start()
    lane, row = lane_index(), row_index()
    size = mail.shape[0]
    rows_count = inner.shape[2]
    count = rows_count // 8
    spans = [slice(8 * j, 8 * j + 8) for j in range(count)]
    me = lax.axis_index("lon")
    even = lax.rem(me, 2) == 0

    halves = [slice(0, 8), slice(8, 16)]
    stacks = [stack_of(fold, depth, span) for span in halves]
    stacks[1].append(lambda: fold_levels(fold))
    folds = edge_columns(stacks)
    west_mail = mail[lax.rem(size - me, size)]
    east_mail = mail[lax.rem(2 * size - 2 - me, size)]
    at_wrap = (me == 0) | (me == size - 1)

    def received(f, j, west):
        place = f * count + j
        wrapped = fold[depth + place // 2, 8 * (place % 2) : 8 * (place % 2) + 8]
        a, b = core[f, spans[j]], jnp.where(at_wrap, wrapped, odd[f, spans[j]])
        return jnp.where(even, b, a) if west else jnp.where(even, a, b)

    def own(b, f, s):
        return blocks[b, f, s]

    sides = []
    for west in (True, False):
        near, far = (0, 1) if west else (3, 2)
        here = [[[own(b, f, s) for s in spans] for f in range(4)] for b in (near, far)]
        there = [[received(f, j, west) for j in range(count)] for f in range(4)]
        letter = west_mail if west else east_mail
        line = [there, here[0], here[1]] if west else [here[1], here[0], there]
        cells_near = [folds[0][near], folds[0][far]]
        flows_near = [folds[1][near], folds[1][far]]
        if west:
            fold_cells = [letter[0:8]] + cells_near
            fold_flows = [letter[8:16]] + flows_near
        else:
            fold_cells = cells_near[::-1] + [letter[0:8]]
            fold_flows = flows_near[::-1] + [letter[8:16]]
        sides.append(
            edge_side(depth, rows_count, [x[0:2] for x in line], [x[2:4] for x in line], fold_cells, fold_flows)
        )

    sides = side_by_side(sides)
    for copy in band:
        copy.wait()
    top_strip(depth, t, e, n, d, fold, strip, folded, top_weights, over)
    order = gather_order()
    group_even = ((lane >> 2) & 1) == 0
    for f in range(2):
        for j, s in enumerate(spans):
            a = take(sides[0][f][j], order)
            b = lanes(take(sides[1][f][j], order), -4)
            merged[0, f, s] = jnp.where(group_even, a, b)
            merged[1, f, s] = jnp.where(group_even, b, a)

    surface = [[jnp.zeros((8, 128), F32) for _ in spans] for _ in range(2)]
    targets.wait()
    for a in range(size):
        for s in range(2):
            goal = target[s, a]
            hits = [row + 8 * j == goal for j in range(count)]
            for f in range(2):
                piece = jnp.broadcast_to(mail[a, PIECE_ROW[f][s] : PIECE_ROW[f][s] + 1], (8, 128))
                surface[f] = [x + jnp.where(hit, piece, 0.0) for x, hit in zip(surface[f], hits)]

    outer = (lane < 4) | (lane >= 124)
    for k in range(depth):
        for f in range(2):
            for j, s in enumerate(spans):
                cell = inner[f, k, s]
                if j == count - 1:
                    cell = jnp.where(row >= 4, strip[f, k], cell)
                out[f, k, s] = jnp.where(outer, lanes(merged[k % 2, f, s], -4 * k), cell)
    partial_value = [[None] * count for _ in range(2)]
    for k in range(depth):
        for f in range(2):
            for j, s in enumerate(spans):
                cell = out[f, k, s]
                if k == 0:
                    cell = cell + FLUX_GAIN * surface[f][j] * wet[s]
                else:
                    cell = cell + columns[1, k - 1, s] * partial_value[f][j]
                value = cell * columns[0, k, s]
                partial_value[f][j] = value
                out[f, k, s] = value
    copies = []
    for k in range(depth - 1, -1, -1):
        if k < depth - 1:
            for f in range(2):
                for j, s in enumerate(spans):
                    value = out[f, k, s] + columns[1, k, s] * columns[0, k, s] * partial_value[f][j]
                    partial_value[f][j] = value
                    out[f, k, s] = value
        if k % GROUP == 0:
            part = pl.ds(k, min(GROUP, depth - k))
            copy = pltpu.make_async_copy(out.at[:, part], out_hbm.at[:, part], sems.at[k // GROUP])
            copy.start()
            copies.append(copy)
    for copy in copies:
        copy.wait()


def on_device(
    tracers,
    east_flow,
    north_flow,
    mixing,
    depth_levels,
    atm_flux,
    source_blocks,
    target_rows,
    regrid_weights,
):
    size = lax.axis_size("lon")
    depth, lat = tracers.shape[1], tracers.shape[2]
    dma = pltpu.SemaphoreType.DMA
    near = [(i, i + (1 if i % 2 else -1)) for i in range(1, size - 1)]
    band = [
        shape(2, depth, 8, 128),
        shape(depth, 8, 128),
        shape(depth, 8, 128),
        pltpu.VMEM((8, 128), jnp.int32),
    ]
    plane = shape(depth, lat, 128)
    block = [shape(2, depth, lat, 128), plane, plane, pltpu.VMEM((lat, 128), jnp.int32)]
    strips = shape(4, lat, 128)
    fields = in_hbm(tracers, east_flow, north_flow, depth_levels)

    message, west_corner, east_corner, blocks, to_core, to_odd = call(
        functools.partial(pack_kernel, depth),
        (shape(depth + lat // 4, 16, 128), shape(16, 128), shape(16, 128), shape(4, 4, lat, 128), strips, strips),
        [HBM] * 4,
        [*block, dma((4,))],
        cost=cost(0.1),
        name="fold_rows_and_columns",
    )(*fields)
    fold = lax.ppermute(message, "lon", [(i, size - 1 - i) for i in range(size)])
    core = lax.ppermute(to_core, "lon", [(i, i ^ 1) for i in range(size)])
    odd = lax.ppermute(to_odd, "lon", [(0, 0), *near, (size - 1, size - 1)])

    (letters,) = call(
        functools.partial(regrid_kernel, size),
        (shape(size, 16, 128),),
        [HBM, HBM, HBM, VMEM, VMEM],
        [
            pltpu.VMEM((2 * atm_flux.shape[1], 128, 128), F32),
            pltpu.VMEM((size, 2, 128, 128), F32),
            pltpu.VMEM((size, 4, 8, 128), F32),
            pltpu.VMEM(atm_flux.shape, F32),
            pltpu.SMEM((2, size), jnp.int32),
            dma((2,)),
            dma((2,)),
        ],
        cost=cost(0.1),
        name="regrid",
    )(
        *in_hbm(atm_flux, regrid_weights, jnp.transpose(source_blocks[0])),
        *in_vmem(west_corner, east_corner),
    )
    mail = lax.all_to_all(letters, "lon", split_axis=0, concat_axis=0, tiled=True)

    inner, wet, columns = call(
        functools.partial(inner_kernel, depth),
        (shape(2, depth, lat, 128), shape(lat, 128), shape(2, depth, lat, 128)),
        [HBM] * 5,
        [
            *block,
            shape(depth - 1, lat, 128),
            shape(5, depth, lat, 128),
            dma((2,)),
            dma((2, -(-depth // PART))),
            dma((-(-depth // PART),)),
        ],
        cost=cost(0.1),
        name="inner_cells",
    )(*fields, *in_hbm(mixing))

    (result,) = call(
        functools.partial(last_kernel, depth),
        (jax.ShapeDtypeStruct((2, depth, lat, 128), F32),),
        [HBM] * 4 + [VMEM] * 8 + [HBM],
        [
            *band,
            shape(2, depth, 8, 128),
            shape(depth, 8, 128),
            shape(5, depth, 8, 128),
            shape(5, depth, 8, 128),
            pltpu.VMEM((2, 2, lat, 128), F32),
            pltpu.VMEM((2, depth, lat, 128), F32),
            pltpu.SMEM((2, size), jnp.int32),
            dma((-(-depth // GROUP),)),
            dma((5,)),
        ],
        out_specs=[HBM],
        cost=cost(0.1),
        name="edges_and_columns",
    )(
        *fields,
        *in_vmem(wet, inner, blocks, core, odd, fold, mail, columns),
        *in_hbm(jnp.transpose(target_rows[:, 0, :])),
    )
    return result


def solution(mesh):
    return jax.shard_map(
        on_device,
        mesh=mesh,
        in_specs=(
            P(None, "ens", None, "lon"),
            P("ens", None, "lon"),
            P("ens", None, "lon"),
            P("ens", None, "lon"),
            P(None, "lon"),
            P("ens", "lon", None),
            P("lon", None, None),
            P(None, "lon", None),
            P("lon", None, None, None, None),
        ),
        out_specs=P(None, "ens", None, "lon"),
        check_vma=False,
    )
```

```python
import functools

import jax
import jax.numpy as jnp
from jax import lax
from jax.experimental import pallas as pl
from jax.experimental.pallas import tpu as pltpu
from jax.sharding import PartitionSpec as P

SUB = 4
DIFFUSION = 0.12
FLUX_GAIN = 0.5
GROUP = 5
PART = 13
PIECE_ROW = ((0, 4), (8, 12))
F32 = jnp.float32
VMEM = pl.BlockSpec(memory_space=pltpu.VMEM)
SMEM = pl.BlockSpec(memory_space=pltpu.SMEM)
HBM = pl.BlockSpec(memory_space=pltpu.HBM)
VMEM_LIMIT = 16 * 1024 * 1024


def lane_index():
    return lax.broadcasted_iota(jnp.int32, (8, 128), 1)


def row_index():
    return lax.broadcasted_iota(jnp.int32, (8, 128), 0)


def lanes(tile, shift):
    shift = shift % 128
    return pltpu.roll(tile, shift, 1) if shift else tile


def rows(tile, shift):
    shift = shift % 8
    return pltpu.roll(tile, shift, 0) if shift else tile


def take(tile, index):
    return jnp.take_along_axis(tile, index, axis=1)


def spread_order():
    lane = lane_index()
    return 4 * (lane & 31) + (lane >> 5)


def gather_order():
    lane = lane_index()
    return 32 * (lane & 3) + (lane >> 2)


def call(body, out, in_specs, scratch=(), out_specs=None, cost=None, name=None):
    return pl.pallas_call(
        body,
        out_shape=out,
        in_specs=in_specs,
        out_specs=out_specs if out_specs is not None else [VMEM] * len(out),
        scratch_shapes=list(scratch),
        compiler_params=pltpu.CompilerParams(vmem_limit_bytes=VMEM_LIMIT),
        cost_estimate=cost,
        name=name,
    )


def cost(micros):
    return pl.CostEstimate(flops=0, bytes_accessed=int(micros * 3.0e6), transcendentals=0)


def shape(*dims):
    return pltpu.VMEM(dims, F32)


def in_hbm(*arrays):
    return [pltpu.with_memory_space_constraint(x, pltpu.HBM) for x in arrays]


def in_vmem(*arrays):
    return [pltpu.with_memory_space_constraint(x, pltpu.VMEM) for x in arrays]


def face(half, open_face):
    return jnp.where(open_face, half + DIFFUSION, 0.0), jnp.where(open_face, half - DIFFUSION, 0.0)


def stencil(east, north, west, south):
    a_e, b_e = east
    a_n, b_n = north
    a_w, b_w = west
    a_s, b_s = south
    return (((1.0 - a_e) + b_w) - a_n) + b_s, b_e, a_w, b_n, a_s


def advance(weights, cell, east, west, north, south):
    own, b_e, a_w, b_n, a_s = weights
    return (own * cell + (a_w * west - b_e * east)) + (a_s * south - b_n * north)


def north_of(tiles, beyond):
    row = row_index()
    turned = [rows(t, -1) for t in tiles]
    return [jnp.where(row == 7, n, t) for t, n in zip(turned, turned[1:] + [beyond])]


def south_of(tiles):
    row = row_index()
    turned = [rows(t, 1) for t in tiles]
    return [turned[0]] + [jnp.where(row == 0, p, t) for p, t in zip(turned, turned[1:])]


def northern_rows(t_hbm, e_hbm, n_hbm, d_hbm, t, e, n, d, sems):
    top = pl.ds(t_hbm.shape[2] - 8, 8)
    return [
        pltpu.make_async_copy(t_hbm.at[:, :, top], t, sems.at[0]),
        pltpu.make_async_copy(e_hbm.at[:, top], e, sems.at[1]),
        pltpu.make_async_copy(n_hbm.at[:, top], n, sems.at[2]),
        pltpu.make_async_copy(d_hbm.at[top], d, sems.at[3]),
    ]


def edge_columns(stacks):
    lane = lane_index()
    outer = (lane < 8) | (lane >= 120)
    group = [((lane >> 2) & 3) == c for c in range(3)]
    sums = [[None] * 4 for _ in stacks]
    for k in range(max(len(x) for x in stacks)):
        for total, stack in zip(sums, stacks):
            if k < len(stack):
                tile = lanes(jnp.where(outer, stack[k](), 0.0), 4 * k)
                total[k % 4] = tile if total[k % 4] is None else total[k % 4] + tile
    offsets = (0, 1, -2, -1)
    found = []
    for offset in offsets:
        for total in sums:
            a, b, c, d = [total[(g - offset) % 4] for g in range(4)]
            tile = jnp.where(group[0], a, jnp.where(group[1], b, jnp.where(group[2], c, d)))
            found.append(lanes(tile, -4 * offset))
    order = spread_order()
    found = [take(x, order) for x in found]
    return [[found[b * len(stacks) + i] for b in range(4)] for i in range(len(stacks))]


def stack_of(ref, depth, *where):
    return [lambda k=k: ref[(k, *where)] for k in range(depth)]


def pack_kernel(
    depth, t_hbm, e_hbm, n_hbm, d_hbm, w_hbm, atm_hbm, out, west, east, blocks, to_core, to_odd, w, atm,
    t, e, n, d, sems,
):
    copies = [
        pltpu.make_async_copy(d_hbm, d, sems.at[0]),
        pltpu.make_async_copy(t_hbm, t, sems.at[1]),
        pltpu.make_async_copy(e_hbm, e, sems.at[2]),
        pltpu.make_async_copy(n_hbm, n, sems.at[3]),
        pltpu.make_async_copy(atm_hbm, atm, sems.at[4]),
        pltpu.make_async_copy(w_hbm.at[0], w, sems.at[5]),
    ]
    for copy in copies:
        copy.start()
    me = lax.axis_index("lon")
    even = lax.rem(me, 2) == 0
    row = row_index()
    turn = 127 - lane_index()
    count = t.shape[2] // 8
    spans = [slice(8 * j, 8 * j + 8) for j in range(count)]
    fields = (t.at[0], t.at[1], e, n)

    def columns(chosen):
        places = [(f, j) for f in chosen for j in range(count)]
        stacks = [stack_of(fields[f], depth, spans[j]) for f, j in places]
        if 0 in chosen:
            for stack, span in zip(stacks, spans):
                stack.append(lambda span=span: d[span].astype(F32))
        for (f, j), found in zip(places, edge_columns(stacks)):
            for b, tile in enumerate(found):
                blocks[b, f, spans[j]] = tile
            w1, e1 = found[0], found[3]
            to_core[f, spans[j]] = jnp.where(even, e1, w1)
            to_odd[f, spans[j]] = jnp.where(even, w1, e1)
            place = f * count + j
            out[depth + place // 2, 8 * (place % 2) : 8 * (place % 2) + 8] = jnp.where(me == 0, w1, e1)

    copies[0].wait()
    copies[1].wait()
    columns((0, 1))
    copies[2].wait()
    copies[3].wait()
    levels = d[spans[-1]].astype(F32)
    for k in range(depth):
        cells = jnp.where(row < 4, rows(t[0, k, spans[-1]], 4), t[1, k, spans[-1]])
        flows = jnp.where(row < 4, rows(n[k, spans[-1]], 4), e[k, spans[-1]])
        if k < 4:
            flows = jnp.where(row == 4, rows(levels, -k), flows)
        out[k, 0:8] = take(cells, turn)
        out[k, 8:16] = take(flows, turn)
    columns((2, 3))
    halves = [slice(0, 8), slice(8, 16)]
    stacks = [stack_of(out, depth, span) for span in halves]
    stacks[1].append(lambda: take(levels, turn))
    for span, found in zip(halves, edge_columns(stacks)):
        east[span], west[span] = found[0], found[3]
    copies[4].wait()
    copies[5].wait()


def regrid_kernel(size, atm, w, src_hbm, west, east, out, wide, part, src, sems):
    blocks_read = pltpu.make_async_copy(src_hbm, src, sems.at[0])
    blocks_read.start()
    flat = atm[...].reshape(atm.shape[0] * atm.shape[1], atm.shape[2])
    count = flat.shape[0]
    blocks = atm.shape[1]
    columns = jnp.transpose(jnp.concatenate([flat, jnp.zeros((128 - count, 128), F32)], axis=0))
    for c in range(count):
        wide[c] = jnp.broadcast_to(columns[:, c : c + 1], (128, 128))
    row = row_index()
    me = lax.axis_index("lon")
    message = west[...]

    def fill(e, carry):
        out[e] = message
        return carry

    lax.fori_loop(0, size, fill, 0, unroll=8)
    out[lax.rem(2 * size - 2 - me, size)] = east[...]

    def owner(e, carry):
        for s in range(2):
            block = src[s, e]
            sums = [None, None]
            for i in range(16):
                span = slice(8 * i, 8 * i + 8)
                weight = w[e, s, span]
                for f in range(2):
                    term = weight * wide[f * blocks + block, span]
                    sums[f] = term if sums[f] is None else sums[f] + term
            for f in range(2):
                part[e, 2 * f + s] = sums[f]
        return carry

    def letter(e, carry):
        for f in range(2):
            a, b = part[e, 2 * f], part[e, 2 * f + 1]
            tile = jnp.where(row < 4, a, b) + rows(jnp.where(row < 4, b, a), 4)
            tile = tile + rows(tile, -1)
            tile = tile + rows(tile, -2)
            span = slice(8 * f, 8 * f + 8)
            out[e, span] = jnp.where((row & 3) == 0, tile, out[e, span])
        return carry

    blocks_read.wait()
    lax.fori_loop(0, size, owner, 0, unroll=4)
    lax.fori_loop(0, size, letter, 0, unroll=8)


def inner_kernel(
    depth, t_hbm, e_hbm, n_hbm, d_hbm, mix_hbm, out, surface_wet, columns,
    t, e, n, d, mix, weights, sems, flow_sems, cell_sems,
):
    levels = pltpu.make_async_copy(d_hbm, d, sems.at[0])
    mixing = pltpu.make_async_copy(mix_hbm, mix, sems.at[1])
    parts = [pl.ds(k, min(PART, depth - k)) for k in range(0, depth, PART)]
    flows = [
        (
            pltpu.make_async_copy(e_hbm.at[p], e.at[p], flow_sems.at[0, i]),
            pltpu.make_async_copy(n_hbm.at[p], n.at[p], flow_sems.at[1, i]),
        )
        for i, p in enumerate(parts)
    ]
    cells = [pltpu.make_async_copy(t_hbm.at[:, p], t.at[:, p], cell_sems.at[i]) for i, p in enumerate(parts)]
    levels.start()
    for pair in flows:
        for copy in pair:
            copy.start()
    for copy in cells:
        copy.start()
    mixing.start()
    levels.wait()
    row = row_index()
    count = t.shape[2] // 8
    spans = [slice(8 * j, 8 * j + 8) for j in range(count)]
    deep = [d[s].astype(F32) for s in spans]

    def plus(tiles):
        return [lanes(x, 1) for x in tiles]

    def minus(tiles):
        return [lanes(x, -1) for x in tiles]

    east_faces = [jnp.minimum(x, y) for x, y in zip(deep, minus(deep))]
    faces = list(zip(east_faces, plus(east_faces), block_faces(deep, deep[-1])))

    def coefficients(k):
        e_half = [0.5 * e[k, s] for s in spans]
        n_half = [0.5 * n[k, s] for s in spans]
        for s, he, hw, hn, hs, (east, west, (north, south)) in zip(
            spans, e_half, plus(e_half), n_half, south_of(n_half), faces
        ):
            found = stencil(
                face(he, east > float(k)),
                face(hn, north > float(k)),
                face(hw, west > float(k)),
                face(hs, south > float(k)),
            )
            for i, x in enumerate(found):
                weights[i, k, s] = x

    def substep(k, step):
        source = out if step else t
        for f in range(2):
            state = [source[f, k, s] for s in spans]
            up, down = north_of(state, state[-1]), south_of(state)
            for s, c, u, v in zip(spans, state, up, down):
                w = [weights[i, k, s] for i in range(5)]
                out[f, k, s] = advance(w, c, lanes(c, -1), lanes(c, 1), u, v)

    zero = jnp.zeros((8, 128), F32)
    above, ratio = [zero] * count, [zero] * count

    def pivots(k):
        for j, s in enumerate(spans):
            link = jnp.where(deep[j] > float(k + 1), mix[k, s], 0.0) if k < depth - 1 else zero
            inv = 1.0 / (1.0 + above[j] + link + above[j] * ratio[j])
            columns[0, k, s] = inv
            columns[1, k, s] = link
            above[j], ratio[j] = link, -link * inv

    for s, x in zip(spans, deep):
        surface_wet[s] = jnp.where(x > 0.0, 1.0, 0.0)
    for k in range(depth):
        if k % PART == 0:
            for copy in flows[k // PART]:
                copy.wait()
        coefficients(k)
    for k in range(depth):
        if k % PART == 0:
            cells[k // PART].wait()
        substep(k, 0)
    mixing.wait()
    for step in range(1, SUB):
        for k in range(depth):
            substep(k, step)
            if step == 1:
                pivots(k)


def fold_faces(deep, own_deep, toward_east, toward_west):
    easts = [jnp.minimum(x, y) for x, y in zip(deep, toward_east(deep))]
    norths = [jnp.minimum(x, fold_north(x, y, y)) for x, y in zip(deep, own_deep)]
    return list(zip(easts, toward_west(easts), norths, [rows(x, 1) for x in norths]))


def fold_weights(flows, faces, levels, toward_west):
    row = row_index()
    turned = [rows(x, 4) for x in flows]
    e_half = [0.5 * jnp.where(row < 4, y, x) for x, y in zip(flows, turned)]
    n_half = [0.5 * jnp.where(row < 4, x, y) for x, y in zip(flows, turned)]
    w_half = toward_west(e_half)
    s_half = [rows(x, 1) for x in n_half]
    return [
        stencil(face(e, east > k), face(n, north > k), face(w, west > k), face(s, south > k))
        for e, n, w, s, (east, west, north, south), k in zip(e_half, n_half, w_half, s_half, faces, levels)
    ]


def block_faces(deep, beyond):
    norths = [jnp.minimum(x, y) for x, y in zip(deep, north_of(deep, beyond))]
    souths = south_of(norths)
    souths[0] = jnp.where(row_index() == 0, 0.0, souths[0])
    return list(zip(norths, souths))


def fold_north(fold, first, second):
    row = row_index()
    return jnp.where((row & 3) == 3, jnp.where(row < 4, rows(first, 4), second), rows(fold, -1))


def fold_levels(fold):
    row = row_index()
    deep = jnp.zeros((8, 128), F32)
    for r in range(4):
        deep = jnp.where((row & 3) == r, jnp.broadcast_to(fold[r, 12:13], (8, 128)), deep)
    return deep


def strip_kernel(depth, t_hbm, e_hbm, n_hbm, d_hbm, fold, strip, blocks, t, e, n, d, folded, weights, over, sems):
    band = northern_rows(t_hbm, e_hbm, n_hbm, d_hbm, t, e, n, d, sems)
    for copy in band:
        copy.start()
    halves = [slice(0, 8), slice(8, 16)]
    stacks = [stack_of(fold, depth, span) for span in halves]
    stacks[1].append(lambda: fold_levels(fold))
    for span, found in zip(halves, edge_columns(stacks)):
        for b, tile in enumerate(found):
            blocks[b, span] = tile
    for copy in band:
        copy.wait()
    row = row_index()
    deep = d[...].astype(F32)
    fold_deep = fold_levels(fold)

    def plus(tiles):
        return [lanes(x, 1) for x in tiles]

    def minus(tiles):
        return [lanes(x, -1) for x in tiles]

    over_faces = fold_faces([fold_deep], [deep], plus, minus)
    east = jnp.minimum(deep, lanes(deep, -1))
    west = lanes(east, 1)
    north = jnp.minimum(deep, jnp.where(row == 7, fold_deep, rows(deep, -1)))
    south = rows(north, 1)
    for k in range(0, depth, GROUP):
        levels = range(k, min(k + GROUP, depth))
        found = fold_weights(
            [fold[k, 8:16] for k in levels], over_faces * len(levels), [float(k) for k in levels], minus
        )
        for k, tiles in zip(levels, found):
            for i, x in enumerate(tiles):
                over[i, k] = x
    for k in range(depth):
        he, hn = 0.5 * e[k], 0.5 * n[k]
        level = float(k)
        found = stencil(
            face(he, east > level),
            face(hn, north > level),
            face(lanes(he, 1), west > level),
            face(rows(hn, 1), south > level),
        )
        for i, x in enumerate(found):
            weights[i, k] = x
    for step in range(SUB):
        for k in range(depth):
            if step:
                one, two, cells = strip[0, k], strip[1, k], folded[k]
            else:
                one, two, cells = t[0, k], t[1, k], fold[k, 0:8]
            up_one = jnp.where(row == 7, rows(cells, 4), rows(one, -1))
            up_two = jnp.where(row == 7, cells, rows(two, -1))
            if step < SUB - 1:
                up = fold_north(cells, one, two)
                w = [over[i, k] for i in range(5)]
                folded[k] = advance(w, cells, lanes(cells, 1), lanes(cells, -1), up, rows(cells, 1))
            w = [weights[i, k] for i in range(5)]
            strip[0, k] = advance(w, one, lanes(one, -1), lanes(one, 1), up_one, rows(one, 1))
            strip[1, k] = advance(w, two, lanes(two, -1), lanes(two, 1), up_two, rows(two, 1))


def edge_side(depth, rows_count, cells, flows, fold_cells, fold_flows):
    lane, row = lane_index(), row_index()
    level = (lane & 31).astype(F32)
    count = rows_count // 8

    def plus(tiles):
        turned = [lanes(x, 32) for x in tiles]
        return [turned[0]] + [jnp.where(lane < 32, p, x) for p, x in zip(turned, turned[1:])]

    def minus(tiles):
        turned = [lanes(x, -32) for x in tiles]
        return [jnp.where(lane >= 96, q, x) for x, q in zip(turned, turned[1:])] + [turned[2]]

    at_levels = (lane & 96) + depth
    deep = [[take(cells[b][0][j], at_levels) for j in range(count)] for b in range(3)]
    fold_deep = []
    for b in range(3):
        found = take(fold_flows[b], at_levels)
        fold_deep.append(jnp.where(row < 4, rows(found, 4), found))
    over_faces = fold_faces(fold_deep, [deep[b][-1] for b in range(3)], plus, minus)
    over = fold_weights(fold_flows, over_faces, [level] * 3, minus)

    weights = [[None] * count for _ in range(3)]
    meridional = [block_faces(deep[b], fold_deep[b]) for b in range(3)]
    halves = [[0.5 * x for x in flows[b][1]] for b in range(3)]
    southern = [south_of(x) for x in halves]
    for j in range(count):
        yield
        line = [deep[b][j] for b in range(3)]
        easts = [jnp.minimum(x, y) for x, y in zip(line, minus(line))]
        e_half = [0.5 * flows[b][0][j] for b in range(3)]
        for b, (east, west, he, hw) in enumerate(zip(easts, plus(easts), e_half, plus(e_half))):
            north, south = meridional[b][j]
            weights[b][j] = stencil(
                face(he, east > level),
                face(halves[b][j], north > level),
                face(hw, west > level),
                face(southern[b][j], south > level),
            )

    state = [[list(cells[b][f]) for f in range(2)] for b in range(3)]
    folded = list(fold_cells)
    for step in range(SUB):
        yield
        beyond = [(rows(x, 4), x) for x in folded]
        if step < SUB - 1:
            fold_east, fold_west = plus(folded), minus(folded)
            ups = [fold_north(folded[b], state[b][0][-1], state[b][1][-1]) for b in range(3)]
            folded = [
                advance(over[b], folded[b], fold_east[b], fold_west[b], ups[b], rows(folded[b], 1)) for b in range(3)
            ]
        for f in range(2):
            yield
            east, west = [], []
            for j in range(count):
                line = [state[b][f][j] for b in range(3)]
                east.append(minus(line))
                west.append(plus(line))
            yield
            for b in range(3):
                tiles = state[b][f]
                up, down = north_of(tiles, beyond[b][f]), south_of(tiles)
                state[b][f] = [
                    advance(weights[b][j], tiles[j], east[j][b], west[j][b], up[j], down[j]) for j in range(count)
                ]
    return state[1]


def side_by_side(stages):
    results = [None] * len(stages)
    running = list(enumerate(stages))
    while running:
        left = []
        for i, stage in running:
            try:
                next(stage)
                left.append((i, stage))
            except StopIteration as end:
                results[i] = end.value
        running = left
    return results


def last_kernel(
    depth, strip, folds, wet, inner, blocks, core, odd, fold, mail, columns, target_hbm,
    out_hbm, merged, out, target, sems, other,
):
    targets = pltpu.make_async_copy(target_hbm, target, other.at[0])
    targets.start()
    lane, row = lane_index(), row_index()
    size = mail.shape[0]
    rows_count = inner.shape[2]
    count = rows_count // 8
    spans = [slice(8 * j, 8 * j + 8) for j in range(count)]
    me = lax.axis_index("lon")
    even = lax.rem(me, 2) == 0

    west_mail = mail[lax.rem(size - me, size)]
    east_mail = mail[lax.rem(2 * size - 2 - me, size)]
    at_wrap = (me == 0) | (me == size - 1)

    def received(f, j, west):
        place = f * count + j
        wrapped = fold[depth + place // 2, 8 * (place % 2) : 8 * (place % 2) + 8]
        a, b = core[f, spans[j]], jnp.where(at_wrap, wrapped, odd[f, spans[j]])
        return jnp.where(even, b, a) if west else jnp.where(even, a, b)

    def own(b, f, s):
        return blocks[b, f, s]

    sides = []
    for west in (True, False):
        near, far = (0, 1) if west else (3, 2)
        here = [[[own(b, f, s) for s in spans] for f in range(4)] for b in (near, far)]
        there = [[received(f, j, west) for j in range(count)] for f in range(4)]
        letter = west_mail if west else east_mail
        line = [there, here[0], here[1]] if west else [here[1], here[0], there]
        cells_near = [folds[near, 0:8], folds[far, 0:8]]
        flows_near = [folds[near, 8:16], folds[far, 8:16]]
        if west:
            fold_cells = [letter[0:8]] + cells_near
            fold_flows = [letter[8:16]] + flows_near
        else:
            fold_cells = cells_near[::-1] + [letter[0:8]]
            fold_flows = flows_near[::-1] + [letter[8:16]]
        sides.append(
            edge_side(depth, rows_count, [x[0:2] for x in line], [x[2:4] for x in line], fold_cells, fold_flows)
        )

    sides = side_by_side(sides)
    order = gather_order()
    group_even = ((lane >> 2) & 1) == 0
    for f in range(2):
        for j, s in enumerate(spans):
            a = take(sides[0][f][j], order)
            b = lanes(take(sides[1][f][j], order), -4)
            merged[0, f, s] = jnp.where(group_even, a, b)
            merged[1, f, s] = jnp.where(group_even, b, a)

    surface = [[jnp.zeros((8, 128), F32) for _ in spans] for _ in range(2)]
    targets.wait()
    for a in range(size):
        for s in range(2):
            goal = target[s, a]
            hits = [row + 8 * j == goal for j in range(count)]
            for f in range(2):
                piece = jnp.broadcast_to(mail[a, PIECE_ROW[f][s] : PIECE_ROW[f][s] + 1], (8, 128))
                surface[f] = [x + jnp.where(hit, piece, 0.0) for x, hit in zip(surface[f], hits)]

    outer = (lane < 4) | (lane >= 124)
    for k in range(depth):
        for f in range(2):
            for j, s in enumerate(spans):
                cell = inner[f, k, s]
                if j == count - 1:
                    cell = jnp.where(row >= 4, strip[f, k], cell)
                out[f, k, s] = jnp.where(outer, lanes(merged[k % 2, f, s], -4 * k), cell)
    partial_value = [[None] * count for _ in range(2)]
    for k in range(depth):
        for f in range(2):
            for j, s in enumerate(spans):
                cell = out[f, k, s]
                if k == 0:
                    cell = cell + FLUX_GAIN * surface[f][j] * wet[s]
                else:
                    cell = cell + columns[1, k - 1, s] * partial_value[f][j]
                value = cell * columns[0, k, s]
                partial_value[f][j] = value
                out[f, k, s] = value
    copies = []
    for k in range(depth - 1, -1, -1):
        if k < depth - 1:
            for f in range(2):
                for j, s in enumerate(spans):
                    value = out[f, k, s] + columns[1, k, s] * columns[0, k, s] * partial_value[f][j]
                    partial_value[f][j] = value
                    out[f, k, s] = value
        if k % GROUP == 0:
            part = pl.ds(k, min(GROUP, depth - k))
            copy = pltpu.make_async_copy(out.at[:, part], out_hbm.at[:, part], sems.at[k // GROUP])
            copy.start()
            copies.append(copy)
    for copy in copies:
        copy.wait()


def on_device(
    tracers,
    east_flow,
    north_flow,
    mixing,
    depth_levels,
    atm_flux,
    source_blocks,
    target_rows,
    regrid_weights,
):
    size = lax.axis_size("lon")
    depth, lat = tracers.shape[1], tracers.shape[2]
    dma = pltpu.SemaphoreType.DMA
    near = [(i, i + (1 if i % 2 else -1)) for i in range(1, size - 1)]
    band = [
        shape(2, depth, 8, 128),
        shape(depth, 8, 128),
        shape(depth, 8, 128),
        pltpu.VMEM((8, 128), jnp.int32),
    ]
    plane = shape(depth, lat, 128)
    block = [shape(2, depth, lat, 128), plane, plane, pltpu.VMEM((lat, 128), jnp.int32)]
    strips = shape(4, lat, 128)
    fields = in_hbm(tracers, east_flow, north_flow, depth_levels)

    message, west_corner, east_corner, blocks, to_core, to_odd, weights, flux = call(
        functools.partial(pack_kernel, depth),
        (
            shape(depth + lat // 4, 16, 128), shape(16, 128), shape(16, 128), shape(4, 4, lat, 128), strips, strips,
            shape(*regrid_weights.shape[1:]), shape(*atm_flux.shape),
        ),
        [HBM] * 6,
        [*block, dma((6,))],
        cost=cost(0.1),
        name="fold_rows_and_columns",
    )(*fields, *in_hbm(regrid_weights, atm_flux))
    fold = lax.ppermute(message, "lon", [(i, size - 1 - i) for i in range(size)])
    core = lax.ppermute(to_core, "lon", [(i, i ^ 1) for i in range(size)])
    odd = lax.ppermute(to_odd, "lon", [(0, 0), *near, (size - 1, size - 1)])

    (letters,) = call(
        functools.partial(regrid_kernel, size),
        (shape(size, 16, 128),),
        [VMEM, VMEM, HBM, VMEM, VMEM],
        [
            pltpu.VMEM((2 * atm_flux.shape[1], 128, 128), F32),
            pltpu.VMEM((size, 4, 8, 128), F32),
            pltpu.SMEM((2, size), jnp.int32),
            dma((1,)),
        ],
        cost=cost(0.1),
        name="regrid",
    )(
        *in_vmem(flux, weights),
        *in_hbm(jnp.transpose(source_blocks[0])),
        *in_vmem(west_corner, east_corner),
    )
    mail = lax.all_to_all(letters, "lon", split_axis=0, concat_axis=0, tiled=True)

    inner, wet, columns = call(
        functools.partial(inner_kernel, depth),
        (shape(2, depth, lat, 128), shape(lat, 128), shape(2, depth, lat, 128)),
        [HBM] * 5,
        [
            *block,
            shape(depth - 1, lat, 128),
            shape(5, depth, lat, 128),
            dma((2,)),
            dma((2, -(-depth // PART))),
            dma((-(-depth // PART),)),
        ],
        cost=cost(0.1),
        name="inner_cells",
    )(*fields, *in_hbm(mixing))

    strip, folds = call(
        functools.partial(strip_kernel, depth),
        (shape(2, depth, 8, 128), shape(4, 16, 128)),
        [HBM] * 4 + [VMEM],
        [*band, shape(depth, 8, 128), shape(5, depth, 8, 128), shape(5, depth, 8, 128), dma((4,))],
        cost=cost(0.1),
        name="top_strip",
    )(*fields, *in_vmem(fold))

    (result,) = call(
        functools.partial(last_kernel, depth),
        (jax.ShapeDtypeStruct((2, depth, lat, 128), F32),),
        [VMEM] * 10 + [HBM],
        [
            pltpu.VMEM((2, 2, lat, 128), F32),
            pltpu.VMEM((2, depth, lat, 128), F32),
            pltpu.SMEM((2, size), jnp.int32),
            dma((-(-depth // GROUP),)),
            dma((1,)),
        ],
        out_specs=[HBM],
        cost=cost(0.1),
        name="edges_and_columns",
    )(
        *in_vmem(strip, folds, wet, inner, blocks, core, odd, fold, mail, columns),
        *in_hbm(jnp.transpose(target_rows[:, 0, :])),
    )
    return result


def solution(mesh):
    return jax.shard_map(
        on_device,
        mesh=mesh,
        in_specs=(
            P(None, "ens", None, "lon"),
            P("ens", None, "lon"),
            P("ens", None, "lon"),
            P("ens", None, "lon"),
            P(None, "lon"),
            P("ens", "lon", None),
            P("lon", None, None),
            P(None, "lon", None),
            P("lon", None, None, None, None),
        ),
        out_specs=P(None, "ens", None, "lon"),
        check_vma=False,
    )
```

```python
import functools

import jax
import jax.numpy as jnp
from jax import lax
from jax.experimental import pallas as pl
from jax.experimental.pallas import tpu as pltpu
from jax.sharding import PartitionSpec as P

SUB = 4
DIFFUSION = 0.12
FLUX_GAIN = 0.5
GROUP = 5
PART = 13
F32 = jnp.float32
VMEM = pl.BlockSpec(memory_space=pltpu.VMEM)
SMEM = pl.BlockSpec(memory_space=pltpu.SMEM)
HBM = pl.BlockSpec(memory_space=pltpu.HBM)
VMEM_LIMIT = 16 * 1024 * 1024


def lane_index():
    return lax.broadcasted_iota(jnp.int32, (8, 128), 1)


def row_index():
    return lax.broadcasted_iota(jnp.int32, (8, 128), 0)


def lanes(tile, shift):
    shift = shift % 128
    return pltpu.roll(tile, shift, 1) if shift else tile


def rows(tile, shift):
    shift = shift % 8
    return pltpu.roll(tile, shift, 0) if shift else tile


def take(tile, index):
    return jnp.take_along_axis(tile, index, axis=1)


def spread_order():
    lane = lane_index()
    return 4 * (lane & 31) + (lane >> 5)


def gather_order():
    lane = lane_index()
    return 32 * (lane & 3) + (lane >> 2)


def call(body, out, in_specs, scratch=(), out_specs=None, cost=None, name=None):
    return pl.pallas_call(
        body,
        out_shape=out,
        in_specs=in_specs,
        out_specs=out_specs if out_specs is not None else [VMEM] * len(out),
        scratch_shapes=list(scratch),
        compiler_params=pltpu.CompilerParams(vmem_limit_bytes=VMEM_LIMIT),
        cost_estimate=cost,
        name=name,
    )


def cost(micros):
    return pl.CostEstimate(flops=0, bytes_accessed=int(micros * 3.0e6), transcendentals=0)


def shape(*dims):
    return pltpu.VMEM(dims, F32)


def in_hbm(*arrays):
    return [pltpu.with_memory_space_constraint(x, pltpu.HBM) for x in arrays]


def in_vmem(*arrays):
    return [pltpu.with_memory_space_constraint(x, pltpu.VMEM) for x in arrays]


def face(half, open_face):
    return jnp.where(open_face, half + DIFFUSION, 0.0), jnp.where(open_face, half - DIFFUSION, 0.0)


def stencil(east, north, west, south):
    a_e, b_e = east
    a_n, b_n = north
    a_w, b_w = west
    a_s, b_s = south
    return (((1.0 - a_e) + b_w) - a_n) + b_s, b_e, a_w, b_n, a_s


def advance(weights, cell, east, west, north, south):
    own, b_e, a_w, b_n, a_s = weights
    return (own * cell + (a_w * west - b_e * east)) + (a_s * south - b_n * north)


def north_of(tiles, beyond):
    row = row_index()
    turned = [rows(t, -1) for t in tiles]
    return [jnp.where(row == 7, n, t) for t, n in zip(turned, turned[1:] + [beyond])]


def south_of(tiles):
    row = row_index()
    turned = [rows(t, 1) for t in tiles]
    return [turned[0]] + [jnp.where(row == 0, p, t) for p, t in zip(turned, turned[1:])]


def shut_corner(cells, flows, west):
    lane, row = lane_index(), row_index()
    turn, far = (32, lane < 32) if west else (96, lane >= 96)
    first = (row & 3) == 3
    both = [jnp.where(first & far, rows(lanes(x, turn), 2), x) for x in (cells, flows)]
    return jnp.where((row & 2) != 0, both[0], rows(both[1], -2))


def open_corner(tile, west):
    third = (row_index() & 3) == 1
    turn = 96 if west else 32
    return [jnp.where(third, rows(lanes(x, turn), -2), x) for x in (tile, rows(tile, 2))]


def edge_columns(stacks):
    lane = lane_index()
    outer = (lane < 8) | (lane >= 120)
    group = [((lane >> 2) & 3) == c for c in range(3)]
    sums = [[None] * 4 for _ in stacks]
    for k in range(max(len(x) for x in stacks)):
        for total, stack in zip(sums, stacks):
            if k < len(stack):
                tile = lanes(jnp.where(outer, stack[k](), 0.0), 4 * k)
                total[k % 4] = tile if total[k % 4] is None else total[k % 4] + tile
    offsets = (0, 1, -2, -1)
    found = []
    for offset in offsets:
        for total in sums:
            a, b, c, d = [total[(g - offset) % 4] for g in range(4)]
            tile = jnp.where(group[0], a, jnp.where(group[1], b, jnp.where(group[2], c, d)))
            found.append(lanes(tile, -4 * offset))
    order = spread_order()
    found = [take(x, order) for x in found]
    return [[found[b * len(stacks) + i] for b in range(4)] for i in range(len(stacks))]


def stack_of(ref, depth, *where):
    return [lambda k=k: ref[(k, *where)] for k in range(depth)]


def pack_kernel(
    depth, t_hbm, e_hbm, n_hbm, d_hbm, w_hbm, atm_hbm, out, west, east, blocks, to_core, to_odd, w, atm,
    t, e, n, d, sems,
):
    copies = [
        pltpu.make_async_copy(d_hbm, d, sems.at[0]),
        pltpu.make_async_copy(t_hbm, t, sems.at[1]),
        pltpu.make_async_copy(e_hbm, e, sems.at[2]),
        pltpu.make_async_copy(n_hbm, n, sems.at[3]),
        pltpu.make_async_copy(atm_hbm, atm, sems.at[4]),
        pltpu.make_async_copy(w_hbm.at[0], w, sems.at[5]),
    ]
    for copy in copies:
        copy.start()
    me = lax.axis_index("lon")
    even = lax.rem(me, 2) == 0
    row = row_index()
    turn = 127 - lane_index()
    count = t.shape[2] // 8
    spans = [slice(8 * j, 8 * j + 8) for j in range(count)]
    fields = (t.at[0], t.at[1], e, n)

    def columns(chosen):
        places = [(f, j) for f in chosen for j in range(count)]
        stacks = [stack_of(fields[f], depth, spans[j]) for f, j in places]
        if 0 in chosen:
            for stack, span in zip(stacks, spans):
                stack.append(lambda span=span: d[span].astype(F32))
        for (f, j), found in zip(places, edge_columns(stacks)):
            for b, tile in enumerate(found):
                blocks[b, f, spans[j]] = tile
            w1, e1 = found[0], found[3]
            to_core[f, spans[j]] = jnp.where(even, e1, w1)
            to_odd[f, spans[j]] = jnp.where(even, w1, e1)
            place = f * count + j
            out[depth + place // 2, 8 * (place % 2) : 8 * (place % 2) + 8] = jnp.where(me == 0, w1, e1)

    copies[0].wait()
    copies[1].wait()
    columns((0, 1))
    copies[2].wait()
    copies[3].wait()
    levels = d[spans[-1]].astype(F32)
    for k in range(depth):
        cells = jnp.where(row < 4, rows(t[0, k, spans[-1]], 4), t[1, k, spans[-1]])
        flows = jnp.where(row < 4, rows(n[k, spans[-1]], 4), e[k, spans[-1]])
        if k < 4:
            flows = jnp.where(row == 4, rows(levels, -k), flows)
        out[k, 0:8] = take(cells, turn)
        out[k, 8:16] = take(flows, turn)
    columns((2, 3))
    halves = [slice(0, 8), slice(8, 16)]
    stacks = [stack_of(out, depth, span) for span in halves]
    stacks[1].append(lambda: take(levels, turn))
    cells, flows = edge_columns(stacks)
    east[...] = shut_corner(cells[0], flows[0], False)
    west[...] = shut_corner(cells[3], flows[3], True)
    copies[4].wait()
    copies[5].wait()


def regrid_kernel(size, atm, w, src_hbm, west, east, out, wide, part, src, sems):
    blocks_read = pltpu.make_async_copy(src_hbm, src, sems.at[0])
    blocks_read.start()
    flat = atm[...].reshape(atm.shape[0] * atm.shape[1], atm.shape[2])
    count = flat.shape[0]
    blocks = atm.shape[1]
    columns = jnp.transpose(jnp.concatenate([flat, jnp.zeros((128 - count, 128), F32)], axis=0))
    for c in range(count):
        wide[c] = jnp.broadcast_to(columns[:, c : c + 1], (128, 128))
    me = lax.axis_index("lon")

    def send(e, tile):
        out[3 * e + 1] = tile[0:4]
        out[3 * e + 2] = tile[4:8]

    def fill(e, carry):
        send(e, west[...])
        return carry

    lax.fori_loop(0, size, fill, 0, unroll=8)
    send(lax.rem(2 * size - 2 - me, size), east[...])

    def owner(e, carry):
        for s in range(2):
            block = src[s, e]
            sums = [None, None]
            for i in range(16):
                span = slice(8 * i, 8 * i + 8)
                weight = w[e, s, span]
                for f in range(2):
                    term = weight * wide[f * blocks + block, span]
                    sums[f] = term if sums[f] is None else sums[f] + term
            for f in range(2):
                part[e, 2 * f + s] = sums[f]
        return carry

    def pair(e, carry):
        tile = totals([part[2 * e + i // 4, i % 4] for i in range(8)])
        out[6 * e] = tile[0:4]
        out[6 * e + 3] = tile[4:8]
        return carry

    blocks_read.wait()
    lax.fori_loop(0, size, owner, 0, unroll=4)
    lax.fori_loop(0, size // 2, pair, 0, unroll=8)


def totals(tiles):
    row = row_index()
    for step in (4, 2, 1):
        low = (row & step) == 0
        half = len(tiles) // 2
        merged = []
        for a, b in zip(tiles[:half], tiles[half:]):
            kept, moved = jnp.where(low, a, b), jnp.where(low, b, a)
            if step == 4:
                turned = rows(moved, 4)
            else:
                turned = jnp.where(low, rows(moved, -step), rows(moved, step))
            merged.append(kept + turned)
        tiles = merged
    return tiles[0]


def inner_kernel(
    depth, t_hbm, e_hbm, n_hbm, d_hbm, mix_hbm, out, surface_wet, columns, top_t, top_e, top_n, top_d,
    t, e, n, d, mix, weights, sems, flow_sems, cell_sems,
):
    levels = pltpu.make_async_copy(d_hbm, d, sems.at[0])
    mixing = pltpu.make_async_copy(mix_hbm, mix, sems.at[1])
    parts = [pl.ds(k, min(PART, depth - k)) for k in range(0, depth, PART)]
    flows = [
        (
            pltpu.make_async_copy(e_hbm.at[p], e.at[p], flow_sems.at[0, i]),
            pltpu.make_async_copy(n_hbm.at[p], n.at[p], flow_sems.at[1, i]),
        )
        for i, p in enumerate(parts)
    ]
    cells = [pltpu.make_async_copy(t_hbm.at[:, p], t.at[:, p], cell_sems.at[i]) for i, p in enumerate(parts)]
    levels.start()
    for pair in flows:
        for copy in pair:
            copy.start()
    for copy in cells:
        copy.start()
    mixing.start()
    levels.wait()
    row = row_index()
    count = t.shape[2] // 8
    spans = [slice(8 * j, 8 * j + 8) for j in range(count)]
    deep = [d[s].astype(F32) for s in spans]

    def plus(tiles):
        return [lanes(x, 1) for x in tiles]

    def minus(tiles):
        return [lanes(x, -1) for x in tiles]

    east_faces = [jnp.minimum(x, y) for x, y in zip(deep, minus(deep))]
    faces = list(zip(east_faces, plus(east_faces), block_faces(deep, deep[-1])))

    def coefficients(k):
        e_half = [0.5 * e[k, s] for s in spans]
        n_half = [0.5 * n[k, s] for s in spans]
        for s, he, hw, hn, hs, (east, west, (north, south)) in zip(
            spans, e_half, plus(e_half), n_half, south_of(n_half), faces
        ):
            found = stencil(
                face(he, east > float(k)),
                face(hn, north > float(k)),
                face(hw, west > float(k)),
                face(hs, south > float(k)),
            )
            for i, x in enumerate(found):
                weights[i, k, s] = x

    def substep(k, step):
        source = out if step else t
        for f in range(2):
            state = [source[f, k, s] for s in spans]
            up, down = north_of(state, state[-1]), south_of(state)
            for s, c, u, v in zip(spans, state, up, down):
                w = [weights[i, k, s] for i in range(5)]
                out[f, k, s] = advance(w, c, lanes(c, -1), lanes(c, 1), u, v)

    zero = jnp.zeros((8, 128), F32)
    above, ratio = [zero] * count, [zero] * count

    def pivots(k):
        for j, s in enumerate(spans):
            link = jnp.where(deep[j] > float(k + 1), mix[k, s], 0.0) if k < depth - 1 else zero
            inv = 1.0 / (1.0 + above[j] + link + above[j] * ratio[j])
            columns[0, k, s] = inv
            columns[1, k, s] = link
            above[j], ratio[j] = link, -link * inv

    top_d[...] = deep[-1]
    for s, x in zip(spans, deep):
        surface_wet[s] = jnp.where(x > 0.0, 1.0, 0.0)
    for k in range(depth):
        if k % PART == 0:
            for copy in flows[k // PART]:
                copy.wait()
        coefficients(k)
        top_e[k] = e[k, spans[-1]]
        top_n[k] = n[k, spans[-1]]
    for k in range(depth):
        if k % PART == 0:
            cells[k // PART].wait()
        substep(k, 0)
        for f in range(2):
            top_t[f, k] = t[f, k, spans[-1]]
    mixing.wait()
    for step in range(1, SUB):
        for k in range(depth):
            substep(k, step)
            if step == 1:
                pivots(k)


def fold_faces(deep, own_deep, toward_east, toward_west):
    easts = [jnp.minimum(x, y) for x, y in zip(deep, toward_east(deep))]
    norths = [jnp.minimum(x, fold_north(x, y, y)) for x, y in zip(deep, own_deep)]
    return list(zip(easts, toward_west(easts), norths, [rows(x, 1) for x in norths]))


def fold_weights(flows, faces, levels, toward_west):
    row = row_index()
    turned = [rows(x, 4) for x in flows]
    e_half = [0.5 * jnp.where(row < 4, y, x) for x, y in zip(flows, turned)]
    n_half = [0.5 * jnp.where(row < 4, x, y) for x, y in zip(flows, turned)]
    w_half = toward_west(e_half)
    s_half = [rows(x, 1) for x in n_half]
    return [
        stencil(face(e, east > k), face(n, north > k), face(w, west > k), face(s, south > k))
        for e, n, w, s, (east, west, north, south), k in zip(e_half, n_half, w_half, s_half, faces, levels)
    ]


def block_faces(deep, beyond):
    norths = [jnp.minimum(x, y) for x, y in zip(deep, north_of(deep, beyond))]
    souths = south_of(norths)
    souths[0] = jnp.where(row_index() == 0, 0.0, souths[0])
    return list(zip(norths, souths))


def fold_north(fold, first, second):
    row = row_index()
    return jnp.where((row & 3) == 3, jnp.where(row < 4, rows(first, 4), second), rows(fold, -1))


def fold_levels(fold):
    row = row_index()
    deep = jnp.zeros((8, 128), F32)
    for r in range(4):
        deep = jnp.where((row & 3) == r, jnp.broadcast_to(fold[r, 12:13], (8, 128)), deep)
    return deep


def strip_kernel(depth, t, e, n, d, fold, strip, blocks, folded, weights, over):
    halves = [slice(0, 8), slice(8, 16)]
    stacks = [stack_of(fold, depth, span) for span in halves]
    stacks[1].append(lambda: fold_levels(fold))
    for span, found in zip(halves, edge_columns(stacks)):
        for b, tile in enumerate(found):
            blocks[b, span] = tile
    row = row_index()
    deep = d[...]
    fold_deep = fold_levels(fold)

    def plus(tiles):
        return [lanes(x, 1) for x in tiles]

    def minus(tiles):
        return [lanes(x, -1) for x in tiles]

    over_faces = fold_faces([fold_deep], [deep], plus, minus)
    east = jnp.minimum(deep, lanes(deep, -1))
    west = lanes(east, 1)
    north = jnp.minimum(deep, jnp.where(row == 7, fold_deep, rows(deep, -1)))
    south = rows(north, 1)
    for k in range(0, depth, GROUP):
        levels = range(k, min(k + GROUP, depth))
        found = fold_weights(
            [fold[k, 8:16] for k in levels], over_faces * len(levels), [float(k) for k in levels], minus
        )
        for k, tiles in zip(levels, found):
            for i, x in enumerate(tiles):
                over[i, k] = x
    for k in range(depth):
        he, hn = 0.5 * e[k], 0.5 * n[k]
        level = float(k)
        found = stencil(
            face(he, east > level),
            face(hn, north > level),
            face(lanes(he, 1), west > level),
            face(rows(hn, 1), south > level),
        )
        for i, x in enumerate(found):
            weights[i, k] = x
    for step in range(SUB):
        for k in range(depth):
            if step:
                one, two, cells = strip[0, k], strip[1, k], folded[k]
            else:
                one, two, cells = t[0, k], t[1, k], fold[k, 0:8]
            up_one = jnp.where(row == 7, rows(cells, 4), rows(one, -1))
            up_two = jnp.where(row == 7, cells, rows(two, -1))
            if step < SUB - 1:
                up = fold_north(cells, one, two)
                w = [over[i, k] for i in range(5)]
                folded[k] = advance(w, cells, lanes(cells, 1), lanes(cells, -1), up, rows(cells, 1))
            w = [weights[i, k] for i in range(5)]
            strip[0, k] = advance(w, one, lanes(one, -1), lanes(one, 1), up_one, rows(one, 1))
            strip[1, k] = advance(w, two, lanes(two, -1), lanes(two, 1), up_two, rows(two, 1))


def edge_side(depth, rows_count, cells, flows, fold_cells, fold_flows):
    lane, row = lane_index(), row_index()
    level = (lane & 31).astype(F32)
    count = rows_count // 8

    def plus(tiles):
        turned = [lanes(x, 32) for x in tiles]
        return [turned[0]] + [jnp.where(lane < 32, p, x) for p, x in zip(turned, turned[1:])]

    def minus(tiles):
        turned = [lanes(x, -32) for x in tiles]
        return [jnp.where(lane >= 96, q, x) for x, q in zip(turned, turned[1:])] + [turned[2]]

    at_levels = (lane & 96) + depth
    deep = [[take(cells[b][0][j], at_levels) for j in range(count)] for b in range(3)]
    fold_deep = []
    for b in range(3):
        found = take(fold_flows[b], at_levels)
        fold_deep.append(jnp.where(row < 4, rows(found, 4), found))
    over_faces = fold_faces(fold_deep, [deep[b][-1] for b in range(3)], plus, minus)
    over = fold_weights(fold_flows, over_faces, [level] * 3, minus)

    weights = [[None] * count for _ in range(3)]
    meridional = [block_faces(deep[b], fold_deep[b]) for b in range(3)]
    halves = [[0.5 * x for x in flows[b][1]] for b in range(3)]
    southern = [south_of(x) for x in halves]
    for j in range(count):
        yield
        line = [deep[b][j] for b in range(3)]
        easts = [jnp.minimum(x, y) for x, y in zip(line, minus(line))]
        e_half = [0.5 * flows[b][0][j] for b in range(3)]
        for b, (east, west, he, hw) in enumerate(zip(easts, plus(easts), e_half, plus(e_half))):
            north, south = meridional[b][j]
            weights[b][j] = stencil(
                face(he, east > level),
                face(halves[b][j], north > level),
                face(hw, west > level),
                face(southern[b][j], south > level),
            )

    state = [[list(cells[b][f]) for f in range(2)] for b in range(3)]
    folded = list(fold_cells)
    for step in range(SUB):
        yield
        beyond = [(rows(x, 4), x) for x in folded]
        if step < SUB - 1:
            fold_east, fold_west = plus(folded), minus(folded)
            ups = [fold_north(folded[b], state[b][0][-1], state[b][1][-1]) for b in range(3)]
            folded = [
                advance(over[b], folded[b], fold_east[b], fold_west[b], ups[b], rows(folded[b], 1)) for b in range(3)
            ]
        for f in range(2):
            yield
            east, west = [], []
            for j in range(count):
                line = [state[b][f][j] for b in range(3)]
                east.append(minus(line))
                west.append(plus(line))
            yield
            for b in range(3):
                tiles = state[b][f]
                up, down = north_of(tiles, beyond[b][f]), south_of(tiles)
                state[b][f] = [
                    advance(weights[b][j], tiles[j], east[j][b], west[j][b], up[j], down[j]) for j in range(count)
                ]
    return state[1]


def side_by_side(stages):
    results = [None] * len(stages)
    running = list(enumerate(stages))
    while running:
        left = []
        for i, stage in running:
            try:
                next(stage)
                left.append((i, stage))
            except StopIteration as end:
                results[i] = end.value
        running = left
    return results


def last_kernel(
    depth, strip, folds, wet, inner, blocks, core, odd, fold, mail, columns, target_hbm,
    out_hbm, merged, out, target, sems, other,
):
    targets = pltpu.make_async_copy(target_hbm, target, other.at[0])
    targets.start()
    lane, row = lane_index(), row_index()
    size = mail.shape[0] // 3
    rows_count = inner.shape[2]
    count = rows_count // 8
    spans = [slice(8 * j, 8 * j + 8) for j in range(count)]
    me = lax.axis_index("lon")
    even = lax.rem(me, 2) == 0

    def corner(sender, west):
        place = 3 * lax.rem(sender, size)
        return open_corner(jnp.concatenate([mail[place + 1], mail[place + 2]], axis=0), west)

    west_mail, east_mail = corner(size - me, True), corner(2 * size - 2 - me, False)
    at_wrap = (me == 0) | (me == size - 1)

    def received(f, j, west):
        place = f * count + j
        wrapped = fold[depth + place // 2, 8 * (place % 2) : 8 * (place % 2) + 8]
        a, b = core[f, spans[j]], jnp.where(at_wrap, wrapped, odd[f, spans[j]])
        return jnp.where(even, b, a) if west else jnp.where(even, a, b)

    def own(b, f, s):
        return blocks[b, f, s]

    sides = []
    for west in (True, False):
        near, far = (0, 1) if west else (3, 2)
        here = [[[own(b, f, s) for s in spans] for f in range(4)] for b in (near, far)]
        there = [[received(f, j, west) for j in range(count)] for f in range(4)]
        letter = west_mail if west else east_mail
        line = [there, here[0], here[1]] if west else [here[1], here[0], there]
        cells_near = [folds[near, 0:8], folds[far, 0:8]]
        flows_near = [folds[near, 8:16], folds[far, 8:16]]
        if west:
            fold_cells = [letter[0]] + cells_near
            fold_flows = [letter[1]] + flows_near
        else:
            fold_cells = cells_near[::-1] + [letter[0]]
            fold_flows = flows_near[::-1] + [letter[1]]
        sides.append(
            edge_side(depth, rows_count, [x[0:2] for x in line], [x[2:4] for x in line], fold_cells, fold_flows)
        )

    sides = side_by_side(sides)
    order = gather_order()
    group_even = ((lane >> 2) & 1) == 0
    for f in range(2):
        for j, s in enumerate(spans):
            a = take(sides[0][f][j], order)
            b = lanes(take(sides[1][f][j], order), -4)
            merged[0, f, s] = jnp.where(group_even, a, b)
            merged[1, f, s] = jnp.where(group_even, b, a)

    surface = [[jnp.zeros((8, 128), F32) for _ in spans] for _ in range(2)]
    targets.wait()
    for a in range(size):
        for s in range(2):
            goal = target[s, a]
            hits = [row + 8 * j == goal for j in range(count)]
            for f in range(2):
                piece = jnp.broadcast_to(mail[3 * a, 2 * f + s : 2 * f + s + 1], (8, 128))
                surface[f] = [x + jnp.where(hit, piece, 0.0) for x, hit in zip(surface[f], hits)]

    outer = (lane < 4) | (lane >= 124)
    for k in range(depth):
        for f in range(2):
            for j, s in enumerate(spans):
                cell = inner[f, k, s]
                if j == count - 1:
                    cell = jnp.where(row >= 4, strip[f, k], cell)
                out[f, k, s] = jnp.where(outer, lanes(merged[k % 2, f, s], -4 * k), cell)
    partial_value = [[None] * count for _ in range(2)]
    for k in range(depth):
        for f in range(2):
            for j, s in enumerate(spans):
                cell = out[f, k, s]
                if k == 0:
                    cell = cell + FLUX_GAIN * surface[f][j] * wet[s]
                else:
                    cell = cell + columns[1, k - 1, s] * partial_value[f][j]
                value = cell * columns[0, k, s]
                partial_value[f][j] = value
                out[f, k, s] = value
    copies = []
    for k in range(depth - 1, -1, -1):
        if k < depth - 1:
            for f in range(2):
                for j, s in enumerate(spans):
                    value = out[f, k, s] + columns[1, k, s] * columns[0, k, s] * partial_value[f][j]
                    partial_value[f][j] = value
                    out[f, k, s] = value
        if k % GROUP == 0:
            part = pl.ds(k, min(GROUP, depth - k))
            copy = pltpu.make_async_copy(out.at[:, part], out_hbm.at[:, part], sems.at[k // GROUP])
            copy.start()
            copies.append(copy)
    for copy in copies:
        copy.wait()


def on_device(
    tracers,
    east_flow,
    north_flow,
    mixing,
    depth_levels,
    atm_flux,
    source_blocks,
    target_rows,
    regrid_weights,
):
    size = lax.axis_size("lon")
    depth, lat = tracers.shape[1], tracers.shape[2]
    dma = pltpu.SemaphoreType.DMA
    near = [(i, i + (1 if i % 2 else -1)) for i in range(1, size - 1)]
    plane = shape(depth, lat, 128)
    block = [shape(2, depth, lat, 128), plane, plane, pltpu.VMEM((lat, 128), jnp.int32)]
    strips = shape(4, lat, 128)
    fields = in_hbm(tracers, east_flow, north_flow, depth_levels)

    message, west_corner, east_corner, blocks, to_core, to_odd, weights, flux = call(
        functools.partial(pack_kernel, depth),
        (
            shape(depth + lat // 4, 16, 128), shape(8, 128), shape(8, 128), shape(4, 4, lat, 128), strips, strips,
            shape(*regrid_weights.shape[1:]), shape(*atm_flux.shape),
        ),
        [HBM] * 6,
        [*block, dma((6,))],
        cost=cost(0.1),
        name="fold_rows_and_columns",
    )(*fields, *in_hbm(regrid_weights, atm_flux))
    fold = lax.ppermute(message, "lon", [(i, size - 1 - i) for i in range(size)])
    core = lax.ppermute(to_core, "lon", [(i, i ^ 1) for i in range(size)])
    odd = lax.ppermute(to_odd, "lon", [(0, 0), *near, (size - 1, size - 1)])

    (letters,) = call(
        functools.partial(regrid_kernel, size),
        (shape(3 * size, 4, 128),),
        [VMEM, VMEM, HBM, VMEM, VMEM],
        [
            pltpu.VMEM((2 * atm_flux.shape[1], 128, 128), F32),
            pltpu.VMEM((size, 4, 8, 128), F32),
            pltpu.SMEM((2, size), jnp.int32),
            dma((1,)),
        ],
        cost=cost(0.1),
        name="regrid",
    )(
        *in_vmem(flux, weights),
        *in_hbm(jnp.transpose(source_blocks[0])),
        *in_vmem(west_corner, east_corner),
    )
    mail = lax.all_to_all(letters, "lon", split_axis=0, concat_axis=0, tiled=True)

    inner, wet, columns, *band = call(
        functools.partial(inner_kernel, depth),
        (
            shape(2, depth, lat, 128), shape(lat, 128), shape(2, depth, lat, 128),
            shape(2, depth, 8, 128), shape(depth, 8, 128), shape(depth, 8, 128), shape(8, 128),
        ),
        [HBM] * 5,
        [
            *block,
            shape(depth - 1, lat, 128),
            shape(5, depth, lat, 128),
            dma((2,)),
            dma((2, -(-depth // PART))),
            dma((-(-depth // PART),)),
        ],
        cost=cost(0.1),
        name="inner_cells",
    )(*fields, *in_hbm(mixing))

    strip, folds = call(
        functools.partial(strip_kernel, depth),
        (shape(2, depth, 8, 128), shape(4, 16, 128)),
        [VMEM] * 5,
        [shape(depth, 8, 128), shape(5, depth, 8, 128), shape(5, depth, 8, 128)],
        cost=cost(0.1),
        name="top_strip",
    )(*in_vmem(*band, fold))

    (result,) = call(
        functools.partial(last_kernel, depth),
        (jax.ShapeDtypeStruct((2, depth, lat, 128), F32),),
        [VMEM] * 10 + [HBM],
        [
            pltpu.VMEM((2, 2, lat, 128), F32),
            pltpu.VMEM((2, depth, lat, 128), F32),
            pltpu.SMEM((2, size), jnp.int32),
            dma((-(-depth // GROUP),)),
            dma((1,)),
        ],
        out_specs=[HBM],
        cost=cost(0.1),
        name="edges_and_columns",
    )(
        *in_vmem(strip, folds, wet, inner, blocks, core, odd, fold, mail, columns),
        *in_hbm(jnp.transpose(target_rows[:, 0, :])),
    )
    return result


def solution(mesh):
    return jax.shard_map(
        on_device,
        mesh=mesh,
        in_specs=(
            P(None, "ens", None, "lon"),
            P("ens", None, "lon"),
            P("ens", None, "lon"),
            P("ens", None, "lon"),
            P(None, "lon"),
            P("ens", "lon", None),
            P("lon", None, None),
            P(None, "lon", None),
            P("lon", None, None, None, None),
        ),
        out_specs=P(None, "ens", None, "lon"),
        check_vma=False,
    )
```

```python
import functools

import jax
import jax.numpy as jnp
from jax import lax
from jax.experimental import pallas as pl
from jax.experimental.pallas import tpu as pltpu
from jax.sharding import PartitionSpec as P

SUB = 4
DIFFUSION = 0.12
FLUX_GAIN = 0.5
GROUP = 5
PART = 25
F32 = jnp.float32
VMEM = pl.BlockSpec(memory_space=pltpu.VMEM)
SMEM = pl.BlockSpec(memory_space=pltpu.SMEM)
HBM = pl.BlockSpec(memory_space=pltpu.HBM)
VMEM_LIMIT = 16 * 1024 * 1024


def lane_index():
    return lax.broadcasted_iota(jnp.int32, (8, 128), 1)


def row_index():
    return lax.broadcasted_iota(jnp.int32, (8, 128), 0)


def lanes(tile, shift):
    shift = shift % 128
    return pltpu.roll(tile, shift, 1) if shift else tile


def rows(tile, shift):
    shift = shift % 8
    return pltpu.roll(tile, shift, 0) if shift else tile


def take(tile, index):
    return jnp.take_along_axis(tile, index, axis=1)


def spread_order():
    lane = lane_index()
    return 4 * (lane & 31) + (lane >> 5)


def gather_order():
    lane = lane_index()
    return 32 * (lane & 3) + (lane >> 2)


def call(body, out, in_specs, scratch=(), out_specs=None, cost=None, name=None):
    return pl.pallas_call(
        body,
        out_shape=out,
        in_specs=in_specs,
        out_specs=out_specs if out_specs is not None else [VMEM] * len(out),
        scratch_shapes=list(scratch),
        compiler_params=pltpu.CompilerParams(vmem_limit_bytes=VMEM_LIMIT),
        cost_estimate=cost,
        name=name,
    )


def cost(micros):
    return pl.CostEstimate(flops=0, bytes_accessed=int(micros * 3.0e6), transcendentals=0)


def shape(*dims):
    return pltpu.VMEM(dims, F32)


def in_hbm(*arrays):
    return [pltpu.with_memory_space_constraint(x, pltpu.HBM) for x in arrays]


def in_vmem(*arrays):
    return [pltpu.with_memory_space_constraint(x, pltpu.VMEM) for x in arrays]


def face(half, open_face):
    return jnp.where(open_face, half + DIFFUSION, 0.0), jnp.where(open_face, half - DIFFUSION, 0.0)


def stencil(east, north, west, south):
    a_e, b_e = east
    a_n, b_n = north
    a_w, b_w = west
    a_s, b_s = south
    return (((1.0 - a_e) + b_w) - a_n) + b_s, b_e, a_w, b_n, a_s


def advance(weights, cell, east, west, north, south):
    own, b_e, a_w, b_n, a_s = weights
    return (own * cell + (a_w * west - b_e * east)) + (a_s * south - b_n * north)


def north_of(tiles, beyond):
    row = row_index()
    turned = [rows(t, -1) for t in tiles]
    return [jnp.where(row == 7, n, t) for t, n in zip(turned, turned[1:] + [beyond])]


def south_of(tiles):
    row = row_index()
    turned = [rows(t, 1) for t in tiles]
    return [turned[0]] + [jnp.where(row == 0, p, t) for p, t in zip(turned, turned[1:])]


def shut_corner(cells, flows, west):
    lane, row = lane_index(), row_index()
    turn, far = (32, lane < 32) if west else (96, lane >= 96)
    first = (row & 3) == 3
    both = [jnp.where(first & far, rows(lanes(x, turn), 2), x) for x in (cells, flows)]
    return jnp.where((row & 2) != 0, both[0], rows(both[1], -2))


def open_corner(tile, west):
    third = (row_index() & 3) == 1
    turn = 96 if west else 32
    return [jnp.where(third, rows(lanes(x, turn), -2), x) for x in (tile, rows(tile, 2))]


def edge_columns(stacks):
    lane = lane_index()
    outer = (lane < 8) | (lane >= 120)
    group = [((lane >> 2) & 3) == c for c in range(3)]
    sums = [[None] * 4 for _ in stacks]
    for k in range(max(len(x) for x in stacks)):
        for total, stack in zip(sums, stacks):
            if k < len(stack):
                tile = lanes(jnp.where(outer, stack[k](), 0.0), 4 * k)
                total[k % 4] = tile if total[k % 4] is None else total[k % 4] + tile
    offsets = (0, 1, -2, -1)
    found = []
    for offset in offsets:
        for total in sums:
            a, b, c, d = [total[(g - offset) % 4] for g in range(4)]
            tile = jnp.where(group[0], a, jnp.where(group[1], b, jnp.where(group[2], c, d)))
            found.append(lanes(tile, -4 * offset))
    order = spread_order()
    found = [take(x, order) for x in found]
    return [[found[b * len(stacks) + i] for b in range(4)] for i in range(len(stacks))]


def stack_of(ref, depth, *where):
    return [lambda k=k: ref[(k, *where)] for k in range(depth)]


def pack_kernel(
    depth, t_hbm, e_hbm, n_hbm, d_hbm, w_hbm, atm_hbm, out, west, east, blocks, to_core, to_odd, w, atm,
    t, e, n, d, sems,
):
    copies = [
        pltpu.make_async_copy(d_hbm, d, sems.at[0]),
        pltpu.make_async_copy(t_hbm, t, sems.at[1]),
        pltpu.make_async_copy(e_hbm, e, sems.at[2]),
        pltpu.make_async_copy(n_hbm, n, sems.at[3]),
        pltpu.make_async_copy(atm_hbm, atm, sems.at[4]),
        pltpu.make_async_copy(w_hbm.at[0], w, sems.at[5]),
    ]
    for copy in copies:
        copy.start()
    me = lax.axis_index("lon")
    even = lax.rem(me, 2) == 0
    row = row_index()
    turn = 127 - lane_index()
    count = t.shape[2] // 8
    spans = [slice(8 * j, 8 * j + 8) for j in range(count)]
    fields = (t.at[0], t.at[1], e, n)

    def columns(chosen):
        places = [(f, j) for f in chosen for j in range(count)]
        stacks = [stack_of(fields[f], depth, spans[j]) for f, j in places]
        if 0 in chosen:
            for stack, span in zip(stacks, spans):
                stack.append(lambda span=span: d[span].astype(F32))
        for (f, j), found in zip(places, edge_columns(stacks)):
            for b, tile in enumerate(found):
                blocks[b, f, spans[j]] = tile
            w1, e1 = found[0], found[3]
            to_core[f, spans[j]] = jnp.where(even, e1, w1)
            to_odd[f, spans[j]] = jnp.where(even, w1, e1)
            wrapped = jnp.where(me == 0, w1, e1)
            place = f * count + j
            if place < 4 * count - 2:
                out[depth + place // 2, 8 * (place % 2) : 8 * (place % 2) + 8] = wrapped
            else:
                for r in range(8):
                    out[4 + 8 * (place - 4 * count + 2) + r, 12:13] = wrapped[r : r + 1]

    copies[0].wait()
    copies[1].wait()
    columns((0, 1))
    copies[2].wait()
    copies[3].wait()
    levels = d[spans[-1]].astype(F32)
    for k in range(depth):
        cells = jnp.where(row < 4, rows(t[0, k, spans[-1]], 4), t[1, k, spans[-1]])
        flows = jnp.where(row < 4, rows(n[k, spans[-1]], 4), e[k, spans[-1]])
        if k < 4:
            flows = jnp.where(row == 4, rows(levels, -k), flows)
        out[k, 0:8] = take(cells, turn)
        out[k, 8:16] = take(flows, turn)
    columns((2, 3))
    halves = [slice(0, 8), slice(8, 16)]
    stacks = [stack_of(out, depth, span) for span in halves]
    stacks[1].append(lambda: take(levels, turn))
    cells, flows = edge_columns(stacks)
    east[...] = shut_corner(cells[0], flows[0], False)
    west[...] = shut_corner(cells[3], flows[3], True)
    copies[4].wait()
    copies[5].wait()


def regrid_kernel(size, atm, w, src_hbm, west, east, out, wide, part, src, sems):
    blocks_read = pltpu.make_async_copy(src_hbm, src, sems.at[0])
    blocks_read.start()
    flat = atm[...].reshape(atm.shape[0] * atm.shape[1], atm.shape[2])
    count = flat.shape[0]
    blocks = atm.shape[1]
    columns = jnp.transpose(jnp.concatenate([flat, jnp.zeros((128 - count, 128), F32)], axis=0))
    for c in range(count):
        wide[c] = jnp.broadcast_to(columns[:, c : c + 1], (128, 128))
    me = lax.axis_index("lon")

    def send(e, tile):
        out[3 * e + 1] = tile[0:4]
        out[3 * e + 2] = tile[4:8]

    def fill(e, carry):
        send(e, west[...])
        return carry

    lax.fori_loop(0, size, fill, 0, unroll=8)
    send(lax.rem(2 * size - 2 - me, size), east[...])

    def owner(e, carry):
        for s in range(2):
            block = src[s, e]
            sums = [None, None]
            for i in range(16):
                span = slice(8 * i, 8 * i + 8)
                weight = w[e, s, span]
                for f in range(2):
                    term = weight * wide[f * blocks + block, span]
                    sums[f] = term if sums[f] is None else sums[f] + term
            for f in range(2):
                part[e, 2 * f + s] = sums[f]
        return carry

    def pair(e, carry):
        tile = totals([part[2 * e + i // 4, i % 4] for i in range(8)])
        out[6 * e] = tile[0:4]
        out[6 * e + 3] = tile[4:8]
        return carry

    blocks_read.wait()
    lax.fori_loop(0, size, owner, 0, unroll=4)
    lax.fori_loop(0, size // 2, pair, 0, unroll=8)


def totals(tiles):
    row = row_index()
    for step in (4, 2, 1):
        low = (row & step) == 0
        half = len(tiles) // 2
        merged = []
        for a, b in zip(tiles[:half], tiles[half:]):
            kept, moved = jnp.where(low, a, b), jnp.where(low, b, a)
            if step == 4:
                turned = rows(moved, 4)
            else:
                turned = jnp.where(low, rows(moved, -step), rows(moved, step))
            merged.append(kept + turned)
        tiles = merged
    return tiles[0]


def inner_kernel(
    depth, t_hbm, e_hbm, n_hbm, d_hbm, mix_hbm, out, surface_wet, columns, top_t, top_e, top_n, top_d,
    t, e, n, d, mix, weights, sems, flow_sems, cell_sems,
):
    levels = pltpu.make_async_copy(d_hbm, d, sems.at[0])
    mixing = pltpu.make_async_copy(mix_hbm, mix, sems.at[1])
    parts = [pl.ds(k, min(PART, depth - k)) for k in range(0, depth, PART)]
    flows = [
        (
            pltpu.make_async_copy(e_hbm.at[p], e.at[p], flow_sems.at[0, i]),
            pltpu.make_async_copy(n_hbm.at[p], n.at[p], flow_sems.at[1, i]),
        )
        for i, p in enumerate(parts)
    ]
    cells = [pltpu.make_async_copy(t_hbm.at[:, p], t.at[:, p], cell_sems.at[i]) for i, p in enumerate(parts)]
    levels.start()
    for pair in flows:
        for copy in pair:
            copy.start()
    for copy in cells:
        copy.start()
    mixing.start()
    levels.wait()
    row = row_index()
    count = t.shape[2] // 8
    spans = [slice(8 * j, 8 * j + 8) for j in range(count)]
    deep = [d[s].astype(F32) for s in spans]

    def plus(tiles):
        return [lanes(x, 1) for x in tiles]

    def minus(tiles):
        return [lanes(x, -1) for x in tiles]

    east_faces = [jnp.minimum(x, y) for x, y in zip(deep, minus(deep))]
    faces = list(zip(east_faces, plus(east_faces), block_faces(deep, deep[-1])))

    def coefficients(k):
        e_half = [0.5 * e[k, s] for s in spans]
        n_half = [0.5 * n[k, s] for s in spans]
        for s, he, hw, hn, hs, (east, west, (north, south)) in zip(
            spans, e_half, plus(e_half), n_half, south_of(n_half), faces
        ):
            found = stencil(
                face(he, east > float(k)),
                face(hn, north > float(k)),
                face(hw, west > float(k)),
                face(hs, south > float(k)),
            )
            for i, x in enumerate(found):
                weights[i, k, s] = x

    def substep(k, step):
        source = out if step else t
        for f in range(2):
            state = [source[f, k, s] for s in spans]
            up, down = north_of(state, state[-1]), south_of(state)
            for s, c, u, v in zip(spans, state, up, down):
                w = [weights[i, k, s] for i in range(5)]
                out[f, k, s] = advance(w, c, lanes(c, -1), lanes(c, 1), u, v)

    zero = jnp.zeros((8, 128), F32)
    above, ratio = [zero] * count, [zero] * count

    def pivots(k):
        for j, s in enumerate(spans):
            link = jnp.where(deep[j] > float(k + 1), mix[k, s], 0.0) if k < depth - 1 else zero
            inv = 1.0 / (1.0 + above[j] + link + above[j] * ratio[j])
            columns[0, k, s] = inv
            columns[1, k, s] = link
            above[j], ratio[j] = link, -link * inv

    top_d[...] = deep[-1]
    for s, x in zip(spans, deep):
        surface_wet[s] = jnp.where(x > 0.0, 1.0, 0.0)
    for k in range(depth):
        if k % PART == 0:
            for copy in flows[k // PART]:
                copy.wait()
        coefficients(k)
        top_e[k] = e[k, spans[-1]]
        top_n[k] = n[k, spans[-1]]
    for k in range(depth):
        if k % PART == 0:
            cells[k // PART].wait()
        substep(k, 0)
        for f in range(2):
            top_t[f, k] = t[f, k, spans[-1]]
    mixing.wait()
    for step in range(1, SUB):
        for k in range(depth):
            substep(k, step)
            if step == 1:
                pivots(k)


def fold_faces(deep, own_deep, toward_east, toward_west):
    easts = [jnp.minimum(x, y) for x, y in zip(deep, toward_east(deep))]
    norths = [jnp.minimum(x, fold_north(x, y, y)) for x, y in zip(deep, own_deep)]
    return list(zip(easts, toward_west(easts), norths, [rows(x, 1) for x in norths]))


def fold_weights(flows, faces, levels, toward_west):
    row = row_index()
    turned = [rows(x, 4) for x in flows]
    e_half = [0.5 * jnp.where(row < 4, y, x) for x, y in zip(flows, turned)]
    n_half = [0.5 * jnp.where(row < 4, x, y) for x, y in zip(flows, turned)]
    w_half = toward_west(e_half)
    s_half = [rows(x, 1) for x in n_half]
    return [
        stencil(face(e, east > k), face(n, north > k), face(w, west > k), face(s, south > k))
        for e, n, w, s, (east, west, north, south), k in zip(e_half, n_half, w_half, s_half, faces, levels)
    ]


def block_faces(deep, beyond):
    norths = [jnp.minimum(x, y) for x, y in zip(deep, north_of(deep, beyond))]
    souths = south_of(norths)
    souths[0] = jnp.where(row_index() == 0, 0.0, souths[0])
    return list(zip(norths, souths))


def fold_north(fold, first, second):
    row = row_index()
    return jnp.where((row & 3) == 3, jnp.where(row < 4, rows(first, 4), second), rows(fold, -1))


def fold_levels(fold):
    row = row_index()
    deep = jnp.zeros((8, 128), F32)
    for r in range(4):
        deep = jnp.where((row & 3) == r, jnp.broadcast_to(fold[r, 12:13], (8, 128)), deep)
    return deep


def strip_kernel(depth, t, e, n, d, fold, strip, blocks, folded, weights, over):
    halves = [slice(0, 8), slice(8, 16)]
    stacks = [stack_of(fold, depth, span) for span in halves]
    stacks[1].append(lambda: fold_levels(fold))
    for span, found in zip(halves, edge_columns(stacks)):
        for b, tile in enumerate(found):
            blocks[b, span] = tile
    row = row_index()
    deep = d[...]
    fold_deep = fold_levels(fold)

    def plus(tiles):
        return [lanes(x, 1) for x in tiles]

    def minus(tiles):
        return [lanes(x, -1) for x in tiles]

    over_faces = fold_faces([fold_deep], [deep], plus, minus)
    east = jnp.minimum(deep, lanes(deep, -1))
    west = lanes(east, 1)
    north = jnp.minimum(deep, jnp.where(row == 7, fold_deep, rows(deep, -1)))
    south = rows(north, 1)
    for k in range(0, depth, GROUP):
        levels = range(k, min(k + GROUP, depth))
        found = fold_weights(
            [fold[k, 8:16] for k in levels], over_faces * len(levels), [float(k) for k in levels], minus
        )
        for k, tiles in zip(levels, found):
            for i, x in enumerate(tiles):
                over[i, k] = x
    for k in range(depth):
        he, hn = 0.5 * e[k], 0.5 * n[k]
        level = float(k)
        found = stencil(
            face(he, east > level),
            face(hn, north > level),
            face(lanes(he, 1), west > level),
            face(rows(hn, 1), south > level),
        )
        for i, x in enumerate(found):
            weights[i, k] = x
    for step in range(SUB):
        for k in range(depth):
            if step:
                one, two, cells = strip[0, k], strip[1, k], folded[k]
            else:
                one, two, cells = t[0, k], t[1, k], fold[k, 0:8]
            up_one = jnp.where(row == 7, rows(cells, 4), rows(one, -1))
            up_two = jnp.where(row == 7, cells, rows(two, -1))
            if step < SUB - 1:
                up = fold_north(cells, one, two)
                w = [over[i, k] for i in range(5)]
                folded[k] = advance(w, cells, lanes(cells, 1), lanes(cells, -1), up, rows(cells, 1))
            w = [weights[i, k] for i in range(5)]
            strip[0, k] = advance(w, one, lanes(one, -1), lanes(one, 1), up_one, rows(one, 1))
            strip[1, k] = advance(w, two, lanes(two, -1), lanes(two, 1), up_two, rows(two, 1))


def edge_side(depth, rows_count, cells, flows, fold_cells, fold_flows):
    lane, row = lane_index(), row_index()
    level = (lane & 31).astype(F32)
    count = rows_count // 8

    def plus(tiles):
        turned = [lanes(x, 32) for x in tiles]
        return [turned[0]] + [jnp.where(lane < 32, p, x) for p, x in zip(turned, turned[1:])]

    def minus(tiles):
        turned = [lanes(x, -32) for x in tiles]
        return [jnp.where(lane >= 96, q, x) for x, q in zip(turned, turned[1:])] + [turned[2]]

    at_levels = (lane & 96) + depth
    deep = [[take(cells[b][0][j], at_levels) for j in range(count)] for b in range(3)]
    fold_deep = []
    for b in range(3):
        found = take(fold_flows[b], at_levels)
        fold_deep.append(jnp.where(row < 4, rows(found, 4), found))
    over_faces = fold_faces(fold_deep, [deep[b][-1] for b in range(3)], plus, minus)
    over = fold_weights(fold_flows, over_faces, [level] * 3, minus)

    weights = [[None] * count for _ in range(3)]
    meridional = [block_faces(deep[b], fold_deep[b]) for b in range(3)]
    halves = [[0.5 * x for x in flows[b][1]] for b in range(3)]
    southern = [south_of(x) for x in halves]
    for j in range(count):
        yield
        line = [deep[b][j] for b in range(3)]
        easts = [jnp.minimum(x, y) for x, y in zip(line, minus(line))]
        e_half = [0.5 * flows[b][0][j] for b in range(3)]
        for b, (east, west, he, hw) in enumerate(zip(easts, plus(easts), e_half, plus(e_half))):
            north, south = meridional[b][j]
            weights[b][j] = stencil(
                face(he, east > level),
                face(halves[b][j], north > level),
                face(hw, west > level),
                face(southern[b][j], south > level),
            )

    state = [[list(cells[b][f]) for f in range(2)] for b in range(3)]
    folded = list(fold_cells)
    for step in range(SUB):
        yield
        beyond = [(rows(x, 4), x) for x in folded]
        if step < SUB - 1:
            fold_east, fold_west = plus(folded), minus(folded)
            ups = [fold_north(folded[b], state[b][0][-1], state[b][1][-1]) for b in range(3)]
            folded = [
                advance(over[b], folded[b], fold_east[b], fold_west[b], ups[b], rows(folded[b], 1)) for b in range(3)
            ]
        for f in range(2):
            yield
            east, west = [], []
            for j in range(count):
                line = [state[b][f][j] for b in range(3)]
                east.append(minus(line))
                west.append(plus(line))
            yield
            for b in range(3):
                tiles = state[b][f]
                up, down = north_of(tiles, beyond[b][f]), south_of(tiles)
                state[b][f] = [
                    advance(weights[b][j], tiles[j], east[j][b], west[j][b], up[j], down[j]) for j in range(count)
                ]
    return state[1]


def side_by_side(stages):
    results = [None] * len(stages)
    running = list(enumerate(stages))
    while running:
        left = []
        for i, stage in running:
            try:
                next(stage)
                left.append((i, stage))
            except StopIteration as end:
                results[i] = end.value
        running = left
    return results


def last_kernel(
    depth, strip, folds, wet, inner, blocks, core, odd, fold, mail, columns, target_hbm,
    out_hbm, merged, out, target, sems, other,
):
    targets = pltpu.make_async_copy(target_hbm, target, other.at[0])
    targets.start()
    lane, row = lane_index(), row_index()
    size = mail.shape[0] // 3
    rows_count = inner.shape[2]
    count = rows_count // 8
    spans = [slice(8 * j, 8 * j + 8) for j in range(count)]
    me = lax.axis_index("lon")
    even = lax.rem(me, 2) == 0

    def corner(sender, west):
        place = 3 * lax.rem(sender, size)
        return open_corner(jnp.concatenate([mail[place + 1], mail[place + 2]], axis=0), west)

    west_mail, east_mail = corner(size - me, True), corner(2 * size - 2 - me, False)
    at_wrap = (me == 0) | (me == size - 1)

    def received(f, j, west):
        place = f * count + j
        if place < 4 * count - 2:
            wrapped = fold[depth + place // 2, 8 * (place % 2) : 8 * (place % 2) + 8]
        else:
            wrapped = jnp.zeros((8, 128), F32)
            for r in range(8):
                line = fold[4 + 8 * (place - 4 * count + 2) + r, 12:13]
                wrapped = jnp.where(row == r, jnp.broadcast_to(line, (8, 128)), wrapped)
        a, b = core[f, spans[j]], jnp.where(at_wrap, wrapped, odd[f, spans[j]])
        return jnp.where(even, b, a) if west else jnp.where(even, a, b)

    def own(b, f, s):
        return blocks[b, f, s]

    sides = []
    for west in (True, False):
        near, far = (0, 1) if west else (3, 2)
        here = [[[own(b, f, s) for s in spans] for f in range(4)] for b in (near, far)]
        there = [[received(f, j, west) for j in range(count)] for f in range(4)]
        letter = west_mail if west else east_mail
        line = [there, here[0], here[1]] if west else [here[1], here[0], there]
        cells_near = [folds[near, 0:8], folds[far, 0:8]]
        flows_near = [folds[near, 8:16], folds[far, 8:16]]
        if west:
            fold_cells = [letter[0]] + cells_near
            fold_flows = [letter[1]] + flows_near
        else:
            fold_cells = cells_near[::-1] + [letter[0]]
            fold_flows = flows_near[::-1] + [letter[1]]
        sides.append(
            edge_side(depth, rows_count, [x[0:2] for x in line], [x[2:4] for x in line], fold_cells, fold_flows)
        )

    sides = side_by_side(sides)
    order = gather_order()
    group_even = ((lane >> 2) & 1) == 0
    for f in range(2):
        for j, s in enumerate(spans):
            a = take(sides[0][f][j], order)
            b = lanes(take(sides[1][f][j], order), -4)
            merged[0, f, s] = jnp.where(group_even, a, b)
            merged[1, f, s] = jnp.where(group_even, b, a)

    surface = [[jnp.zeros((8, 128), F32) for _ in spans] for _ in range(2)]
    targets.wait()
    for a in range(size):
        for s in range(2):
            goal = target[s, a]
            hits = [row + 8 * j == goal for j in range(count)]
            for f in range(2):
                piece = jnp.broadcast_to(mail[3 * a, 2 * f + s : 2 * f + s + 1], (8, 128))
                surface[f] = [x + jnp.where(hit, piece, 0.0) for x, hit in zip(surface[f], hits)]

    outer = (lane < 4) | (lane >= 124)
    for k in range(depth):
        for f in range(2):
            for j, s in enumerate(spans):
                cell = inner[f, k, s]
                if j == count - 1:
                    cell = jnp.where(row >= 4, strip[f, k], cell)
                out[f, k, s] = jnp.where(outer, lanes(merged[k % 2, f, s], -4 * k), cell)
    partial_value = [[None] * count for _ in range(2)]
    for k in range(depth):
        for f in range(2):
            for j, s in enumerate(spans):
                cell = out[f, k, s]
                if k == 0:
                    cell = cell + FLUX_GAIN * surface[f][j] * wet[s]
                else:
                    cell = cell + columns[1, k - 1, s] * partial_value[f][j]
                value = cell * columns[0, k, s]
                partial_value[f][j] = value
                out[f, k, s] = value
    copies = []
    for k in range(depth - 1, -1, -1):
        if k < depth - 1:
            for f in range(2):
                for j, s in enumerate(spans):
                    value = out[f, k, s] + columns[1, k, s] * columns[0, k, s] * partial_value[f][j]
                    partial_value[f][j] = value
                    out[f, k, s] = value
        if k % GROUP == 0:
            part = pl.ds(k, min(GROUP, depth - k))
            copy = pltpu.make_async_copy(out.at[:, part], out_hbm.at[:, part], sems.at[k // GROUP])
            copy.start()
            copies.append(copy)
    for copy in copies:
        copy.wait()


def on_device(
    tracers,
    east_flow,
    north_flow,
    mixing,
    depth_levels,
    atm_flux,
    source_blocks,
    target_rows,
    regrid_weights,
):
    size = lax.axis_size("lon")
    depth, lat = tracers.shape[1], tracers.shape[2]
    dma = pltpu.SemaphoreType.DMA
    near = [(i, i + (1 if i % 2 else -1)) for i in range(1, size - 1)]
    plane = shape(depth, lat, 128)
    block = [shape(2, depth, lat, 128), plane, plane, pltpu.VMEM((lat, 128), jnp.int32)]
    strips = shape(4, lat, 128)
    fields = in_hbm(tracers, east_flow, north_flow, depth_levels)

    message, west_corner, east_corner, blocks, to_core, to_odd, weights, flux = call(
        functools.partial(pack_kernel, depth),
        (
            shape(depth + lat // 4 - 1, 16, 128), shape(8, 128), shape(8, 128), shape(4, 4, lat, 128), strips, strips,
            shape(*regrid_weights.shape[1:]), shape(*atm_flux.shape),
        ),
        [HBM] * 6,
        [*block, dma((6,))],
        cost=cost(0.1),
        name="fold_rows_and_columns",
    )(*fields, *in_hbm(regrid_weights, atm_flux))
    fold = lax.ppermute(message, "lon", [(i, size - 1 - i) for i in range(size)])
    core = lax.ppermute(to_core, "lon", [(i, i ^ 1) for i in range(size)])
    odd = lax.ppermute(to_odd, "lon", [(0, 0), *near, (size - 1, size - 1)])

    (letters,) = call(
        functools.partial(regrid_kernel, size),
        (shape(3 * size, 4, 128),),
        [VMEM, VMEM, HBM, VMEM, VMEM],
        [
            pltpu.VMEM((2 * atm_flux.shape[1], 128, 128), F32),
            pltpu.VMEM((size, 4, 8, 128), F32),
            pltpu.SMEM((2, size), jnp.int32),
            dma((1,)),
        ],
        cost=cost(0.1),
        name="regrid",
    )(
        *in_vmem(flux, weights),
        *in_hbm(jnp.transpose(source_blocks[0])),
        *in_vmem(west_corner, east_corner),
    )
    mail = lax.all_to_all(letters, "lon", split_axis=0, concat_axis=0, tiled=True)

    inner, wet, columns, *band = call(
        functools.partial(inner_kernel, depth),
        (
            shape(2, depth, lat, 128), shape(lat, 128), shape(2, depth, lat, 128),
            shape(2, depth, 8, 128), shape(depth, 8, 128), shape(depth, 8, 128), shape(8, 128),
        ),
        [HBM] * 5,
        [
            *block,
            shape(depth - 1, lat, 128),
            shape(5, depth, lat, 128),
            dma((2,)),
            dma((2, -(-depth // PART))),
            dma((-(-depth // PART),)),
        ],
        cost=cost(0.1),
        name="inner_cells",
    )(*fields, *in_hbm(mixing))

    strip, folds = call(
        functools.partial(strip_kernel, depth),
        (shape(2, depth, 8, 128), shape(4, 16, 128)),
        [VMEM] * 5,
        [shape(depth, 8, 128), shape(5, depth, 8, 128), shape(5, depth, 8, 128)],
        cost=cost(0.1),
        name="top_strip",
    )(*in_vmem(*band, fold))

    (result,) = call(
        functools.partial(last_kernel, depth),
        (jax.ShapeDtypeStruct((2, depth, lat, 128), F32),),
        [VMEM] * 10 + [HBM],
        [
            pltpu.VMEM((2, 2, lat, 128), F32),
            pltpu.VMEM((2, depth, lat, 128), F32),
            pltpu.SMEM((2, size), jnp.int32),
            dma((-(-depth // GROUP),)),
            dma((1,)),
        ],
        out_specs=[HBM],
        cost=cost(0.1),
        name="edges_and_columns",
    )(
        *in_vmem(strip, folds, wet, inner, blocks, core, odd, fold, mail, columns),
        *in_hbm(jnp.transpose(target_rows[:, 0, :])),
    )
    return result


def solution(mesh):
    return jax.shard_map(
        on_device,
        mesh=mesh,
        in_specs=(
            P(None, "ens", None, "lon"),
            P("ens", None, "lon"),
            P("ens", None, "lon"),
            P("ens", None, "lon"),
            P(None, "lon"),
            P("ens", "lon", None),
            P("lon", None, None),
            P(None, "lon", None),
            P("lon", None, None, None, None),
        ),
        out_specs=P(None, "ens", None, "lon"),
        check_vma=False,
    )
```

```python
import functools

import jax
import jax.numpy as jnp
from jax import lax
from jax.experimental import pallas as pl
from jax.experimental.pallas import tpu as pltpu
from jax.sharding import PartitionSpec as P

SUB = 4
DIFFUSION = 0.12
FLUX_GAIN = 0.5
GROUP = 5
PART = 25
F32 = jnp.float32
VMEM = pl.BlockSpec(memory_space=pltpu.VMEM)
SMEM = pl.BlockSpec(memory_space=pltpu.SMEM)
HBM = pl.BlockSpec(memory_space=pltpu.HBM)
VMEM_LIMIT = 16 * 1024 * 1024


def lane_index():
    return lax.broadcasted_iota(jnp.int32, (8, 128), 1)


def row_index():
    return lax.broadcasted_iota(jnp.int32, (8, 128), 0)


def lanes(tile, shift):
    shift = shift % 128
    return pltpu.roll(tile, shift, 1) if shift else tile


def rows(tile, shift):
    shift = shift % 8
    return pltpu.roll(tile, shift, 0) if shift else tile


def take(tile, index):
    return jnp.take_along_axis(tile, index, axis=1)


def spread_order():
    lane = lane_index()
    return 4 * (lane & 31) + (lane >> 5)


def gather_order():
    lane = lane_index()
    return 32 * (lane & 3) + (lane >> 2)


def call(body, out, in_specs, scratch=(), out_specs=None, cost=None, name=None):
    return pl.pallas_call(
        body,
        out_shape=out,
        in_specs=in_specs,
        out_specs=out_specs if out_specs is not None else [VMEM] * len(out),
        scratch_shapes=list(scratch),
        compiler_params=pltpu.CompilerParams(vmem_limit_bytes=VMEM_LIMIT),
        cost_estimate=cost,
        name=name,
    )


def cost(micros):
    return pl.CostEstimate(flops=0, bytes_accessed=int(micros * 3.0e6), transcendentals=0)


def shape(*dims):
    return pltpu.VMEM(dims, F32)


def in_hbm(*arrays):
    return [pltpu.with_memory_space_constraint(x, pltpu.HBM) for x in arrays]


def in_vmem(*arrays):
    return [pltpu.with_memory_space_constraint(x, pltpu.VMEM) for x in arrays]


def face(half, open_face):
    return jnp.where(open_face, half + DIFFUSION, 0.0), jnp.where(open_face, half - DIFFUSION, 0.0)


def stencil(east, north, west, south):
    a_e, b_e = east
    a_n, b_n = north
    a_w, b_w = west
    a_s, b_s = south
    return (((1.0 - a_e) + b_w) - a_n) + b_s, b_e, a_w, b_n, a_s


def advance(weights, cell, east, west, north, south):
    own, b_e, a_w, b_n, a_s = weights
    return (own * cell + (a_w * west - b_e * east)) + (a_s * south - b_n * north)


def north_of(tiles, beyond):
    row = row_index()
    turned = [rows(t, -1) for t in tiles]
    return [jnp.where(row == 7, n, t) for t, n in zip(turned, turned[1:] + [beyond])]


def south_of(tiles):
    row = row_index()
    turned = [rows(t, 1) for t in tiles]
    return [turned[0]] + [jnp.where(row == 0, p, t) for p, t in zip(turned, turned[1:])]


def shut_corner(cells, flows, west):
    lane, row = lane_index(), row_index()
    turn, far = (32, lane < 32) if west else (96, lane >= 96)
    first = (row & 3) == 3
    both = [jnp.where(first & far, rows(lanes(x, turn), 2), x) for x in (cells, flows)]
    return jnp.where((row & 2) != 0, both[0], rows(both[1], -2))


def open_corner(tile, west):
    third = (row_index() & 3) == 1
    turn = 96 if west else 32
    return [jnp.where(third, rows(lanes(x, turn), -2), x) for x in (tile, rows(tile, 2))]


def edge_columns(stacks):
    lane = lane_index()
    outer = (lane < 8) | (lane >= 120)
    group = [((lane >> 2) & 3) == c for c in range(3)]
    sums = [[None] * 4 for _ in stacks]
    for k in range(max(len(x) for x in stacks)):
        for total, stack in zip(sums, stacks):
            if k < len(stack):
                tile = lanes(jnp.where(outer, stack[k](), 0.0), 4 * k)
                total[k % 4] = tile if total[k % 4] is None else total[k % 4] + tile
    offsets = (0, 1, -2, -1)
    found = []
    for offset in offsets:
        for total in sums:
            a, b, c, d = [total[(g - offset) % 4] for g in range(4)]
            tile = jnp.where(group[0], a, jnp.where(group[1], b, jnp.where(group[2], c, d)))
            found.append(lanes(tile, -4 * offset))
    order = spread_order()
    found = [take(x, order) for x in found]
    return [[found[b * len(stacks) + i] for b in range(4)] for i in range(len(stacks))]


def stack_of(ref, depth, *where):
    return [lambda k=k: ref[(k, *where)] for k in range(depth)]


def pack_kernel(
    depth, t_hbm, e_hbm, n_hbm, d_hbm, w_hbm, atm_hbm, out, blocks, to_core, to_odd, w, atm,
    t, e, n, d, sems,
):
    copies = [
        pltpu.make_async_copy(d_hbm, d, sems.at[0]),
        pltpu.make_async_copy(t_hbm, t, sems.at[1]),
        pltpu.make_async_copy(e_hbm, e, sems.at[2]),
        pltpu.make_async_copy(n_hbm, n, sems.at[3]),
        pltpu.make_async_copy(atm_hbm, atm, sems.at[4]),
        pltpu.make_async_copy(w_hbm.at[0], w, sems.at[5]),
    ]
    for copy in copies:
        copy.start()
    me = lax.axis_index("lon")
    even = lax.rem(me, 2) == 0
    row = row_index()
    turn = 127 - lane_index()
    count = t.shape[2] // 8
    spans = [slice(8 * j, 8 * j + 8) for j in range(count)]
    fields = (t.at[0], t.at[1], e, n)

    def columns(chosen):
        places = [(f, j) for f in chosen for j in range(count)]
        stacks = [stack_of(fields[f], depth, spans[j]) for f, j in places]
        if 0 in chosen:
            for stack, span in zip(stacks, spans):
                stack.append(lambda span=span: d[span].astype(F32))
        for (f, j), found in zip(places, edge_columns(stacks)):
            for b, tile in enumerate(found):
                blocks[b, f, spans[j]] = tile
            w1, e1 = found[0], found[3]
            to_core[f, spans[j]] = jnp.where(even, e1, w1)
            to_odd[f, spans[j]] = jnp.where(even, w1, e1)
            wrapped = jnp.where(me == 0, w1, e1)
            place = f * count + j
            if place < 4 * count - 2:
                out[depth + place // 2, 8 * (place % 2) : 8 * (place % 2) + 8] = wrapped
            else:
                for r in range(8):
                    out[4 + 8 * (place - 4 * count + 2) + r, 12:13] = wrapped[r : r + 1]

    copies[0].wait()
    copies[1].wait()
    columns((0, 1))
    copies[2].wait()
    copies[3].wait()
    levels = d[spans[-1]].astype(F32)
    for k in range(depth):
        cells = jnp.where(row < 4, rows(t[0, k, spans[-1]], 4), t[1, k, spans[-1]])
        flows = jnp.where(row < 4, rows(n[k, spans[-1]], 4), e[k, spans[-1]])
        if k < 4:
            flows = jnp.where(row == 4, rows(levels, -k), flows)
        out[k, 0:8] = take(cells, turn)
        out[k, 8:16] = take(flows, turn)
    columns((2, 3))
    copies[4].wait()
    copies[5].wait()


def regrid_kernel(depth, size, atm, w, src_hbm, fold, out, wide, part, src, sems):
    blocks_read = pltpu.make_async_copy(src_hbm, src, sems.at[0])
    blocks_read.start()
    flat = atm[...].reshape(atm.shape[0] * atm.shape[1], atm.shape[2])
    count = flat.shape[0]
    blocks = atm.shape[1]
    columns = jnp.transpose(jnp.concatenate([flat, jnp.zeros((128 - count, 128), F32)], axis=0))
    for c in range(count):
        wide[c] = jnp.broadcast_to(columns[:, c : c + 1], (128, 128))
    me = lax.axis_index("lon")

    halves = [slice(0, 8), slice(8, 16)]
    stacks = [stack_of(fold, depth, span) for span in halves]
    stacks[1].append(lambda: fold_levels(fold))
    cells, flows = edge_columns(stacks)
    east = shut_corner(cells[0], flows[0], False)
    west = shut_corner(cells[3], flows[3], True)

    def send(e, tile):
        out[3 * e + 1] = tile[0:4]
        out[3 * e + 2] = tile[4:8]

    def fill(e, carry):
        send(e, west)
        return carry

    lax.fori_loop(0, size, fill, 0, unroll=8)
    send(lax.rem(2 * size - 2 - me, size), east)

    def owner(e, carry):
        for s in range(2):
            block = src[s, e]
            sums = [None, None]
            for i in range(16):
                span = slice(8 * i, 8 * i + 8)
                weight = w[e, s, span]
                for f in range(2):
                    term = weight * wide[f * blocks + block, span]
                    sums[f] = term if sums[f] is None else sums[f] + term
            for f in range(2):
                part[e, 2 * f + s] = sums[f]
        return carry

    def pair(e, carry):
        tile = totals([part[2 * e + i // 4, i % 4] for i in range(8)])
        out[6 * e] = tile[0:4]
        out[6 * e + 3] = tile[4:8]
        return carry

    blocks_read.wait()
    lax.fori_loop(0, size, owner, 0, unroll=4)
    lax.fori_loop(0, size // 2, pair, 0, unroll=8)


def totals(tiles):
    row = row_index()
    for step in (4, 2, 1):
        low = (row & step) == 0
        half = len(tiles) // 2
        merged = []
        for a, b in zip(tiles[:half], tiles[half:]):
            kept, moved = jnp.where(low, a, b), jnp.where(low, b, a)
            if step == 4:
                turned = rows(moved, 4)
            else:
                turned = jnp.where(low, rows(moved, -step), rows(moved, step))
            merged.append(kept + turned)
        tiles = merged
    return tiles[0]


def inner_kernel(
    depth, t_hbm, e_hbm, n_hbm, d_hbm, mix_hbm, out, surface_wet, columns, top_t, top_e, top_n, top_d,
    t, e, n, d, mix, weights, sems, flow_sems, cell_sems,
):
    levels = pltpu.make_async_copy(d_hbm, d, sems.at[0])
    mixing = pltpu.make_async_copy(mix_hbm, mix, sems.at[1])
    parts = [pl.ds(k, min(PART, depth - k)) for k in range(0, depth, PART)]
    flows = [
        (
            pltpu.make_async_copy(e_hbm.at[p], e.at[p], flow_sems.at[0, i]),
            pltpu.make_async_copy(n_hbm.at[p], n.at[p], flow_sems.at[1, i]),
        )
        for i, p in enumerate(parts)
    ]
    cells = [pltpu.make_async_copy(t_hbm.at[:, p], t.at[:, p], cell_sems.at[i]) for i, p in enumerate(parts)]
    levels.start()
    for pair in flows:
        for copy in pair:
            copy.start()
    for copy in cells:
        copy.start()
    mixing.start()
    levels.wait()
    row = row_index()
    count = t.shape[2] // 8
    spans = [slice(8 * j, 8 * j + 8) for j in range(count)]
    deep = [d[s].astype(F32) for s in spans]

    def plus(tiles):
        return [lanes(x, 1) for x in tiles]

    def minus(tiles):
        return [lanes(x, -1) for x in tiles]

    east_faces = [jnp.minimum(x, y) for x, y in zip(deep, minus(deep))]
    faces = list(zip(east_faces, plus(east_faces), block_faces(deep, deep[-1])))

    def coefficients(k):
        e_half = [0.5 * e[k, s] for s in spans]
        n_half = [0.5 * n[k, s] for s in spans]
        for s, he, hw, hn, hs, (east, west, (north, south)) in zip(
            spans, e_half, plus(e_half), n_half, south_of(n_half), faces
        ):
            found = stencil(
                face(he, east > float(k)),
                face(hn, north > float(k)),
                face(hw, west > float(k)),
                face(hs, south > float(k)),
            )
            for i, x in enumerate(found):
                weights[i, k, s] = x

    def substep(k, step):
        source = out if step else t
        for f in range(2):
            state = [source[f, k, s] for s in spans]
            up, down = north_of(state, state[-1]), south_of(state)
            for s, c, u, v in zip(spans, state, up, down):
                w = [weights[i, k, s] for i in range(5)]
                out[f, k, s] = advance(w, c, lanes(c, -1), lanes(c, 1), u, v)

    zero = jnp.zeros((8, 128), F32)
    above, ratio = [zero] * count, [zero] * count

    def pivots(k):
        for j, s in enumerate(spans):
            link = jnp.where(deep[j] > float(k + 1), mix[k, s], 0.0) if k < depth - 1 else zero
            inv = 1.0 / (1.0 + above[j] + link + above[j] * ratio[j])
            columns[0, k, s] = inv
            columns[1, k, s] = link
            above[j], ratio[j] = link, -link * inv

    top_d[...] = deep[-1]
    for s, x in zip(spans, deep):
        surface_wet[s] = jnp.where(x > 0.0, 1.0, 0.0)
    for k in range(depth):
        if k % PART == 0:
            for copy in flows[k // PART]:
                copy.wait()
        coefficients(k)
        top_e[k] = e[k, spans[-1]]
        top_n[k] = n[k, spans[-1]]
    for k in range(depth):
        if k % PART == 0:
            cells[k // PART].wait()
        substep(k, 0)
        for f in range(2):
            top_t[f, k] = t[f, k, spans[-1]]
    mixing.wait()
    for step in range(1, SUB):
        for k in range(depth):
            substep(k, step)
            if step == 1:
                pivots(k)


def fold_faces(deep, own_deep, toward_east, toward_west):
    easts = [jnp.minimum(x, y) for x, y in zip(deep, toward_east(deep))]
    norths = [jnp.minimum(x, fold_north(x, y, y)) for x, y in zip(deep, own_deep)]
    return list(zip(easts, toward_west(easts), norths, [rows(x, 1) for x in norths]))


def fold_weights(flows, faces, levels, toward_west):
    row = row_index()
    turned = [rows(x, 4) for x in flows]
    e_half = [0.5 * jnp.where(row < 4, y, x) for x, y in zip(flows, turned)]
    n_half = [0.5 * jnp.where(row < 4, x, y) for x, y in zip(flows, turned)]
    w_half = toward_west(e_half)
    s_half = [rows(x, 1) for x in n_half]
    return [
        stencil(face(e, east > k), face(n, north > k), face(w, west > k), face(s, south > k))
        for e, n, w, s, (east, west, north, south), k in zip(e_half, n_half, w_half, s_half, faces, levels)
    ]


def block_faces(deep, beyond):
    norths = [jnp.minimum(x, y) for x, y in zip(deep, north_of(deep, beyond))]
    souths = south_of(norths)
    souths[0] = jnp.where(row_index() == 0, 0.0, souths[0])
    return list(zip(norths, souths))


def fold_north(fold, first, second):
    row = row_index()
    return jnp.where((row & 3) == 3, jnp.where(row < 4, rows(first, 4), second), rows(fold, -1))


def fold_levels(fold):
    row = row_index()
    deep = jnp.zeros((8, 128), F32)
    for r in range(4):
        deep = jnp.where((row & 3) == r, jnp.broadcast_to(fold[r, 12:13], (8, 128)), deep)
    return deep


def strip_kernel(depth, t, e, n, d, fold, strip, blocks, folded, weights, over):
    halves = [slice(0, 8), slice(8, 16)]
    stacks = [stack_of(fold, depth, span) for span in halves]
    stacks[1].append(lambda: fold_levels(fold))
    for span, found in zip(halves, edge_columns(stacks)):
        for b, tile in enumerate(found):
            blocks[b, span] = tile
    row = row_index()
    deep = d[...]
    fold_deep = fold_levels(fold)

    def plus(tiles):
        return [lanes(x, 1) for x in tiles]

    def minus(tiles):
        return [lanes(x, -1) for x in tiles]

    over_faces = fold_faces([fold_deep], [deep], plus, minus)
    east = jnp.minimum(deep, lanes(deep, -1))
    west = lanes(east, 1)
    north = jnp.minimum(deep, jnp.where(row == 7, fold_deep, rows(deep, -1)))
    south = rows(north, 1)
    for k in range(0, depth, GROUP):
        levels = range(k, min(k + GROUP, depth))
        found = fold_weights(
            [fold[k, 8:16] for k in levels], over_faces * len(levels), [float(k) for k in levels], minus
        )
        for k, tiles in zip(levels, found):
            for i, x in enumerate(tiles):
                over[i, k] = x
    for k in range(depth):
        he, hn = 0.5 * e[k], 0.5 * n[k]
        level = float(k)
        found = stencil(
            face(he, east > level),
            face(hn, north > level),
            face(lanes(he, 1), west > level),
            face(rows(hn, 1), south > level),
        )
        for i, x in enumerate(found):
            weights[i, k] = x
    for step in range(SUB):
        for k in range(depth):
            if step:
                one, two, cells = strip[0, k], strip[1, k], folded[k]
            else:
                one, two, cells = t[0, k], t[1, k], fold[k, 0:8]
            up_one = jnp.where(row == 7, rows(cells, 4), rows(one, -1))
            up_two = jnp.where(row == 7, cells, rows(two, -1))
            if step < SUB - 1:
                up = fold_north(cells, one, two)
                w = [over[i, k] for i in range(5)]
                folded[k] = advance(w, cells, lanes(cells, 1), lanes(cells, -1), up, rows(cells, 1))
            w = [weights[i, k] for i in range(5)]
            strip[0, k] = advance(w, one, lanes(one, -1), lanes(one, 1), up_one, rows(one, 1))
            strip[1, k] = advance(w, two, lanes(two, -1), lanes(two, 1), up_two, rows(two, 1))


def edge_side(depth, rows_count, cells, flows, fold_cells, fold_flows):
    lane, row = lane_index(), row_index()
    level = (lane & 31).astype(F32)
    count = rows_count // 8

    def plus(tiles):
        turned = [lanes(x, 32) for x in tiles]
        return [turned[0]] + [jnp.where(lane < 32, p, x) for p, x in zip(turned, turned[1:])]

    def minus(tiles):
        turned = [lanes(x, -32) for x in tiles]
        return [jnp.where(lane >= 96, q, x) for x, q in zip(turned, turned[1:])] + [turned[2]]

    at_levels = (lane & 96) + depth
    deep = [[take(cells[b][0][j], at_levels) for j in range(count)] for b in range(3)]
    fold_deep = []
    for b in range(3):
        found = take(fold_flows[b], at_levels)
        fold_deep.append(jnp.where(row < 4, rows(found, 4), found))
    over_faces = fold_faces(fold_deep, [deep[b][-1] for b in range(3)], plus, minus)
    over = fold_weights(fold_flows, over_faces, [level] * 3, minus)

    weights = [[None] * count for _ in range(3)]
    meridional = [block_faces(deep[b], fold_deep[b]) for b in range(3)]
    halves = [[0.5 * x for x in flows[b][1]] for b in range(3)]
    southern = [south_of(x) for x in halves]
    for j in range(count):
        yield
        line = [deep[b][j] for b in range(3)]
        easts = [jnp.minimum(x, y) for x, y in zip(line, minus(line))]
        e_half = [0.5 * flows[b][0][j] for b in range(3)]
        for b, (east, west, he, hw) in enumerate(zip(easts, plus(easts), e_half, plus(e_half))):
            north, south = meridional[b][j]
            weights[b][j] = stencil(
                face(he, east > level),
                face(halves[b][j], north > level),
                face(hw, west > level),
                face(southern[b][j], south > level),
            )

    state = [[list(cells[b][f]) for f in range(2)] for b in range(3)]
    folded = list(fold_cells)
    for step in range(SUB):
        yield
        beyond = [(rows(x, 4), x) for x in folded]
        if step < SUB - 1:
            fold_east, fold_west = plus(folded), minus(folded)
            ups = [fold_north(folded[b], state[b][0][-1], state[b][1][-1]) for b in range(3)]
            folded = [
                advance(over[b], folded[b], fold_east[b], fold_west[b], ups[b], rows(folded[b], 1)) for b in range(3)
            ]
        for f in range(2):
            yield
            east, west = [], []
            for j in range(count):
                line = [state[b][f][j] for b in range(3)]
                east.append(minus(line))
                west.append(plus(line))
            yield
            for b in range(3):
                tiles = state[b][f]
                up, down = north_of(tiles, beyond[b][f]), south_of(tiles)
                state[b][f] = [
                    advance(weights[b][j], tiles[j], east[j][b], west[j][b], up[j], down[j]) for j in range(count)
                ]
    return state[1]


def side_by_side(stages):
    results = [None] * len(stages)
    running = list(enumerate(stages))
    while running:
        left = []
        for i, stage in running:
            try:
                next(stage)
                left.append((i, stage))
            except StopIteration as end:
                results[i] = end.value
        running = left
    return results


def last_kernel(
    depth, strip, folds, wet, inner, blocks, core, odd, fold, mail, columns, target_hbm,
    out_hbm, merged, out, target, sems, other,
):
    targets = pltpu.make_async_copy(target_hbm, target, other.at[0])
    targets.start()
    lane, row = lane_index(), row_index()
    size = mail.shape[0] // 3
    rows_count = inner.shape[2]
    count = rows_count // 8
    spans = [slice(8 * j, 8 * j + 8) for j in range(count)]
    me = lax.axis_index("lon")
    even = lax.rem(me, 2) == 0

    def corner(sender, west):
        place = 3 * lax.rem(sender, size)
        return open_corner(jnp.concatenate([mail[place + 1], mail[place + 2]], axis=0), west)

    west_mail, east_mail = corner(size - me, True), corner(2 * size - 2 - me, False)
    at_wrap = (me == 0) | (me == size - 1)

    def received(f, j, west):
        place = f * count + j
        if place < 4 * count - 2:
            wrapped = fold[depth + place // 2, 8 * (place % 2) : 8 * (place % 2) + 8]
        else:
            wrapped = jnp.zeros((8, 128), F32)
            for r in range(8):
                line = fold[4 + 8 * (place - 4 * count + 2) + r, 12:13]
                wrapped = jnp.where(row == r, jnp.broadcast_to(line, (8, 128)), wrapped)
        a, b = core[f, spans[j]], jnp.where(at_wrap, wrapped, odd[f, spans[j]])
        return jnp.where(even, b, a) if west else jnp.where(even, a, b)

    def own(b, f, s):
        return blocks[b, f, s]

    sides = []
    for west in (True, False):
        near, far = (0, 1) if west else (3, 2)
        here = [[[own(b, f, s) for s in spans] for f in range(4)] for b in (near, far)]
        there = [[received(f, j, west) for j in range(count)] for f in range(4)]
        letter = west_mail if west else east_mail
        line = [there, here[0], here[1]] if west else [here[1], here[0], there]
        cells_near = [folds[near, 0:8], folds[far, 0:8]]
        flows_near = [folds[near, 8:16], folds[far, 8:16]]
        if west:
            fold_cells = [letter[0]] + cells_near
            fold_flows = [letter[1]] + flows_near
        else:
            fold_cells = cells_near[::-1] + [letter[0]]
            fold_flows = flows_near[::-1] + [letter[1]]
        sides.append(
            edge_side(depth, rows_count, [x[0:2] for x in line], [x[2:4] for x in line], fold_cells, fold_flows)
        )

    sides = side_by_side(sides)
    order = gather_order()
    group_even = ((lane >> 2) & 1) == 0
    for f in range(2):
        for j, s in enumerate(spans):
            a = take(sides[0][f][j], order)
            b = lanes(take(sides[1][f][j], order), -4)
            merged[0, f, s] = jnp.where(group_even, a, b)
            merged[1, f, s] = jnp.where(group_even, b, a)

    surface = [[jnp.zeros((8, 128), F32) for _ in spans] for _ in range(2)]
    targets.wait()
    for a in range(size):
        for s in range(2):
            goal = target[s, a]
            hits = [row + 8 * j == goal for j in range(count)]
            for f in range(2):
                piece = jnp.broadcast_to(mail[3 * a, 2 * f + s : 2 * f + s + 1], (8, 128))
                surface[f] = [x + jnp.where(hit, piece, 0.0) for x, hit in zip(surface[f], hits)]

    outer = (lane < 4) | (lane >= 124)
    for k in range(depth):
        for f in range(2):
            for j, s in enumerate(spans):
                cell = inner[f, k, s]
                if j == count - 1:
                    cell = jnp.where(row >= 4, strip[f, k], cell)
                out[f, k, s] = jnp.where(outer, lanes(merged[k % 2, f, s], -4 * k), cell)
    partial_value = [[None] * count for _ in range(2)]
    for k in range(depth):
        for f in range(2):
            for j, s in enumerate(spans):
                cell = out[f, k, s]
                if k == 0:
                    cell = cell + FLUX_GAIN * surface[f][j] * wet[s]
                else:
                    cell = cell + columns[1, k - 1, s] * partial_value[f][j]
                value = cell * columns[0, k, s]
                partial_value[f][j] = value
                out[f, k, s] = value
    copies = []
    for k in range(depth - 1, -1, -1):
        if k < depth - 1:
            for f in range(2):
                for j, s in enumerate(spans):
                    value = out[f, k, s] + columns[1, k, s] * columns[0, k, s] * partial_value[f][j]
                    partial_value[f][j] = value
                    out[f, k, s] = value
        if k % GROUP == 0:
            part = pl.ds(k, min(GROUP, depth - k))
            copy = pltpu.make_async_copy(out.at[:, part], out_hbm.at[:, part], sems.at[k // GROUP])
            copy.start()
            copies.append(copy)
    for copy in copies:
        copy.wait()


def on_device(
    tracers,
    east_flow,
    north_flow,
    mixing,
    depth_levels,
    atm_flux,
    source_blocks,
    target_rows,
    regrid_weights,
):
    size = lax.axis_size("lon")
    depth, lat = tracers.shape[1], tracers.shape[2]
    dma = pltpu.SemaphoreType.DMA
    near = [(i, i + (1 if i % 2 else -1)) for i in range(1, size - 1)]
    plane = shape(depth, lat, 128)
    block = [shape(2, depth, lat, 128), plane, plane, pltpu.VMEM((lat, 128), jnp.int32)]
    strips = shape(4, lat, 128)
    fields = in_hbm(tracers, east_flow, north_flow, depth_levels)

    message, blocks, to_core, to_odd, weights, flux = call(
        functools.partial(pack_kernel, depth),
        (
            shape(depth + lat // 4 - 1, 16, 128), shape(4, 4, lat, 128), strips, strips,
            shape(*regrid_weights.shape[1:]), shape(*atm_flux.shape),
        ),
        [HBM] * 6,
        [*block, dma((6,))],
        cost=cost(0.1),
        name="fold_rows_and_columns",
    )(*fields, *in_hbm(regrid_weights, atm_flux))
    fold = lax.ppermute(message, "lon", [(i, size - 1 - i) for i in range(size)])
    core = lax.ppermute(to_core, "lon", [(i, i ^ 1) for i in range(size)])
    odd = lax.ppermute(to_odd, "lon", [(0, 0), *near, (size - 1, size - 1)])

    (letters,) = call(
        functools.partial(regrid_kernel, depth, size),
        (shape(3 * size, 4, 128),),
        [VMEM, VMEM, HBM, VMEM],
        [
            pltpu.VMEM((2 * atm_flux.shape[1], 128, 128), F32),
            pltpu.VMEM((size, 4, 8, 128), F32),
            pltpu.SMEM((2, size), jnp.int32),
            dma((1,)),
        ],
        cost=cost(0.1),
        name="regrid",
    )(
        *in_vmem(flux, weights),
        *in_hbm(jnp.transpose(source_blocks[0])),
        *in_vmem(message),
    )
    mail = lax.all_to_all(letters, "lon", split_axis=0, concat_axis=0, tiled=True)

    inner, wet, columns, *band = call(
        functools.partial(inner_kernel, depth),
        (
            shape(2, depth, lat, 128), shape(lat, 128), shape(2, depth, lat, 128),
            shape(2, depth, 8, 128), shape(depth, 8, 128), shape(depth, 8, 128), shape(8, 128),
        ),
        [HBM] * 5,
        [
            *block,
            shape(depth - 1, lat, 128),
            shape(5, depth, lat, 128),
            dma((2,)),
            dma((2, -(-depth // PART))),
            dma((-(-depth // PART),)),
        ],
        cost=cost(0.1),
        name="inner_cells",
    )(*fields, *in_hbm(mixing))

    strip, folds = call(
        functools.partial(strip_kernel, depth),
        (shape(2, depth, 8, 128), shape(4, 16, 128)),
        [VMEM] * 5,
        [shape(depth, 8, 128), shape(5, depth, 8, 128), shape(5, depth, 8, 128)],
        cost=cost(0.1),
        name="top_strip",
    )(*in_vmem(*band, fold))

    (result,) = call(
        functools.partial(last_kernel, depth),
        (jax.ShapeDtypeStruct((2, depth, lat, 128), F32),),
        [VMEM] * 10 + [HBM],
        [
            pltpu.VMEM((2, 2, lat, 128), F32),
            pltpu.VMEM((2, depth, lat, 128), F32),
            pltpu.SMEM((2, size), jnp.int32),
            dma((-(-depth // GROUP),)),
            dma((1,)),
        ],
        out_specs=[HBM],
        cost=cost(0.1),
        name="edges_and_columns",
    )(
        *in_vmem(strip, folds, wet, inner, blocks, core, odd, fold, mail, columns),
        *in_hbm(jnp.transpose(target_rows[:, 0, :])),
    )
    return result


def solution(mesh):
    return jax.shard_map(
        on_device,
        mesh=mesh,
        in_specs=(
            P(None, "ens", None, "lon"),
            P("ens", None, "lon"),
            P("ens", None, "lon"),
            P("ens", None, "lon"),
            P(None, "lon"),
            P("ens", "lon", None),
            P("lon", None, None),
            P(None, "lon", None),
            P("lon", None, None, None, None),
        ),
        out_specs=P(None, "ens", None, "lon"),
        check_vma=False,
    )
```
